32 devices in a mesh: dp: 8 (over y, x, core), tensor: 4 (over z).
Axes of the slice: x: 2, y: 2, z: 4, core: 2. Of those that a mesh axis runs over, the one named last changes fastest.
Arguments:
- hidden: bfloat16 [2, 1024, 2048], P(None, 'dp'), may hold values from -6 to 6
- embedding: bfloat16 [2, 1024, 2048], P(None, 'dp'), may hold values from -6 to 6
- lengths: int32 [2, 8, 5], P(None, 'dp'), may hold values from 1 to 64, 128 in all within a row
- query_key_value_weight: bfloat16 [4096, 3, 4096], P('dp', None, 'tensor'), may hold values from -0.09375 to 0.09375
- attention_output_weight: bfloat16 [4096, 4096], P('tensor', 'dp'), may hold values from -0.375 to 0.375
- attention_gain: bfloat16 [4096], P('dp'), may hold values from 0.099609375 to 1.8984375
- feedforward_gain: bfloat16 [4096], P('dp'), may hold values from 0.099609375 to 1.8984375
- gate_up_weight: bfloat16 [4096, 2, 8192], P('dp', None, 'tensor'), may hold values from -0.09375 to 0.09375
- adapter_down: bfloat16 [4096, 128], P('dp'), may hold values from -0.09375 to 0.09375
- adapter_up: bfloat16 [128, 2, 8192], P('dp', None, 'tensor'), may hold values from -0.5 to 0.5
- down_weight: bfloat16 [8192, 4096], P('tensor', 'dp'), may hold values from -0.0625 to 0.0625
- shared_projection_weight: bfloat16 [4096, 2048], P('tensor', 'dp'), may hold values from -0.09375 to 0.09375
- mixer_gain: bfloat16 [2048], P('dp'), may hold values from 0.099609375 to 1.8984375
- mixer_input_weight: bfloat16 [2048, 2, 4096], P('dp', None, 'tensor'), may hold values from -0.125 to 0.125
- state_map_weight: bfloat16 [2048, 256], P('dp'), may hold values from -0.125 to 0.125
- step_weight: bfloat16 [2048, 64], P('dp', 'tensor'), may hold values from -0.125 to 0.125
- mixer_output_weight: bfloat16 [4096, 2048], P('tensor', 'dp'), may hold values from -0.09375 to 0.09375
- mixer_input_taps: float32 [4, 4096], P(None, 'tensor'), may hold values from -3 to 3
- state_map_taps: float32 [4, 256], replicated, may hold values from -3 to 3
- step_bias: float32 [64], P('tensor'), may hold values from -6 to -2
- decay_logarithm: float32 [64], P('tensor'), may hold values from 0 to 2.77
- head_skip_weight: float32 [64], P('tensor'), may hold values from 0.5 to 1.5
- gated_norm_gain: float32 [4096], P('tensor'), may hold values from 0.1 to 1.9
- cotangent: bfloat16 [2, 1024, 2048], P(None, 'dp'), may hold values from -6 to 6
Outputs:
- output: bfloat16 [2, 1024, 2048], P(None, 'dp')
- d_hidden: bfloat16 [2, 1024, 2048], P(None, 'dp')
- d_embedding: bfloat16 [2, 1024, 2048], P(None, 'dp')
- grad_w_qkv: float32 [4096, 3, 4096], P('dp', None, 'tensor')
- grad_w_out: float32 [4096, 4096], P('tensor', 'dp')
- grad_g_attn: float32 [4096], P('dp')
- grad_g_mlp: float32 [4096], P('dp')
- grad_w_gate_up: float32 [4096, 2, 8192], P('dp', None, 'tensor')
- adapter_down_gradient: float32 [4096, 128], P('dp')
- adapter_up_gradient: float32 [128, 2, 8192], P('dp', None, 'tensor')
- grad_w_down: float32 [8192, 4096], P('tensor', 'dp')
- grad_w_proj: float32 [4096, 2048], P('tensor', 'dp')
- grad_g_mamba: float32 [2048], P('dp')
- grad_w_in: float32 [2048, 2, 4096], P('dp', None, 'tensor')
- grad_w_bc: float32 [2048, 256], P('dp')
- grad_w_dt: float32 [2048, 64], P('dp', 'tensor')
- grad_w_mout: float32 [4096, 2048], P('tensor', 'dp')
- grad_conv_x: float32 [4, 4096], P(None, 'tensor')
- grad_conv_bc: float32 [4, 256], replicated
- grad_dt_bias: float32 [64], P('tensor')
- grad_a_log: float32 [64], P('tensor')
- grad_d_skip: float32 [64], P('tensor')
- grad_g_gate: float32 [4096], P('tensor')
The draws below stay inside these ranges and needn't reach their ends.
Inputs may be any that keep to these rules, and one draw needn't show every extreme that they name: Each row of lengths is one bin of 128 rows: its first 4 entries are the lengths of the sequences packed in order from the bin's first row, the last entry is the count of padding rows at the bin's end; each row sums to 128 and its largest entry is exactly 64.
All inputs are finite; a program needn't handle non-finite values.
Results may differ from the reference program's by a relative error of at most 0.03.
Values may be sent and summed in bfloat16 or wider, within the bound.
A program may use at most 448 MiB of HBM per device.

```python
import math
import jax
import jax.numpy as jnp
import numpy as np
from jax import lax

D = 2048
JOINED_FEATURES = 4096
HEAD = 128
ATT = 4096
FEEDFWD_UNITS = 8192
ADAPTER_RANK = 128
MHEADS = 64
INNER = 4096
STATE = 128
CONV = 4
MB = 2
SEQS = 4
TOK_DEV = 128
TOKENS = 1024
N_DP = 8


def block_scale(key, shape, shards, least, high):
    loudness, own = 1.0, jax.random.fold_in(key, 6)
    for dim, blocks in shards:
        draws = jnp.exp(jax.random.uniform(jax.random.fold_in(own, dim), (blocks,), jnp.float32, least / len(shards), high / len(shards)))
        loudness = loudness * jnp.repeat(draws, shape[dim] // blocks).reshape([-1 if axis == dim else 1 for axis in range(len(shape))])
    return loudness


def split_up(amount, total, most, skew):
    loads = [(1 << 20) // math.isqrt(rank ** skew) + 1 for rank in range(2, amount + 1)]
    spare, given = total - most - (amount - 1), [1] * (amount - 1)
    while spare > 0:
        candidates = [i for i in range(amount - 1) if given[i] < most]
        mass, remaining = sum([loads[i] for i in candidates]), spare
        for i in candidates:
            extra = min(most - given[i], max(1, remaining * loads[i] // mass), spare)
            given[i] = given[i] + extra
            spare = spare - extra
    return np.array([most] + given)


def uneven(stream_key, number_of, total, bound, skew):
    if number_of == 2:
        one = jax.random.randint(stream_key, (), max(1, total - bound), min(bound, total - 1) + 1)
        return jnp.stack([one, total - one])
    sizes = jnp.asarray(split_up(number_of, total, bound, skew), jnp.int32)
    couples = (number_of - 1) // 2
    giver, sink = sizes[1:1 + 2 * couples:2], sizes[2:2 + 2 * couples:2]
    margin = jnp.minimum(giver - 1, bound - sink)
    moved = jax.random.randint(jax.random.fold_in(stream_key, 1), (couples,), 0, 1 << 20) % (margin + 1)
    sizes = sizes.at[1:1 + 2 * couples:2].set(giver - moved).at[2:2 + 2 * couples:2].set(sink + moved)
    return sizes[jax.random.permutation(jax.random.fold_in(stream_key, 2), number_of)]


def scatter_about(rng, extent, width, reach, split=(), kind=jnp.bfloat16):
    values = jax.random.normal(rng, extent, jnp.float32) * width
    if len(split) > 0:
        values = block_scale(rng, extent, split, -0.22, 0.18) * values
    return jnp.clip(values, min=-reach, max=reach).astype(kind)


def setup_inputs(seed: int = 0) -> dict:
    streams_of = jax.random.split(jax.random.key(seed), 25)
    return {
        "hidden": scatter_about(streams_of[0], (MB, TOKENS, D), 1.0, 6.0, ((1, 8),)),
        "embedding": scatter_about(streams_of[1], (MB, TOKENS, D), 1.0, 6.0, ((1, 8),)),
        "lengths": jax.vmap(lambda own: uneven(own, SEQS + 1, TOK_DEV, TOK_DEV // 2, 2))(jax.random.split(streams_of[2], MB * N_DP)).reshape((MB, N_DP, SEQS + 1)).astype(jnp.int32),
        "query_key_value_weight": scatter_about(streams_of[3], (JOINED_FEATURES, 3, ATT), JOINED_FEATURES ** -0.5, 0.09375, ((0, 8), (2, 4))),
        "attention_output_weight": scatter_about(streams_of[4], (ATT, JOINED_FEATURES), (JOINED_FEATURES // 16) ** -0.5, 0.375, ((0, 4), (1, 8))),
        "attention_gain": jnp.clip(1.0 + 0.18 * jax.random.normal(streams_of[5], (JOINED_FEATURES,), jnp.float32), 0.099609375, 1.8984375).astype(jnp.bfloat16),
        "feedforward_gain": jnp.clip(1.0 + 0.18 * jax.random.normal(streams_of[6], (JOINED_FEATURES,), jnp.float32), 0.099609375, 1.8984375).astype(jnp.bfloat16),
        "gate_up_weight": scatter_about(streams_of[7], (JOINED_FEATURES, 2, FEEDFWD_UNITS), JOINED_FEATURES ** -0.5, 0.09375, ((0, 8), (2, 4))),
        "adapter_down": scatter_about(streams_of[8], (JOINED_FEATURES, ADAPTER_RANK), JOINED_FEATURES ** -0.5, 0.09375, ((0, 8),)),
        "adapter_up": scatter_about(streams_of[9], (ADAPTER_RANK, 2, FEEDFWD_UNITS), ADAPTER_RANK ** -0.5, 0.5, ((0, 8), (2, 4))),
        "down_weight": scatter_about(streams_of[10], (FEEDFWD_UNITS, JOINED_FEATURES), FEEDFWD_UNITS ** -0.5, 0.0625, ((0, 4), (1, 8))),
        "shared_projection_weight": scatter_about(streams_of[11], (JOINED_FEATURES, D), JOINED_FEATURES ** -0.5, 0.09375, ((0, 4), (1, 8))),
        "mixer_gain": jnp.clip(1.0 + 0.18 * jax.random.normal(streams_of[12], (D,), jnp.float32), 0.099609375, 1.8984375).astype(jnp.bfloat16),
        "mixer_input_weight": scatter_about(streams_of[13], (D, 2, INNER), D ** -0.5, 0.125, ((0, 8), (2, 4))),
        "state_map_weight": scatter_about(streams_of[14], (D, 2 * STATE), D ** -0.5, 0.125, ((0, 8),)),
        "step_weight": scatter_about(streams_of[15], (D, MHEADS), D ** -0.5, 0.125, ((0, 8), (1, 4))),
        "mixer_output_weight": scatter_about(streams_of[16], (INNER, D), INNER ** -0.5, 0.09375, ((0, 4), (1, 8))),
        "mixer_input_taps": scatter_about(streams_of[17], (CONV, INNER), CONV ** -0.5, 3.0, ((1, 4),), jnp.float32),
        "state_map_taps": scatter_about(streams_of[18], (CONV, 2 * STATE), CONV ** -0.5, 3.0, (), jnp.float32),
        "step_bias": jnp.clip(-6.0 + 4.0 * jax.random.uniform(streams_of[19], (MHEADS,), jnp.float32) ** block_scale(streams_of[19], (MHEADS,), ((0, 4),), -0.2, 0.2), -6.0, -2.0),
        "decay_logarithm": jnp.clip(2.77 * jax.random.uniform(streams_of[20], (MHEADS,), jnp.float32) ** block_scale(streams_of[20], (MHEADS,), ((0, 4),), -0.2, 0.2), 0.0, 2.77),
        "head_skip_weight": jnp.clip(0.5 + 1.0 * jax.random.uniform(streams_of[21], (MHEADS,), jnp.float32) ** block_scale(streams_of[21], (MHEADS,), ((0, 4),), -0.2, 0.2), 0.5, 1.5),
        "gated_norm_gain": jnp.clip(1.0 + 0.18 * jax.random.normal(streams_of[22], (INNER,), jnp.float32), 0.1, 1.9),
        "cotangent": scatter_about(streams_of[23], (MB, TOKENS, D), 1.0, 6.0, ((1, 8),)),
    }


EPSILON = 1e-05
ROPE_BASE = 10000.0
MASKED = -1e+30
TOP_PRECISION = lax.Precision.HIGHEST

@jax.custom_vjp
def narrow_cast(v):
    return lax.optimization_barrier(v.astype(jnp.bfloat16)).astype(jnp.float32)

@jax.custom_vjp
def narrow_cast_backward(v):
    return v

def low_keep(v):
    return (narrow_cast(v), None)

def low_pass(kept, grad):
    return (grad,)

def back_keep(v):
    return (v, None)

def back_low(kept, grad):
    return (narrow_cast(grad),)
narrow_cast.defvjp(low_keep, low_pass)
narrow_cast_backward.defvjp(back_keep, back_low)

def layout(len_row, row_count):
    bounds = jnp.cumsum(len_row).astype(jnp.int32)[:-1]
    places = jnp.arange(row_count, dtype=jnp.int32)
    passed = places[:, None] >= bounds[None, :]
    segment = lax.optimization_barrier(jnp.sum(passed.astype(jnp.int32), axis=1)).astype(jnp.int32)
    starts = lax.optimization_barrier(jnp.max(jnp.where(passed, bounds[None, :], 0), axis=1)).astype(jnp.int32)
    position = places - starts
    valid = segment < bounds.shape[0]
    allowed = (segment[:, None] == segment[None, :]) & (places[None, :] <= places[:, None])
    return (segment, position, valid, allowed)

def rms_norm(values, gain):
    return values * lax.rsqrt(lax.optimization_barrier(jnp.mean(values * values, axis=-1, keepdims=True)) + EPSILON) * gain

def rotate(values, position):
    half_size = values.shape[-1] // 2
    frequency = ROPE_BASE ** (-2.0 * jnp.arange(half_size, dtype=jnp.float32) / values.shape[-1])
    angles = position.astype(jnp.float32)[:, None] * frequency[None, :]
    cosine = jnp.cos(angles)[:, None, :]
    sine_part = jnp.sin(angles)[:, None, :]
    leading = values[..., :half_size]
    trailing = values[..., half_size:]
    return jnp.concatenate([leading * cosine - trailing * sine_part, trailing * cosine + leading * sine_part], axis=-1)

def causal_conv(values, taps, segment):
    row_count = values.shape[0]
    summed = jnp.zeros_like(values)
    for offset in range(taps.shape[0]):
        shifted = jnp.pad(values, ((offset, 0), (0, 0)))[:row_count]
        shifted_seg = jnp.pad(segment, (offset, 0), constant_values=-1)[:row_count]
        summed = summed + jnp.where((shifted_seg == segment)[:, None], shifted, 0.0) * taps[offset][None, :]
    return summed

def state_mix(inputs, step_size, log_decay, b_part, c_part, allowed, head_skip_weight):
    running = jnp.cumsum(log_decay, axis=0)
    log_gap = jnp.where(allowed[:, :, None], running[:, None, :] - running[None, :, :], MASKED)
    affinity = jnp.dot(c_part, b_part.T, precision=TOP_PRECISION)
    mixing = jnp.exp(log_gap) * affinity[:, :, None] * step_size[None, :, :]
    return jnp.einsum('tsh,shp->thp', mixing, inputs, precision=TOP_PRECISION) + head_skip_weight[None, :, None] * inputs

def mamba_local(gate_x, state_io, step_raw, mixer_input_taps, state_map_taps, step_bias, decay_logarithm, head_skip_weight, segment, allowed):
    row_count = gate_x.shape[0]
    head_count = step_raw.shape[1]
    head_size = gate_x.shape[2] // head_count
    conv_out = jax.nn.silu(causal_conv(gate_x[:, 1], mixer_input_taps, segment))
    state_conv = jax.nn.silu(causal_conv(state_io, state_map_taps, segment))
    state_size = state_io.shape[1] // 2
    step_size = jax.nn.softplus(step_raw + step_bias)
    log_decay = -step_size * jnp.exp(decay_logarithm)
    mixed_out = state_mix(conv_out.reshape(row_count, head_count, head_size), step_size, log_decay, state_conv[:, :state_size], state_conv[:, state_size:], allowed, head_skip_weight)
    return mixed_out.reshape(row_count, head_count * head_size) * jax.nn.silu(gate_x[:, 0])

def gated_gelu(gate_up_apply):
    return jax.nn.gelu(gate_up_apply[:, 0], approximate=True) * gate_up_apply[:, 1]

def bin_forward(parameter_tree, hid_row, emb_row, len_row):
    query_key_value_weight, attention_output_weight, attention_gain, feedforward_gain, gate_up_weight, adapter_down, adapter_up, down_weight, shared_projection_weight, mixer_gain, mixer_input_weight, state_map_weight, step_weight, mixer_output_weight, mixer_input_taps, state_map_taps, step_bias, decay_logarithm, head_skip_weight, gated_norm_gain = parameter_tree
    row_count = hid_row.shape[0]
    segment, position, valid, allowed = layout(len_row, row_count)
    head_count = attention_output_weight.shape[0] // HEAD
    joined = jnp.concatenate([hid_row, emb_row], axis=1)
    attn_in = narrow_cast(rms_norm(joined, attention_gain))
    qkv_rows = narrow_cast_backward(jnp.einsum('td,dkc->tkc', attn_in, query_key_value_weight, precision=TOP_PRECISION))
    query = narrow_cast(rotate(qkv_rows[:, 0].reshape(row_count, head_count, HEAD), position))
    key_rot = narrow_cast(rotate(qkv_rows[:, 1].reshape(row_count, head_count, HEAD), position))
    value_rows = narrow_cast(qkv_rows[:, 2].reshape(row_count, head_count, HEAD))
    scores = narrow_cast_backward(jnp.einsum('thc,shc->hts', query, key_rot, precision=TOP_PRECISION)) * HEAD ** (-0.5)
    scores = jnp.where(allowed[None], scores, MASKED)
    probs = narrow_cast(jax.nn.softmax(scores, axis=-1))
    attended = jnp.einsum('hts,shc->thc', probs, value_rows, precision=TOP_PRECISION).reshape(row_count, head_count * HEAD)
    attended = narrow_cast(narrow_cast_backward(attended))
    mid_res = joined + narrow_cast_backward(jnp.dot(attended, attention_output_weight, precision=TOP_PRECISION))
    feedforward_input = narrow_cast(rms_norm(mid_res, feedforward_gain))
    adapter_apply = narrow_cast(narrow_cast_backward(jnp.dot(feedforward_input, adapter_down, precision=TOP_PRECISION)))
    gate_up_apply = jnp.einsum('td,dkc->tkc', feedforward_input, gate_up_weight, precision=TOP_PRECISION)
    gate_up_apply = narrow_cast_backward(gate_up_apply + jnp.einsum('yb,bos->yos', adapter_apply, adapter_up, precision=TOP_PRECISION))
    hidden_act = narrow_cast(gated_gelu(gate_up_apply))
    block = narrow_cast(mid_res + narrow_cast_backward(jnp.dot(hidden_act, down_weight, precision=TOP_PRECISION)))
    shared = narrow_cast(narrow_cast_backward(jnp.dot(block, shared_projection_weight, precision=TOP_PRECISION)))
    mamba_in = hid_row + shared
    ssm_in = narrow_cast(rms_norm(mamba_in, mixer_gain))
    gate_x = narrow_cast_backward(jnp.einsum('td,dkc->tkc', ssm_in, mixer_input_weight, precision=TOP_PRECISION))
    state_io = narrow_cast_backward(jnp.dot(ssm_in, state_map_weight, precision=TOP_PRECISION))
    step_raw = narrow_cast_backward(jnp.dot(ssm_in, step_weight, precision=TOP_PRECISION))
    gated = mamba_local(gate_x, state_io, step_raw, mixer_input_taps, state_map_taps, step_bias, decay_logarithm, head_skip_weight, segment, allowed)
    gated_norm = narrow_cast(rms_norm(gated, gated_norm_gain))
    mamba_out = narrow_cast_backward(jnp.dot(gated_norm, mixer_output_weight, precision=TOP_PRECISION))
    return (mamba_in + mamba_out) * valid[:, None].astype(jnp.float32)

def reference(hidden, embedding, lengths, query_key_value_weight, attention_output_weight, attention_gain, feedforward_gain, gate_up_weight, adapter_down, adapter_up, down_weight, shared_projection_weight, mixer_gain, mixer_input_weight, state_map_weight, step_weight, mixer_output_weight, mixer_input_taps, state_map_taps, step_bias, decay_logarithm, head_skip_weight, gated_norm_gain, cotangent):
    parameter_tree = tuple((leaf_item.astype(jnp.float32) for leaf_item in (query_key_value_weight, attention_output_weight, attention_gain, feedforward_gain, gate_up_weight, adapter_down, adapter_up, down_weight, shared_projection_weight, mixer_gain, mixer_input_weight, state_map_weight, step_weight, mixer_output_weight, mixer_input_taps, state_map_taps, step_bias, decay_logarithm, head_skip_weight, gated_norm_gain)))
    bin_count = lengths.shape[0] * lengths.shape[1]
    len_rows = lengths.reshape(bin_count, lengths.shape[2])
    bin_rows = hidden.shape[1] // lengths.shape[1]
    stepper = jax.checkpoint(bin_forward)

    def forward(weights, hid_all, emb_all):
        hid_bins = hid_all.reshape(bin_count, bin_rows, hid_all.shape[2])
        emb_bins = emb_all.reshape(bin_count, bin_rows, emb_all.shape[2])

        def apply_bin(items):
            return stepper(weights, items[0], items[1], items[2])
        outputs = lax.map(apply_bin, (hid_bins, emb_bins, len_rows))
        return outputs.reshape(hid_all.shape)
    result, pullback = jax.vjp(forward, parameter_tree, hidden.astype(jnp.float32), embedding.astype(jnp.float32))
    grads, d_hidden, d_embedding = pullback(cotangent.astype(jnp.float32))
    return (result.astype(jnp.bfloat16), d_hidden.astype(jnp.bfloat16), d_embedding.astype(jnp.bfloat16), grads[0], grads[1], grads[2], grads[3], grads[4], grads[5], grads[6], grads[7], grads[8], grads[9], grads[10], grads[11], grads[12], grads[13], grads[14], grads[15], grads[16], grads[17], grads[18], grads[19])
```

```python
from functools import partial
from types import SimpleNamespace

import jax
import jax.numpy as jnp
from jax import lax
from jax.experimental import pallas as pl
from jax.experimental.pallas import tpu as pltpu
from jax.sharding import PartitionSpec as P

HEAD = 128
EPSILON = 1e-05
ROPE_BASE = 10000.0
MASKED = -1e30
TOP_PRECISION = lax.Precision.HIGHEST
F32 = jnp.float32
BF16 = jnp.bfloat16


def layout(len_row, places):
    bounds = jnp.cumsum(len_row)[:-1]
    passed = places[:, None] >= bounds[None, :]
    segment = jnp.sum(passed.astype(jnp.int32), axis=1)
    starts = jnp.max(jnp.where(passed, bounds[None, :], 0), axis=1)
    position = places - starts
    valid = segment < bounds.shape[0]
    allowed = (segment[:, None] == segment[None, :]) & (places[None, :] <= places[:, None])
    return (segment, position, valid, allowed)


def rope_tables(position):
    half = HEAD // 2
    frequency = ROPE_BASE ** (-2.0 * jnp.arange(half, dtype=F32) / HEAD)
    angles = position.astype(F32)[:, None] * frequency[None, :]
    cosine, sine = jnp.cos(angles), jnp.sin(angles)
    return jnp.concatenate([cosine, cosine], axis=1), jnp.concatenate([-sine, sine], axis=1)


def rows_down(x, count):
    return x if count == 0 else pltpu.roll(x, count, 0)


def rows_up(x, count):
    return x if count == 0 else pltpu.roll(x, x.shape[0] - count, 0)


def conv_taps(x, taps_ref, same_ref):
    summed = x * taps_ref[0:1, :]
    for j in range(1, taps_ref.shape[0]):
        summed = summed + rows_down(x, j) * same_ref[:, j : j + 1] * taps_ref[j : j + 1, :]
    return summed


def conv_taps_back(x, d_out, taps_ref, same_ref, d_taps_ref, cols):
    d_x = d_out * taps_ref[0:1, cols]
    d_taps_ref[0:1, cols] = jnp.sum(d_out * x, axis=0, keepdims=True)
    for j in range(1, taps_ref.shape[0]):
        kept = d_out * same_ref[:, j : j + 1]
        d_taps_ref[j : j + 1, cols] = jnp.sum(kept * rows_down(x, j), axis=0, keepdims=True)
        d_x = d_x + rows_up(kept * taps_ref[j : j + 1, cols], j)
    return d_x


def exact(a, b, dims):
    return lax.dot_general(
        a, b, (dims, ((), ())), precision=TOP_PRECISION, preferred_element_type=F32
    )


def fast(a, b, dims):
    return lax.dot_general(
        a.astype(BF16), b.astype(BF16), (dims, ((), ())), preferred_element_type=F32
    )


PLAIN = ((1,), (0,))
BY_COLS = ((1,), (1,))
BY_ROWS = ((0,), (0,))


def triangle(rows):
    t = lax.broadcasted_iota(jnp.int32, (rows, rows), 0)
    s = lax.broadcasted_iota(jnp.int32, (rows, rows), 1)
    return t, s


def step_terms(step_ref, bias_ref, decay_ref, rows):
    t, s = triangle(rows)
    raw = step_ref[...] + bias_ref[...]
    step = jnp.maximum(raw, 0.0) + jnp.log1p(jnp.exp(-jnp.abs(raw)))
    log_decay = -step * jnp.exp(decay_ref[...])
    running = exact((s <= t).astype(F32), log_decay, PLAIN)
    running_t = exact(log_decay, (t <= s).astype(F32), BY_ROWS)
    step_t = exact(step, (t == s).astype(F32), BY_ROWS)
    return raw, step, log_decay, running, running_t, step_t


def decayed(running, running_t, h, allowed):
    gap = running[:, h : h + 1] - running_t[h : h + 1, :]
    return jnp.exp(jnp.where(allowed, gap, MASKED))


def mix_kernel(
    gate_ref, state_ref, step_ref, taps_x_ref, taps_bc_ref, bias_ref, decay_ref, skip_ref,
    same_ref, allowed_ref, d_scaled_ref, gated_ref, sums_ref,
):
    rows = state_ref.shape[0]
    size = state_ref.shape[1] // 2
    heads = step_ref.shape[1]
    lanes = 128
    per = lanes * heads // gate_ref.shape[2]
    allowed = allowed_ref[...] > 0.0
    _, _, _, running, running_t, step_t = step_terms(step_ref, bias_ref, decay_ref, rows)
    conv_bc = conv_taps(state_ref[...], taps_bc_ref, same_ref)
    state = conv_bc * jax.nn.sigmoid(conv_bc)
    affinity = exact(state[:, size:], state[:, :size], BY_COLS)
    lane = lax.broadcasted_iota(jnp.int32, (rows, lanes), 1) * per // lanes
    squares = jnp.zeros((rows, lanes), F32)
    weighted = jnp.zeros((rows, lanes), F32)
    for group in range(gate_ref.shape[2] // lanes):
        cols = slice(group * lanes, (group + 1) * lanes)
        x = gate_ref[1, :, cols]
        conv = x * taps_x_ref[0:1, cols]
        for j in range(1, taps_x_ref.shape[0]):
            conv = conv + rows_down(x, j) * same_ref[:, j : j + 1] * taps_x_ref[j : j + 1, cols]
        act = conv * jax.nn.sigmoid(conv)
        mixed = act * skip_ref[0:1, cols]
        for i in range(per):
            h = group * per + i
            mixing = decayed(running, running_t, h, allowed) * affinity * step_t[h : h + 1, :]
            mixed = mixed + jnp.where(lane == i, fast(mixing, act, PLAIN), 0.0)
        z = gate_ref[0, :, cols]
        gated = mixed * (z * jax.nn.sigmoid(z))
        gated_ref[:, cols] = gated
        squares = squares + gated * gated
        weighted = weighted + gated * d_scaled_ref[:, cols]
    sums_ref[:, 0:1] = jnp.sum(squares, axis=1, keepdims=True)
    sums_ref[:, 1:2] = jnp.sum(weighted, axis=1, keepdims=True)


def mix_back_kernel(
    gate_ref, state_ref, step_ref, taps_x_ref, taps_bc_ref, bias_ref, decay_ref, skip_ref,
    same_ref, allowed_ref, d_scaled_ref, gated_ref, scales_ref,
    d_gate_ref, d_state_ref, d_step_ref, d_taps_x_ref, d_taps_bc_ref, d_bias_ref, d_decay_ref,
    d_skip_ref,
):
    rows = state_ref.shape[0]
    size = state_ref.shape[1] // 2
    heads = step_ref.shape[1]
    lanes = 128
    per = lanes * heads // gate_ref.shape[2]
    allowed = allowed_ref[...] > 0.0
    raw, step, log_decay, running, running_t, step_t = step_terms(
        step_ref, bias_ref, decay_ref, rows
    )
    conv_bc = conv_taps(state_ref[...], taps_bc_ref, same_ref)
    sig_bc = jax.nn.sigmoid(conv_bc)
    state = conv_bc * sig_bc
    affinity = exact(state[:, size:], state[:, :size], BY_COLS)
    lane = lax.broadcasted_iota(jnp.int32, (rows, lanes), 1) * per // lanes
    head_lane = lax.broadcasted_iota(jnp.int32, (rows, heads), 1)
    head_row = lax.broadcasted_iota(jnp.int32, (heads, rows), 0)
    d_affinity = jnp.zeros((rows, rows), F32)
    d_run = jnp.zeros((rows, heads), F32)
    d_step_t = jnp.zeros((heads, rows), F32)
    for group in range(gate_ref.shape[2] // lanes):
        cols = slice(group * lanes, (group + 1) * lanes)
        x = gate_ref[1, :, cols]
        conv = x * taps_x_ref[0:1, cols]
        for j in range(1, taps_x_ref.shape[0]):
            conv = conv + rows_down(x, j) * same_ref[:, j : j + 1] * taps_x_ref[j : j + 1, cols]
        sig = jax.nn.sigmoid(conv)
        act = conv * sig
        z = gate_ref[0, :, cols]
        sig_z = jax.nn.sigmoid(z)
        d_gated = d_scaled_ref[:, cols] * scales_ref[:, 0:1] - gated_ref[:, cols] * scales_ref[:, 1:2]
        d_mixed = d_gated * (z * sig_z)
        mixed = act * skip_ref[0:1, cols]
        d_act = d_mixed * skip_ref[0:1, cols]
        d_skip_ref[0:1, cols] = jnp.sum(d_mixed * act, axis=0, keepdims=True)
        for i in range(per):
            h = group * per + i
            decay = decayed(running, running_t, h, allowed)
            weight = affinity * step_t[h : h + 1, :]
            mixing = decay * weight
            mixed = mixed + jnp.where(lane == i, fast(mixing, act, PLAIN), 0.0)
            d_act = d_act + jnp.where(lane == i, fast(mixing, d_mixed, BY_ROWS), 0.0)
            d_mixing = fast(jnp.where(lane == i, d_mixed, 0.0), act, BY_COLS) * decay
            d_affinity = d_affinity + d_mixing * step_t[h : h + 1, :]
            by_aff = d_mixing * affinity
            d_step_t = d_step_t + jnp.where(
                head_row == h, jnp.sum(by_aff, axis=0, keepdims=True), 0.0
            )
            by_gap = jnp.sum(by_aff * step_t[h : h + 1, :], axis=1, keepdims=True)
            d_run = d_run + jnp.where(head_lane == h, by_gap, 0.0)
        d_gate_ref[0, :, cols] = (d_gated * mixed * (sig_z * (1.0 + z * (1.0 - sig_z)))).astype(BF16)
        d_conv = d_act * (sig * (1.0 + conv * (1.0 - sig)))
        d_x = conv_taps_back(x, d_conv, taps_x_ref, same_ref, d_taps_x_ref, cols)
        d_gate_ref[1, :, cols] = d_x.astype(BF16)
    t, s = triangle(rows)
    eye = (t == s).astype(F32)
    d_run = d_run - exact(eye, d_step_t * step_t, BY_COLS)
    d_log = exact((s >= t).astype(F32), d_run, PLAIN)
    d_step = exact(eye, d_step_t, BY_COLS) - jnp.exp(decay_ref[...]) * d_log
    d_raw = d_step * jax.nn.sigmoid(raw)
    d_step_ref[...] = d_raw
    d_bias_ref[...] = jnp.sum(d_raw, axis=0, keepdims=True)
    d_decay_ref[...] = jnp.sum(d_log * log_decay, axis=0, keepdims=True)
    d_b = exact(d_affinity, state[:, size:], BY_ROWS)
    d_c = exact(d_affinity, state[:, :size], PLAIN)
    d_silu = sig_bc * (1.0 + conv_bc * (1.0 - sig_bc))
    for part, d_part in enumerate((d_b, d_c)):
        cols = slice(part * size, (part + 1) * size)
        d_conv = d_part * d_silu[:, cols]
        d_x = conv_taps_back(
            state_ref[:, cols], d_conv, taps_bc_ref, same_ref, d_taps_bc_ref, cols
        )
        d_state_ref[:, cols] = d_x.astype(BF16)


def turned(x, cos_ref, sin_ref, sign):
    return x * cos_ref[...] + pltpu.roll(x, HEAD // 2, 1) * (sign * sin_ref[...])


def probabilities(query, key, allowed):
    scores = fast(query, key, BY_COLS) * HEAD ** (-0.5)
    scores = jnp.where(allowed, scores, MASKED)
    raised = jnp.exp(scores - jnp.max(scores, axis=1, keepdims=True))
    return raised / jnp.sum(raised, axis=1, keepdims=True)


def attend_kernel(qkv_ref, cos_ref, sin_ref, allowed_ref, low_ref, attended_ref):
    allowed = allowed_ref[...] > 0.0
    width = attended_ref.shape[1]
    for h in range(width // HEAD):
        q, k, v = (slice(i * width + h * HEAD, i * width + (h + 1) * HEAD) for i in range(3))
        query = turned(qkv_ref[:, q], cos_ref, sin_ref, 1.0).astype(BF16)
        key = turned(qkv_ref[:, k], cos_ref, sin_ref, 1.0).astype(BF16)
        value = qkv_ref[:, v].astype(BF16)
        low_ref[:, q] = query
        low_ref[:, k] = key
        low_ref[:, v] = value
        probs = probabilities(query, key, allowed)
        attended_ref[:, q] = fast(probs, value, PLAIN).astype(BF16)


def attend_back_kernel(low_ref, d_ref, cos_ref, sin_ref, allowed_ref, d_qkv_ref):
    allowed = allowed_ref[...] > 0.0
    width = d_ref.shape[1]
    for h in range(width // HEAD):
        q, k, v = (slice(i * width + h * HEAD, i * width + (h + 1) * HEAD) for i in range(3))
        query, key, value = low_ref[:, q], low_ref[:, k], low_ref[:, v]
        d_out = d_ref[:, q].astype(BF16)
        probs = probabilities(query, key, allowed)
        d_qkv_ref[:, v] = fast(probs, d_out, BY_ROWS).astype(BF16)
        d_probs = fast(d_out, value, BY_COLS)
        inner = jnp.sum(probs * d_probs, axis=1, keepdims=True)
        d_scores = (probs * (d_probs - inner) * HEAD ** (-0.5)).astype(BF16)
        d_query = fast(d_scores, key, PLAIN)
        d_key = fast(d_scores, query, BY_ROWS)
        d_qkv_ref[:, q] = turned(d_query, cos_ref, sin_ref, -1.0).astype(BF16)
        d_qkv_ref[:, k] = turned(d_key, cos_ref, sin_ref, -1.0).astype(BF16)


def in_vmem(kernel, outs, args, flops):
    size = sum(x.size * x.dtype.itemsize for x in tuple(args) + tuple(outs))
    return pl.pallas_call(
        kernel,
        out_shape=outs,
        in_specs=[pl.BlockSpec(memory_space=pltpu.VMEM)] * len(args),
        out_specs=[pl.BlockSpec(memory_space=pltpu.VMEM)] * len(outs),
        compiler_params=pltpu.CompilerParams(vmem_limit_bytes=40 * 2**20),
        cost_estimate=pl.CostEstimate(flops=flops, bytes_accessed=size, transcendentals=0),
    )(*args)


def gated_gelu(gate_up):
    half = gate_up.shape[1] // 2
    return jax.nn.gelu(gate_up[:, :half], approximate=True) * gate_up[:, half:]


def total(values):
    summed = values[0]
    for value in values[1:]:
        summed = summed + value
    return summed


def after(x, done):
    mark = done[(-1,) * done.ndim].astype(F32)
    return x + jnp.minimum(jnp.abs(mark), 0.0).astype(x.dtype)


class Links:
    def __init__(self, n_dp, n_t):
        self.n_dp = n_dp
        self.n_t = n_t
        self.chips = n_dp // 2
        self.chip_bits = self.chips.bit_length() - 1
        self.z_bits = n_t.bit_length() - 1
        d = lax.axis_index("dp")
        self.d = d
        self.core = d % 2
        self.chip = d // 2
        self.t = lax.axis_index("tensor")

    def core_swap(self, x):
        return lax.ppermute(x, "dp", [(i, i ^ 1) for i in range(self.n_dp)])

    def chip_swap(self, x, rel):
        return lax.ppermute(x, "dp", [(i, i ^ (rel << 1)) for i in range(self.n_dp)])

    def z_swap(self, x, rel):
        return lax.ppermute(x, "tensor", [(i, i ^ rel) for i in range(self.n_t)])

    def row_parts(self, rows):
        count = max(1, min(self.chip_bits, rows // 16))
        units = rows // 16
        edges = [0] + [16 * ((units * (i + 1)) // count) for i in range(count)]
        edges[-1] = rows
        return [(edges[i], edges[i + 1]) for i in range(count)]

    def chip_rs(self, terms, axis, direct=False):
        if direct:
            blocks = [
                lax.index_in_dim(terms, rel, axis, keepdims=False) for rel in range(self.chips)
            ]
            return total([block.astype(F32) for block in self.chip_a2a(blocks)])
        outs = []
        bits = self.chip_bits
        for number, (low, high) in enumerate(self.row_parts(terms.shape[axis + 1])):
            cur = lax.slice_in_dim(terms, low, high, axis=axis + 1)
            cur = cur.reshape(cur.shape[:axis] + (2,) * bits + cur.shape[axis + 1 :])
            left = list(range(bits))[::-1]
            for step in range(bits):
                bit = (number + step) % bits
                at = axis + left.index(bit)
                left.remove(bit)
                keep = lax.index_in_dim(cur, 0, at, keepdims=False)
                send = lax.index_in_dim(cur, 1, at, keepdims=False)
                got = self.chip_swap(send.astype(BF16), 1 << bit)
                cur = keep.astype(F32) + got.astype(F32)
            outs.append(cur)
        return outs[0] if len(outs) == 1 else jnp.concatenate(outs, axis=axis)

    def chip_ag(self, x, axis, direct=False):
        if direct:
            return jnp.stack(self.chip_a2a([x] * self.chips), axis=axis)
        bits = self.chip_bits
        outs = []
        for number, (low, high) in enumerate(self.row_parts(x.shape[axis])):
            blocks = {0: lax.slice_in_dim(x, low, high, axis=axis)}
            for step in range(bits):
                bit = (number + step) % bits
                for rel in list(blocks):
                    blocks[rel | (1 << bit)] = self.chip_swap(blocks[rel], 1 << bit)
            outs.append([blocks[rel] for rel in range(self.chips)])
        merged = []
        for rel in range(self.chips):
            pieces = [part[rel] for part in outs]
            merged.append(pieces[0] if len(pieces) == 1 else jnp.concatenate(pieces, axis=axis))
        return jnp.stack(merged, axis=axis)

    def chip_a2a(self, blocks):
        return [blocks[0]] + [self.chip_swap(blocks[rel], rel) for rel in range(1, self.chips)]

    def chip_sum(self, x):
        total = x
        for rel in range(1, self.chips):
            moved = jnp.stack([x[i ^ rel] for i in range(self.chips)], 0)
            total = total + self.chip_swap(moved, rel)
        return total

    def z_sum(self, x):
        return total([x] + [self.z_swap(x, rel) for rel in range(1, self.n_t)])

    def dp_sum(self, x):
        x = x + self.core_swap(x)
        return total(self.chip_a2a([x] * self.chips))

    def z_rs(self, terms, axis):
        bits = self.z_bits
        cur = terms.reshape(terms.shape[:axis] + (2,) * bits + terms.shape[axis + 1 :])
        left = list(range(bits))[::-1]
        for bit in range(bits):
            at = axis + left.index(bit)
            left.remove(bit)
            keep = lax.index_in_dim(cur, 0, at, keepdims=False)
            send = lax.index_in_dim(cur, 1, at, keepdims=False)
            got = self.z_swap(send.astype(BF16), 1 << bit)
            cur = keep.astype(F32) + got.astype(F32)
        return cur

    def z_ag(self, x, axis):
        blocks = {0: x}
        for bit in range(self.z_bits)[::-1]:
            for rel in list(blocks):
                blocks[rel | (1 << bit)] = self.z_swap(blocks[rel], 1 << bit)
        return jnp.stack([blocks[rel] for rel in range(self.n_t)], axis=axis)

    def by_index(self, x, axis, own):
        count = x.shape[axis]
        return jnp.concatenate(
            [lax.dynamic_slice_in_dim(x, own ^ i, 1, axis=axis) for i in range(count)], axis=axis
        )

    def rows_by_t(self, x):
        rows = x.shape[0]
        split = x.reshape((self.n_t, rows // self.n_t) + x.shape[1:])
        return self.by_index(split, 0, self.t).reshape(x.shape)


def core_pair(links, x, axis):
    return jnp.concatenate([x, links.core_swap(x)], axis=axis)


def core_rs(links, x, axis):
    half = x.shape[axis] // 2
    own = lax.slice_in_dim(x, 0, half, axis=axis)
    other = lax.slice_in_dim(x, half, 2 * half, axis=axis)
    return own + links.core_swap(other.astype(BF16)).astype(F32)


def dotf(spec, a, b):
    return jnp.einsum(spec, a, b, preferred_element_type=F32)


def dotl(spec, a, b):
    return jnp.einsum(spec, a, b, preferred_element_type=F32).astype(BF16)


def proj_spread(links, w):
    rows = links.z_ag(w, 0)
    if links.chips == links.n_t:
        blocks = [
            lax.dynamic_index_in_dim(rows, links.chip ^ links.t ^ rel, 0, keepdims=False)
            for rel in range(links.chips)
        ]
    else:
        rows = links.by_index(rows, 0, links.t).reshape(links.chips, -1, w.shape[1])
        blocks = [
            lax.dynamic_index_in_dim(rows, links.chip ^ rel, 0, keepdims=False)
            for rel in range(links.chips)
        ]
    came = jnp.stack(links.chip_a2a(blocks), 0)
    return jnp.stack([came, links.core_swap(came)], 1)


def proj_collect(links, own, other):
    mine = (own + links.core_swap(other).astype(F32)).astype(BF16)
    blocks = [mine[:, rel] for rel in range(links.chips)]
    rows = jnp.stack(links.chip_a2a(blocks), 0)
    if links.chips == links.n_t:
        rows = links.by_index(rows, 0, links.chip ^ links.t)
    else:
        rows = links.by_index(rows, 0, links.chip).reshape(links.n_t, -1, own.shape[2])
        rows = links.by_index(rows, 0, links.t)
    return links.z_rs(rows, 0)


def core_halves(links, x):
    split = x.reshape(x.shape[:-1] + (2, x.shape[-1] // 2))
    return links.by_index(split, x.ndim - 1, links.core).reshape(x.shape)


def enter(links, w, m):
    rows = m.hid.shape[0]
    joined = links.rows_by_t(jnp.concatenate([m.hid, m.emb], axis=1))
    wide = joined.astype(F32)
    m.inverse = lax.rsqrt(jnp.mean(wide * wide, axis=1) + EPSILON)
    half = joined.shape[1] // links.n_dp
    blocks = []
    for rel in range(links.chips):
        at = 2 * (links.chip ^ rel)
        pieces = [
            lax.dynamic_slice_in_dim(joined, (at + (links.core ^ j)) * half, half, axis=1)
            for j in range(2)
        ]
        blocks.append(jnp.concatenate(pieces, axis=1))
    m.joined = jnp.stack(links.chip_a2a(blocks), 0)
    places = jnp.arange(rows, dtype=jnp.int32)
    m.true = layout(m.lens, places)
    _, position, _, allowed = layout(m.lens, links.rows_by_t(places))
    m.allowed_rel = allowed.astype(F32)
    m.cos, m.sin = rope_tables(position)


def attend(links, w, m):
    wide = m.joined.astype(F32) * m.inv_attn[:, :, None]
    m.attn_in = lax.optimization_barrier((wide * w.g_attn).astype(BF16))
    qkv = links.chip_rs(dotl("crd,dn->crn", m.attn_in, w.qkv), 0)
    rows, width = qkv.shape[0], qkv.shape[1] // 3
    outs = (
        jax.ShapeDtypeStruct((rows, 3 * width), BF16),
        jax.ShapeDtypeStruct((rows, width), BF16),
    )
    args = (qkv, m.cos, m.sin, m.allowed_rel)
    m.qkv_low, attended = in_vmem(attend_kernel, outs, args, 4 * rows * rows * width)
    m.attended = links.chip_ag(attended, 0, direct=True)


def z_split(links, x, axis):
    rows = x.shape[axis]
    return x.reshape(x.shape[:axis] + (links.n_t, rows // links.n_t) + x.shape[axis + 1 :])


def z_join(x, axis):
    return x.reshape(x.shape[:axis] + (-1,) + x.shape[axis + 2 :])


def attend_out(links, w, m):
    part = dotl("crn,nd->crd", m.attended, w.out)
    summed = links.z_rs(z_split(links, part, 1), 1)
    rows = summed.shape[1]
    m.joined_z = m.joined[:, :rows].astype(F32)
    m.inv_attn_z = m.inv_attn[:, :rows]
    mid = m.joined_z + summed
    m.mid = mid
    squares = links.chip_sum(jnp.sum(mid * mid, axis=2))
    width = mid.shape[2] * links.chips
    m.inv_mlp = lax.rsqrt(squares / width + EPSILON)
    low = (mid * m.inv_mlp[:, :, None] * w.g_mlp).astype(BF16)
    m.mlp_in = z_join(links.z_ag(low, 1), 1)


def feed(links, w, m):
    summed = links.chip_rs(dotl("crd,dn->crn", m.mlp_in, w.gate_up), 0)
    units = 2 * w.down.shape[0]
    m.adapter = summed[:, units:].astype(BF16)
    gate_up = summed[:, :units] + dotf("ra,an->rn", m.adapter, w.adapter_up)
    activated, m.gate_back = jax.vjp(gated_gelu, gate_up)
    m.hidden = links.chip_ag(activated.astype(BF16), 0, direct=True)


def feed_out(links, w, m):
    part = dotl("crn,nd->crd", m.hidden, w.down)
    summed = links.z_rs(z_split(links, part, 1), 1)
    m.block = (m.mid + summed).astype(BF16)
    m.block = core_halves(links, m.block)
    part = dotl("crd,xydn->xycrn", m.block, w.proj)
    part = links.by_index(links.by_index(part, 1, links.core), 0, links.chip)
    part = z_join(part, 0).transpose(1, 2, 0, 3)
    part = part.reshape(part.shape[:2] + (-1,))
    shared = links.chip_rs(part, 0, direct=True).astype(BF16)
    whole = links.by_index(links.z_ag(shared, 0), 0, links.t)
    shared_full = whole.reshape(-1, whole.shape[2])
    m.mamba_in = m.hid.astype(F32) + shared_full.astype(F32)
    own = z_split(links, m.hid, 0)
    own = lax.dynamic_index_in_dim(own, links.t, 0, keepdims=False)
    m.mamba_in_z = own.astype(F32) + shared.astype(F32)


def mix(links, w, m):
    taps_x, taps_bc, step_bias, decay_log, skip, gate_gain = w.smalls
    segment, _, valid, allowed = m.true
    mamba_in = m.mamba_in
    inverse = lax.rsqrt(jnp.mean(mamba_in * mamba_in, axis=1, keepdims=True) + EPSILON)
    ssm_in = (mamba_in * inverse * w.g_mamba).astype(BF16)
    gate_x = dotf("td,kdc->ktc", ssm_in, w.w_in)
    state_io = dotf("td,dn->tn", ssm_in, w.bc)
    step_raw = dotf("td,dn->tn", ssm_in, w.dt)
    grad_low = m.cot * valid[:, None].astype(BF16)
    d_norm = dotf("tn,in->ti", grad_low, w.mout)
    d_scaled = d_norm * gate_gain
    rows, width = gate_x.shape[1:]
    heads = step_raw.shape[1]
    earlier = [jnp.pad(segment, (j, 0), constant_values=-1)[:rows] for j in range(taps_x.shape[0])]
    same = jnp.stack([(e == segment).astype(F32) for e in earlier], 1)
    skips = jnp.repeat(skip, width // heads)[None, :]
    args = (gate_x, state_io, step_raw, taps_x, taps_bc, step_bias[None, :], decay_log[None, :])
    args += (skips, same, allowed.astype(F32), d_scaled)
    outs = (jax.ShapeDtypeStruct((rows, width), F32), jax.ShapeDtypeStruct((rows, 2), F32))
    gated, sums = in_vmem(mix_kernel, outs, args, 4 * rows * rows * width)
    inner = width * links.n_t
    sums = links.z_sum(sums)
    squares, weighted = sums[:, 0], sums[:, 1]
    row_scale = lax.rsqrt(squares / inner + EPSILON)
    m.gated_norm = (gated * row_scale[:, None] * gate_gain).astype(BF16)
    m.mamba_out = dotl("ti,in->tn", m.gated_norm, w.mout)

    grad_gain = jnp.sum(d_norm * gated * row_scale[:, None], axis=0)
    scales = jnp.stack([row_scale, row_scale**3 * weighted / inner], 1)
    outs = (
        jax.ShapeDtypeStruct(gate_x.shape, BF16),
        jax.ShapeDtypeStruct(state_io.shape, BF16),
        jax.ShapeDtypeStruct(step_raw.shape, F32),
        jax.ShapeDtypeStruct(taps_x.shape, F32),
        jax.ShapeDtypeStruct(taps_bc.shape, F32),
        jax.ShapeDtypeStruct((1, heads), F32),
        jax.ShapeDtypeStruct((1, heads), F32),
        jax.ShapeDtypeStruct((1, width), F32),
    )
    args += (gated, scales)
    grads = in_vmem(mix_back_kernel, outs, args, 16 * rows * rows * width)
    m.gate_x_low, d_state_io, d_step, d_taps_x, d_taps_bc, d_bias, d_decay, d_skip = grads
    d_skip = jnp.sum(d_skip.reshape(heads, width // heads), axis=1)
    m.step_low = d_step.astype(BF16)
    part_in = dotf("ktc,kdc->td", m.gate_x_low, w.w_in) + dotf("tn,dn->td", m.step_low, w.dt)
    terms = jnp.concatenate([part_in.astype(BF16), d_state_io], axis=1)
    m.terms = z_split(links, links.rows_by_t(terms), 0)
    m.ssm_in = ssm_in
    m.ssm_in_z = own_rows(links, ssm_in)
    m.grad_low = grad_low
    m.sums_dp = (d_taps_x, grad_gain, d_bias[0], d_decay[0], d_skip)
    m.d_taps_bc = d_taps_bc


def settle(links, w, m):
    summed = links.z_rs(m.terms, 0)
    model_width = m.mamba_in_z.shape[1]
    m.state_low = summed[:, model_width:].astype(BF16)
    dy = summed[:, :model_width] + dotf("tn,dn->td", m.state_low, w.bc)
    v = m.mamba_in_z
    inv = lax.rsqrt(jnp.mean(v * v, axis=1, keepdims=True) + EPSILON)
    scaled = dy * w.g_mamba
    dv = inv * scaled - v * (inv**3 * jnp.mean(scaled * v, axis=1, keepdims=True))
    grad_g_mamba = jnp.sum(dy * v * inv, axis=0)
    m.sums_all = (m.d_taps_bc, grad_g_mamba)
    m.d_mamba = dv + own_rows(links, m.grad_low).astype(F32)
    m.shared_low = links.chip_ag(m.d_mamba.astype(BF16), 0, direct=True)
    split = m.shared_low.reshape(m.shared_low.shape[:2] + w.proj.shape[:2] + (-1,))
    m.shared_cols = links.by_index(links.by_index(split, 3, links.core), 2, links.chip)
    d_block = core_halves(links, dotf("crxyn,xydn->crd", m.shared_cols, w.proj))
    m.d_block = d_block
    m.mlp_low = z_join(links.z_ag(d_block.astype(BF16), 1), 1)


def own_rows(links, x):
    return lax.dynamic_index_in_dim(z_split(links, x, 0), links.t, 0, keepdims=False)


def finish_output(links, micro):
    terms = jnp.stack([z_split(links, links.rows_by_t(m.mamba_out), 0) for m in micro], 0)
    summed = links.z_rs(terms, 1)
    base = jnp.stack([m.mamba_in_z for m in micro], 0)
    valid = jnp.stack([own_rows(links, m.true[2]) for m in micro], 0)
    low = ((base + summed) * valid[:, :, None].astype(F32)).astype(BF16)
    whole = links.by_index(links.z_ag(low, 1), 1, links.t)
    return z_join(whole, 1)


def feed_back(links, w, m):
    part = dotl("crd,nd->crn", m.mlp_low, w.down)
    d_hidden = links.chip_rs(part, 0)
    (d_gate_up,) = m.gate_back(d_hidden)
    m.gate_up_own = d_gate_up.astype(BF16)
    part = dotl("rn,an->ra", m.gate_up_own, w.adapter_up)
    m.gate_up_low = links.chip_ag(jnp.concatenate([m.gate_up_own, part], 1), 0)


def feed_back_out(links, w, m):
    part = dotl("crn,dn->crd", m.gate_up_low, w.gate_up)
    dy = links.z_rs(z_split(links, part, 1), 1)
    scaled = dy * w.g_mlp
    v, inv = m.mid, m.inv_mlp
    weighted = links.chip_sum(jnp.sum(scaled * v, axis=2))
    width = v.shape[2] * links.chips
    dv = scaled * inv[:, :, None] - v * (inv**3 * weighted / width)[:, :, None]
    m.grad_g_mlp = jnp.sum(dy * v * inv[:, :, None], axis=(0, 1))
    m.d_mid = dv + m.d_block
    m.attn_low = z_join(links.z_ag(m.d_mid.astype(BF16), 1), 1)


def attend_back(links, w, m):
    part = dotl("crd,nd->crn", m.attn_low, w.out)
    d_attended = links.chip_rs(part, 0, direct=True)
    rows, width = d_attended.shape
    outs = (jax.ShapeDtypeStruct((rows, 3 * width), BF16),)
    args = (m.qkv_low, d_attended, m.cos, m.sin, m.allowed_rel)
    (d_qkv,) = in_vmem(attend_back_kernel, outs, args, 10 * rows * rows * width)
    m.d_qkv = links.chip_ag(d_qkv, 0)


def leave(links, w, m):
    part = dotl("crn,dn->crd", m.d_qkv, w.qkv)
    dy = links.z_rs(z_split(links, part, 1), 1)
    scaled = dy * w.g_attn
    v, inv = m.joined_z, m.inv_attn_z
    weighted = links.chip_sum(jnp.sum(scaled * v, axis=2))
    width = v.shape[2] * links.chips
    dv = scaled * inv[:, :, None] - v * (inv**3 * weighted / width)[:, :, None]
    m.grad_g_attn = jnp.sum(dy * v * inv[:, :, None], axis=(0, 1))
    d_joined = (dv + m.d_mid).astype(BF16)
    came = jnp.stack(links.chip_a2a([d_joined[rel] for rel in range(links.chips)]), 0)
    rows = came.shape[1]
    came = came.reshape(links.chips, rows, 2, -1)
    came = links.by_index(links.by_index(came, 2, links.core), 0, links.chip)
    came = came.transpose(1, 0, 2, 3).reshape(rows, -1)
    model_width = m.d_mamba.shape[1]
    d_hid = (came[:, :model_width].astype(F32) + m.d_mamba).astype(BF16)
    both = jnp.concatenate([d_hid, came[:, model_width:]], axis=1)
    whole = links.by_index(links.z_ag(both, 0), 0, links.t)
    whole = whole.reshape(-1, both.shape[1])
    m.d_hid, m.d_emb = whole[:, :model_width], whole[:, model_width:]


def local(
    hidden,
    embedding,
    lengths,
    query_key_value_weight,
    attention_output_weight,
    attention_gain,
    feedforward_gain,
    gate_up_weight,
    adapter_down,
    adapter_up,
    down_weight,
    shared_projection_weight,
    mixer_gain,
    mixer_input_weight,
    state_map_weight,
    step_weight,
    mixer_output_weight,
    mixer_input_taps,
    state_map_taps,
    step_bias,
    decay_logarithm,
    head_skip_weight,
    gated_norm_gain,
    cotangent,
    n_dp,
    n_t,
):
    links = Links(n_dp, n_t)
    smalls = (
        mixer_input_taps,
        state_map_taps,
        step_bias,
        decay_logarithm,
        head_skip_weight,
        gated_norm_gain,
    )
    micro = [
        SimpleNamespace(
            hid=hidden[b], emb=embedding[b], lens=lengths[b, 0], cot=cotangent[b]
        )
        for b in range(hidden.shape[0])
    ]
    w = SimpleNamespace()
    gains = core_pair(links, jnp.stack([attention_gain, feedforward_gain], 0), 1).astype(F32)
    w.g_attn, w.g_mlp = gains[0], gains[1]
    flat = jnp.concatenate([query_key_value_weight[:, i] for i in range(3)], axis=1)
    w.qkv = lax.optimization_barrier(core_pair(links, flat, 0))
    def stage(work, m):
        with jax.named_scope(f"{work.__name__}_micro{micro.index(m)}"):
            work(links, w, m)

    for m in micro:
        stage(enter, m)
    inverses = jnp.stack([m.inverse for m in micro], 0)
    inverses = jnp.stack(links.chip_a2a([inverses] * links.chips), 1)
    for b, m in enumerate(micro):
        m.inv_attn = inverses[b]
    first = micro[0]
    units = gate_up_weight.shape[2]
    up_own = adapter_up.reshape(adapter_up.shape[0], 2 * units)
    cols = jnp.concatenate([gate_up_weight[:, 0], gate_up_weight[:, 1], adapter_down], axis=1)
    w.out = lax.optimization_barrier(core_pair(links, attention_output_weight, 1))
    w.gate_up = lax.optimization_barrier(core_pair(links, cols, 0))
    w.down = lax.optimization_barrier(core_pair(links, down_weight, 1))
    state_cols, step_cols = state_map_weight.shape[1], step_weight.shape[1]
    packed = jnp.concatenate([state_map_weight, step_weight, mixer_gain[:, None]], axis=1)

    w.smalls = smalls
    stages = [attend, attend_out, feed, feed_out, mix, settle]
    stages += [feed_back, feed_back_out, attend_back, leave]
    entries = ["joined", "attended", "mlp_in", "hidden", "mamba_in", "terms"]
    entries += ["mlp_low", "gate_up_low", "attn_low", "d_qkv"]
    for work, entry in zip(stages, entries):
        for m in micro:
            setattr(m, entry, lax.optimization_barrier(getattr(m, entry)))
            stage(work, m)
        if work is attend:
            w.adapter_up = lax.all_gather(after(up_own, first.joined), "dp", axis=0, tiled=True)
            w.proj = proj_spread(links, shared_projection_weight)
            packed = lax.all_gather(after(packed, first.attended), "dp", axis=0, tiled=True)
            w.bc = packed[:, :state_cols]
            w.dt = packed[:, state_cols : state_cols + step_cols]
            w.g_mamba = packed[:, state_cols + step_cols].astype(F32)
            shard = after(mixer_input_weight.transpose(1, 0, 2), first.attended)
            w.w_in = lax.all_gather(shard, "dp", axis=1, tiled=True)
            shard = after(mixer_output_weight, first.attended)
            w.mout = lax.all_gather(shard, "dp", axis=1, tiled=True)
    with jax.named_scope("outputs"):
        results = finish_output(links, micro)

    def both(get, axis=0):
        return jnp.concatenate([get(m) for m in micro], axis=axis)

    ssm_in = both(lambda m: m.ssm_in)
    grad_in = dotl("td,ktc->kdc", ssm_in, both(lambda m: m.gate_x_low, 1))
    grad_in = lax.psum_scatter(grad_in, "dp", scatter_dimension=1, tiled=True)
    grad_mout = dotl("tn,ti->ni", both(lambda m: m.grad_low), both(lambda m: m.gated_norm))
    grad_mout = lax.psum_scatter(grad_mout, "dp", scatter_dimension=0, tiled=True)
    grad_bc = dotl("td,tn->dn", both(lambda m: m.ssm_in_z), both(lambda m: m.state_low))
    grad_dt = dotl("td,tn->dn", ssm_in, both(lambda m: m.step_low))
    grad_small = jnp.concatenate([grad_bc, grad_dt], axis=1)
    grad_small = lax.psum_scatter(grad_small, "dp", scatter_dimension=0, tiled=True)
    grad_up = dotl("ra,rn->an", both(lambda m: m.adapter), both(lambda m: m.gate_up_own))
    grad_up = lax.psum_scatter(grad_up, "dp", scatter_dimension=0, tiled=True)

    sums_dp = jax.tree.map(lambda *v: total(v), *[m.sums_dp for m in micro])
    sums_all = jax.tree.map(lambda *v: total(v), *[m.sums_all for m in micro])
    flat_all = links.z_sum(jnp.concatenate([v.reshape(-1) for v in sums_all]))
    flat = links.dp_sum(jnp.concatenate([v.reshape(-1) for v in sums_dp] + [flat_all]))
    small_sums = []
    for v in sums_dp + sums_all:
        small_sums.append(flat[: v.size].reshape(v.shape))
        flat = flat[v.size :]
    own_gain = mixer_gain.shape[0]
    grad_g_mamba = lax.dynamic_slice_in_dim(small_sums[6], links.d * own_gain, own_gain)

    g_rows = total([jnp.stack([m.grad_g_attn, m.grad_g_mlp], 0) for m in micro])
    half = g_rows.shape[1] // 2
    g_rows = g_rows[:, :half] + links.core_swap(g_rows[:, half:])
    g_rows = links.z_sum(g_rows)

    def grad(spec, get_a, get_b, axis):
        return core_rs(links, total([dotf(spec, get_a(m), get_b(m)) for m in micro]), axis)

    block = both(lambda m: m.block)
    cols = both(lambda m: m.shared_cols)
    spec = "crd,crxn->dxn"
    grad_proj = proj_collect(
        links, dotf(spec, block, cols[:, :, :, 0]), dotl(spec, block, cols[:, :, :, 1])
    )
    grad_down = grad("crn,crd->nd", lambda m: m.hidden, lambda m: m.mlp_low, 1)
    grad_cols = grad("crd,crn->dn", lambda m: m.mlp_in, lambda m: m.gate_up_low, 0)
    grad_out = grad("crn,crd->nd", lambda m: m.attended, lambda m: m.attn_low, 1)
    grad_qkv = grad("crd,crn->dn", lambda m: m.attn_in, lambda m: m.d_qkv, 0)
    grad_qkv = jnp.stack(jnp.split(grad_qkv, 3, axis=1), 1)
    grad_gate_up = jnp.stack([grad_cols[:, :units], grad_cols[:, units : 2 * units]], 1)
    partial_t = [grad_cols[:, 2 * units :].astype(BF16), grad_small[:, :state_cols]]
    sizes = [v.size for v in partial_t]
    whole_t = links.z_sum(jnp.concatenate([v.reshape(-1, HEAD) for v in partial_t], 0))
    split = sizes[0] // HEAD
    grad_adapter_down = whole_t[:split].reshape(partial_t[0].shape).astype(F32)
    grad_bc = whole_t[split:].reshape(partial_t[1].shape).astype(F32)

    return (
        results,
        jnp.stack([m.d_hid for m in micro]),
        jnp.stack([m.d_emb for m in micro]),
        grad_qkv,
        grad_out,
        g_rows[0],
        g_rows[1],
        grad_gate_up,
        grad_adapter_down,
        grad_up.reshape(adapter_up.shape).astype(F32),
        grad_down,
        grad_proj,
        grad_g_mamba,
        grad_in.transpose(1, 0, 2).astype(F32),
        grad_bc,
        grad_small[:, state_cols:].astype(F32),
        grad_mout.T.astype(F32),
        small_sums[0],
        small_sums[5],
        small_sums[2],
        small_sums[3],
        small_sums[4],
        small_sums[1],
    )


def solution(mesh):
    rows = P(None, "dp", None)
    by_dp = P("dp", None, "tensor")
    by_t = P("tensor", "dp")
    weights = (by_dp, by_t, P("dp"), P("dp"), by_dp, P("dp", None), by_dp, by_t, by_t, P("dp"))
    weights += (by_dp, P("dp", None), P("dp", "tensor"), by_t)
    smalls = (P(None, "tensor"), P(), P("tensor"), P("tensor"), P("tensor"), P("tensor"))
    return jax.shard_map(
        partial(local, n_dp=mesh.shape["dp"], n_t=mesh.shape["tensor"]),
        mesh=mesh,
        in_specs=(rows, rows, rows) + weights + smalls + (rows,),
        out_specs=(rows, rows, rows) + weights + smalls,
        check_vma=False,
    )
```

```python
from functools import partial
from types import SimpleNamespace

import jax
import jax.numpy as jnp
from jax import lax
from jax.experimental import pallas as pl
from jax.experimental.pallas import tpu as pltpu
from jax.sharding import PartitionSpec as P

HEAD = 128
EPSILON = 1e-05
ROPE_BASE = 10000.0
MASKED = -1e30
TOP_PRECISION = lax.Precision.HIGHEST
F32 = jnp.float32
BF16 = jnp.bfloat16


def layout(len_row, places):
    bounds = jnp.cumsum(len_row)[:-1]
    passed = places[:, None] >= bounds[None, :]
    segment = jnp.sum(passed.astype(jnp.int32), axis=1)
    starts = jnp.max(jnp.where(passed, bounds[None, :], 0), axis=1)
    position = places - starts
    valid = segment < bounds.shape[0]
    allowed = (segment[:, None] == segment[None, :]) & (places[None, :] <= places[:, None])
    return (segment, position, valid, allowed)


def rope_tables(position):
    half = HEAD // 2
    frequency = ROPE_BASE ** (-2.0 * jnp.arange(half, dtype=F32) / HEAD)
    angles = position.astype(F32)[:, None] * frequency[None, :]
    cosine, sine = jnp.cos(angles), jnp.sin(angles)
    return jnp.concatenate([cosine, cosine], axis=1), jnp.concatenate([-sine, sine], axis=1)


def rows_down(x, count):
    return x if count == 0 else pltpu.roll(x, count, 0)


def rows_up(x, count):
    return x if count == 0 else pltpu.roll(x, x.shape[0] - count, 0)


def conv_taps(x, taps_ref, same_ref):
    summed = x * taps_ref[0:1, :]
    for j in range(1, taps_ref.shape[0]):
        summed = summed + rows_down(x, j) * same_ref[:, j : j + 1] * taps_ref[j : j + 1, :]
    return summed


def conv_taps_back(x, d_out, taps_ref, same_ref, d_taps_ref, cols):
    d_x = d_out * taps_ref[0:1, cols]
    d_taps_ref[0:1, cols] = jnp.sum(d_out * x, axis=0, keepdims=True)
    for j in range(1, taps_ref.shape[0]):
        kept = d_out * same_ref[:, j : j + 1]
        d_taps_ref[j : j + 1, cols] = jnp.sum(kept * rows_down(x, j), axis=0, keepdims=True)
        d_x = d_x + rows_up(kept * taps_ref[j : j + 1, cols], j)
    return d_x


def exact(a, b, dims):
    return lax.dot_general(
        a, b, (dims, ((), ())), precision=TOP_PRECISION, preferred_element_type=F32
    )


def fast(a, b, dims):
    return lax.dot_general(
        a.astype(BF16), b.astype(BF16), (dims, ((), ())), preferred_element_type=F32
    )


PLAIN = ((1,), (0,))
BY_COLS = ((1,), (1,))
BY_ROWS = ((0,), (0,))


def triangle(rows):
    t = lax.broadcasted_iota(jnp.int32, (rows, rows), 0)
    s = lax.broadcasted_iota(jnp.int32, (rows, rows), 1)
    return t, s


def step_terms(step_ref, bias_ref, decay_ref, rows):
    t, s = triangle(rows)
    raw = step_ref[...] + bias_ref[...]
    step = jnp.maximum(raw, 0.0) + jnp.log1p(jnp.exp(-jnp.abs(raw)))
    log_decay = -step * jnp.exp(decay_ref[...])
    running = exact((s <= t).astype(F32), log_decay, PLAIN)
    running_t = exact(log_decay, (t <= s).astype(F32), BY_ROWS)
    step_t = exact(step, (t == s).astype(F32), BY_ROWS)
    return raw, step, log_decay, running, running_t, step_t


def decayed(running, running_t, h, allowed):
    gap = running[:, h : h + 1] - running_t[h : h + 1, :]
    return jnp.exp(jnp.where(allowed, gap, MASKED))


def mix_kernel(
    gate_ref, state_ref, step_ref, taps_x_ref, taps_bc_ref, bias_ref, decay_ref, skip_ref,
    same_ref, allowed_ref, d_scaled_ref, gated_ref, sums_ref,
):
    rows = state_ref.shape[0]
    size = state_ref.shape[1] // 2
    heads = step_ref.shape[1]
    lanes = 128
    per = lanes * heads // gate_ref.shape[2]
    allowed = allowed_ref[...] > 0.0
    _, _, _, running, running_t, step_t = step_terms(step_ref, bias_ref, decay_ref, rows)
    conv_bc = conv_taps(state_ref[...], taps_bc_ref, same_ref)
    state = conv_bc * jax.nn.sigmoid(conv_bc)
    affinity = exact(state[:, size:], state[:, :size], BY_COLS)
    lane = lax.broadcasted_iota(jnp.int32, (rows, lanes), 1) * per // lanes
    squares = jnp.zeros((rows, lanes), F32)
    weighted = jnp.zeros((rows, lanes), F32)
    for group in range(gate_ref.shape[2] // lanes):
        cols = slice(group * lanes, (group + 1) * lanes)
        x = gate_ref[1, :, cols]
        conv = x * taps_x_ref[0:1, cols]
        for j in range(1, taps_x_ref.shape[0]):
            conv = conv + rows_down(x, j) * same_ref[:, j : j + 1] * taps_x_ref[j : j + 1, cols]
        act = conv * jax.nn.sigmoid(conv)
        mixed = act * skip_ref[0:1, cols]
        for i in range(per):
            h = group * per + i
            mixing = decayed(running, running_t, h, allowed) * affinity * step_t[h : h + 1, :]
            mixed = mixed + jnp.where(lane == i, fast(mixing, act, PLAIN), 0.0)
        z = gate_ref[0, :, cols]
        gated = mixed * (z * jax.nn.sigmoid(z))
        gated_ref[:, cols] = gated
        squares = squares + gated * gated
        weighted = weighted + gated * d_scaled_ref[:, cols]
    sums_ref[:, 0:1] = jnp.sum(squares, axis=1, keepdims=True)
    sums_ref[:, 1:2] = jnp.sum(weighted, axis=1, keepdims=True)


def mix_back_kernel(
    gate_ref, state_ref, step_ref, taps_x_ref, taps_bc_ref, bias_ref, decay_ref, skip_ref,
    same_ref, allowed_ref, d_scaled_ref, gated_ref, scales_ref,
    d_gate_ref, d_state_ref, d_step_ref, d_taps_x_ref, d_taps_bc_ref, d_bias_ref, d_decay_ref,
    d_skip_ref,
):
    rows = state_ref.shape[0]
    size = state_ref.shape[1] // 2
    heads = step_ref.shape[1]
    lanes = 128
    per = lanes * heads // gate_ref.shape[2]
    allowed = allowed_ref[...] > 0.0
    raw, step, log_decay, running, running_t, step_t = step_terms(
        step_ref, bias_ref, decay_ref, rows
    )
    conv_bc = conv_taps(state_ref[...], taps_bc_ref, same_ref)
    sig_bc = jax.nn.sigmoid(conv_bc)
    state = conv_bc * sig_bc
    affinity = exact(state[:, size:], state[:, :size], BY_COLS)
    lane = lax.broadcasted_iota(jnp.int32, (rows, lanes), 1) * per // lanes
    head_lane = lax.broadcasted_iota(jnp.int32, (rows, heads), 1)
    head_row = lax.broadcasted_iota(jnp.int32, (heads, rows), 0)
    d_affinity = jnp.zeros((rows, rows), F32)
    d_run = jnp.zeros((rows, heads), F32)
    d_step_t = jnp.zeros((heads, rows), F32)
    for group in range(gate_ref.shape[2] // lanes):
        cols = slice(group * lanes, (group + 1) * lanes)
        x = gate_ref[1, :, cols]
        conv = x * taps_x_ref[0:1, cols]
        for j in range(1, taps_x_ref.shape[0]):
            conv = conv + rows_down(x, j) * same_ref[:, j : j + 1] * taps_x_ref[j : j + 1, cols]
        sig = jax.nn.sigmoid(conv)
        act = conv * sig
        z = gate_ref[0, :, cols]
        sig_z = jax.nn.sigmoid(z)
        d_gated = d_scaled_ref[:, cols] * scales_ref[:, 0:1] - gated_ref[:, cols] * scales_ref[:, 1:2]
        d_mixed = d_gated * (z * sig_z)
        mixed = act * skip_ref[0:1, cols]
        d_act = d_mixed * skip_ref[0:1, cols]
        d_skip_ref[0:1, cols] = jnp.sum(d_mixed * act, axis=0, keepdims=True)
        for i in range(per):
            h = group * per + i
            decay = decayed(running, running_t, h, allowed)
            weight = affinity * step_t[h : h + 1, :]
            mixing = decay * weight
            mixed = mixed + jnp.where(lane == i, fast(mixing, act, PLAIN), 0.0)
            d_act = d_act + jnp.where(lane == i, fast(mixing, d_mixed, BY_ROWS), 0.0)
            d_mixing = fast(jnp.where(lane == i, d_mixed, 0.0), act, BY_COLS) * decay
            d_affinity = d_affinity + d_mixing * step_t[h : h + 1, :]
            by_aff = d_mixing * affinity
            d_step_t = d_step_t + jnp.where(
                head_row == h, jnp.sum(by_aff, axis=0, keepdims=True), 0.0
            )
            by_gap = jnp.sum(by_aff * step_t[h : h + 1, :], axis=1, keepdims=True)
            d_run = d_run + jnp.where(head_lane == h, by_gap, 0.0)
        d_gate_ref[0, :, cols] = (d_gated * mixed * (sig_z * (1.0 + z * (1.0 - sig_z)))).astype(BF16)
        d_conv = d_act * (sig * (1.0 + conv * (1.0 - sig)))
        d_x = conv_taps_back(x, d_conv, taps_x_ref, same_ref, d_taps_x_ref, cols)
        d_gate_ref[1, :, cols] = d_x.astype(BF16)
    t, s = triangle(rows)
    eye = (t == s).astype(F32)
    d_run = d_run - exact(eye, d_step_t * step_t, BY_COLS)
    d_log = exact((s >= t).astype(F32), d_run, PLAIN)
    d_step = exact(eye, d_step_t, BY_COLS) - jnp.exp(decay_ref[...]) * d_log
    d_raw = d_step * jax.nn.sigmoid(raw)
    d_step_ref[...] = d_raw
    d_bias_ref[...] = jnp.sum(d_raw, axis=0, keepdims=True)
    d_decay_ref[...] = jnp.sum(d_log * log_decay, axis=0, keepdims=True)
    d_b = exact(d_affinity, state[:, size:], BY_ROWS)
    d_c = exact(d_affinity, state[:, :size], PLAIN)
    d_silu = sig_bc * (1.0 + conv_bc * (1.0 - sig_bc))
    for part, d_part in enumerate((d_b, d_c)):
        cols = slice(part * size, (part + 1) * size)
        d_conv = d_part * d_silu[:, cols]
        d_x = conv_taps_back(
            state_ref[:, cols], d_conv, taps_bc_ref, same_ref, d_taps_bc_ref, cols
        )
        d_state_ref[:, cols] = d_x.astype(BF16)


def turned(x, cos_ref, sin_ref, sign):
    return x * cos_ref[...] + pltpu.roll(x, HEAD // 2, 1) * (sign * sin_ref[...])


def probabilities(query, key, allowed):
    scores = fast(query, key, BY_COLS) * HEAD ** (-0.5)
    scores = jnp.where(allowed, scores, MASKED)
    raised = jnp.exp(scores - jnp.max(scores, axis=1, keepdims=True))
    return raised / jnp.sum(raised, axis=1, keepdims=True)


def attend_kernel(qkv_ref, cos_ref, sin_ref, allowed_ref, low_ref, attended_ref):
    allowed = allowed_ref[...] > 0.0
    width = attended_ref.shape[1]
    for h in range(width // HEAD):
        q, k, v = (slice(i * width + h * HEAD, i * width + (h + 1) * HEAD) for i in range(3))
        query = turned(qkv_ref[:, q], cos_ref, sin_ref, 1.0).astype(BF16)
        key = turned(qkv_ref[:, k], cos_ref, sin_ref, 1.0).astype(BF16)
        value = qkv_ref[:, v].astype(BF16)
        low_ref[:, q] = query
        low_ref[:, k] = key
        low_ref[:, v] = value
        probs = probabilities(query, key, allowed)
        attended_ref[:, q] = fast(probs, value, PLAIN).astype(BF16)


def attend_back_kernel(low_ref, d_ref, cos_ref, sin_ref, allowed_ref, d_qkv_ref):
    allowed = allowed_ref[...] > 0.0
    width = d_ref.shape[1]
    for h in range(width // HEAD):
        q, k, v = (slice(i * width + h * HEAD, i * width + (h + 1) * HEAD) for i in range(3))
        query, key, value = low_ref[:, q], low_ref[:, k], low_ref[:, v]
        d_out = d_ref[:, q].astype(BF16)
        probs = probabilities(query, key, allowed)
        d_qkv_ref[:, v] = fast(probs, d_out, BY_ROWS).astype(BF16)
        d_probs = fast(d_out, value, BY_COLS)
        inner = jnp.sum(probs * d_probs, axis=1, keepdims=True)
        d_scores = (probs * (d_probs - inner) * HEAD ** (-0.5)).astype(BF16)
        d_query = fast(d_scores, key, PLAIN)
        d_key = fast(d_scores, query, BY_ROWS)
        d_qkv_ref[:, q] = turned(d_query, cos_ref, sin_ref, -1.0).astype(BF16)
        d_qkv_ref[:, k] = turned(d_key, cos_ref, sin_ref, -1.0).astype(BF16)


def in_vmem(kernel, outs, args, flops):
    size = sum(x.size * x.dtype.itemsize for x in tuple(args) + tuple(outs))
    return pl.pallas_call(
        kernel,
        out_shape=outs,
        in_specs=[pl.BlockSpec(memory_space=pltpu.VMEM)] * len(args),
        out_specs=[pl.BlockSpec(memory_space=pltpu.VMEM)] * len(outs),
        compiler_params=pltpu.CompilerParams(vmem_limit_bytes=40 * 2**20),
        cost_estimate=pl.CostEstimate(flops=flops, bytes_accessed=size, transcendentals=0),
    )(*args)


def gated_gelu(gate_up):
    half = gate_up.shape[1] // 2
    return jax.nn.gelu(gate_up[:, :half], approximate=True) * gate_up[:, half:]


def total(values):
    summed = values[0]
    for value in values[1:]:
        summed = summed + value
    return summed


def after(x, done):
    mark = done[(-1,) * done.ndim].astype(F32)
    return x + jnp.minimum(jnp.abs(mark), 0.0).astype(x.dtype)


class Links:
    def __init__(self, n_dp, n_t):
        self.n_dp = n_dp
        self.n_t = n_t
        self.chips = n_dp // 2
        self.chip_bits = self.chips.bit_length() - 1
        self.z_bits = n_t.bit_length() - 1
        d = lax.axis_index("dp")
        self.d = d
        self.core = d % 2
        self.chip = d // 2
        self.t = lax.axis_index("tensor")

    def core_swap(self, x):
        return lax.ppermute(x, "dp", [(i, i ^ 1) for i in range(self.n_dp)])

    def chip_swap(self, x, rel):
        return lax.ppermute(x, "dp", [(i, i ^ (rel << 1)) for i in range(self.n_dp)])

    def z_swap(self, x, rel):
        return lax.ppermute(x, "tensor", [(i, i ^ rel) for i in range(self.n_t)])

    def row_parts(self, rows):
        count = max(1, min(self.chip_bits, rows // 16))
        units = rows // 16
        edges = [0] + [16 * ((units * (i + 1)) // count) for i in range(count)]
        edges[-1] = rows
        return [(edges[i], edges[i + 1]) for i in range(count)]

    def chip_rs(self, terms, axis, direct=False):
        if direct:
            blocks = [
                lax.index_in_dim(terms, rel, axis, keepdims=False) for rel in range(self.chips)
            ]
            return total([block.astype(F32) for block in self.chip_a2a(blocks)])
        outs = []
        bits = self.chip_bits
        for number, (low, high) in enumerate(self.row_parts(terms.shape[axis + 1])):
            cur = lax.slice_in_dim(terms, low, high, axis=axis + 1)
            cur = cur.reshape(cur.shape[:axis] + (2,) * bits + cur.shape[axis + 1 :])
            left = list(range(bits))[::-1]
            for step in range(bits):
                bit = (number + step) % bits
                at = axis + left.index(bit)
                left.remove(bit)
                keep = lax.index_in_dim(cur, 0, at, keepdims=False)
                send = lax.index_in_dim(cur, 1, at, keepdims=False)
                got = self.chip_swap(send.astype(BF16), 1 << bit)
                cur = keep.astype(F32) + got.astype(F32)
            outs.append(cur)
        return outs[0] if len(outs) == 1 else jnp.concatenate(outs, axis=axis)

    def chip_ag(self, x, axis, direct=False):
        if direct:
            return jnp.stack(self.chip_a2a([x] * self.chips), axis=axis)
        bits = self.chip_bits
        outs = []
        for number, (low, high) in enumerate(self.row_parts(x.shape[axis])):
            blocks = {0: lax.slice_in_dim(x, low, high, axis=axis)}
            for step in range(bits):
                bit = (number + step) % bits
                for rel in list(blocks):
                    blocks[rel | (1 << bit)] = self.chip_swap(blocks[rel], 1 << bit)
            outs.append([blocks[rel] for rel in range(self.chips)])
        merged = []
        for rel in range(self.chips):
            pieces = [part[rel] for part in outs]
            merged.append(pieces[0] if len(pieces) == 1 else jnp.concatenate(pieces, axis=axis))
        return jnp.stack(merged, axis=axis)

    def chip_a2a(self, blocks):
        return [blocks[0]] + [self.chip_swap(blocks[rel], rel) for rel in range(1, self.chips)]

    def chip_sum(self, x):
        total = x
        for rel in range(1, self.chips):
            moved = jnp.stack([x[i ^ rel] for i in range(self.chips)], 0)
            total = total + self.chip_swap(moved, rel)
        return total

    def z_sum(self, x):
        return total([x] + [self.z_swap(x, rel) for rel in range(1, self.n_t)])

    def dp_sum(self, x):
        x = x + self.core_swap(x)
        return total(self.chip_a2a([x] * self.chips))

    def z_rs(self, terms, axis):
        bits = self.z_bits
        cur = terms.reshape(terms.shape[:axis] + (2,) * bits + terms.shape[axis + 1 :])
        left = list(range(bits))[::-1]
        for bit in range(bits):
            at = axis + left.index(bit)
            left.remove(bit)
            keep = lax.index_in_dim(cur, 0, at, keepdims=False)
            send = lax.index_in_dim(cur, 1, at, keepdims=False)
            got = self.z_swap(send.astype(BF16), 1 << bit)
            cur = keep.astype(F32) + got.astype(F32)
        return cur

    def z_ag(self, x, axis):
        blocks = {0: x}
        for bit in range(self.z_bits)[::-1]:
            for rel in list(blocks):
                blocks[rel | (1 << bit)] = self.z_swap(blocks[rel], 1 << bit)
        return jnp.stack([blocks[rel] for rel in range(self.n_t)], axis=axis)

    def by_index(self, x, axis, own):
        count = x.shape[axis]
        return jnp.concatenate(
            [lax.dynamic_slice_in_dim(x, own ^ i, 1, axis=axis) for i in range(count)], axis=axis
        )

    def rows_by_t(self, x):
        rows = x.shape[0]
        split = x.reshape((self.n_t, rows // self.n_t) + x.shape[1:])
        return self.by_index(split, 0, self.t).reshape(x.shape)


def core_pair(links, x, axis):
    return jnp.concatenate([x, links.core_swap(x)], axis=axis)


def core_rs(links, x, axis):
    half = x.shape[axis] // 2
    own = lax.slice_in_dim(x, 0, half, axis=axis)
    other = lax.slice_in_dim(x, half, 2 * half, axis=axis)
    return own + links.core_swap(other.astype(BF16)).astype(F32)


def dotf(spec, a, b):
    return jnp.einsum(spec, a, b, preferred_element_type=F32)


def dotl(spec, a, b):
    return jnp.einsum(spec, a, b, preferred_element_type=F32).astype(BF16)


def flip(index, bit):
    return index + (1 - 2 * ((index // bit) % 2)) * bit


def chip_partner(rel):
    d = lax.axis_index("dp")
    for bit in (1, 2):
        if rel & bit:
            d = flip(d, 2 * bit)
    return {"dp": d}


def z_partner(rel):
    return {"tensor": flip(lax.axis_index("tensor"), rel)}


class Wire:
    def __init__(self, send, recv):
        self.send, self.recv, self.used = send, recv, 0

    def start(self, src, dst, partner):
        i = self.used
        self.used += 1
        copy = pltpu.make_async_remote_copy(
            src_ref=src,
            dst_ref=dst,
            send_sem=self.send.at[i],
            recv_sem=self.recv.at[i],
            device_id=partner,
            device_id_type=pl.DeviceIdType.MESH,
        )
        copy.start()
        return copy


def tile_of(width):
    return next(size for size in (384, 256, 128) if width % size == 0)


def over_tiles(width, body):
    tile = tile_of(width)

    def step(i, carry):
        body(pl.ds(pl.multiple_of(i * tile, 128), tile))
        return carry

    lax.fori_loop(0, width // tile, step, 0)


class ByChips:
    copies = 12
    partners = [("dp", 1), ("dp", 2)]

    def __init__(self, x, w, by_cols, out_width, local, args, outs, scratch=()):
        self.by_cols, self.local, self.count = by_cols, local, len(args)
        self.rows = x.shape[1]
        self.width = w.shape[0] if by_cols else w.shape[1]
        self.args = (x, w) + tuple(args)
        self.outs = (jax.ShapeDtypeStruct((4, self.rows, out_width), BF16),) + tuple(outs)
        half = self.rows // 2
        self.scratch = [
            pltpu.VMEM((4, self.rows, self.width), BF16),
            pltpu.VMEM((2, 2, half, self.width), BF16),
            pltpu.VMEM((2, half, self.width), BF16),
            pltpu.VMEM((self.rows, self.width), F32),
        ] + list(scratch)
        self.flops = 8 * self.rows * x.shape[2] * self.width

    def run(self, wire, args, outs, scratch):
        x, w = args[:2]
        part, first, second, summed = scratch[:4]
        gathered = outs[0]
        rows, depth, half = self.rows, x.shape[2], self.rows // 2
        dims = BY_COLS if self.by_cols else PLAIN

        def dot(low, high):
            def body(cols):
                tile = w[cols, :] if self.by_cols else w[:, cols]
                left = x[low:high].reshape((high - low) * rows, depth)
                part[low:high, :, cols] = fast(left, tile, dims).astype(BF16).reshape(
                    high - low, rows, tile_of(self.width)
                )

            over_tiles(self.width, body)

        def piece(p):
            return slice(p * half, (p + 1) * half), 1 << p, 1 << (1 - p)

        dot(1, 4)
        sent = []
        for p in range(2):
            at, bit, _ = piece(p)
            for i, rel in enumerate((bit, 3)):
                sent.append(wire.start(part.at[rel, at], first.at[p, i], chip_partner(bit)))
        dot(0, 1)
        yield
        later = []
        for p in range(2):
            at, _, other = piece(p)
            sent[2 * p + 1].wait_recv()

            def add(cols, p=p, at=at, other=other):
                both = part[other, at, cols].astype(F32) + first[p, 1, :, cols].astype(F32)
                part[other, at, cols] = both.astype(BF16)

            over_tiles(self.width, add)
            later.append(wire.start(part.at[other, at], second.at[p], chip_partner(other)))
        yield
        for p in range(2):
            at, _, _ = piece(p)
            sent[2 * p].wait_recv()
            later[p].wait_recv()

            def finish(cols, p=p, at=at):
                both = part[0, at, cols].astype(F32) + first[p, 0, :, cols].astype(F32)
                summed[at, cols] = both + second[p, :, cols].astype(F32)

            over_tiles(self.width, finish)
        self.local(summed, gathered.at[0], args[2:], outs[1:], scratch[4:])
        near, far = [], []
        for p in range(2):
            at, bit, other = piece(p)
            near.append(wire.start(gathered.at[0, at], gathered.at[bit, at], chip_partner(bit)))
            far.append(wire.start(gathered.at[0, at], gathered.at[other, at], chip_partner(other)))
        yield
        last = []
        for p in range(2):
            at, bit, other = piece(p)
            near[p].wait_recv()
            last.append(wire.start(gathered.at[bit, at], gathered.at[3, at], chip_partner(other)))
        yield
        for copy in far + last:
            copy.wait_recv()
        for copy in sent + later + near + far + last:
            copy.wait_send()


class ByTensor:
    copies = 9
    partners = [("tensor", 1), ("tensor", 2), ("dp", 1), ("dp", 2), ("dp", 3)]

    def __init__(self, x, w, by_cols, local, args, outs, gather=True):
        self.by_cols, self.local, self.gather = by_cols, local, gather
        self.rows = x.shape[1]
        self.width = w.shape[0] if by_cols else w.shape[1]
        self.args = (x, w) + tuple(args)
        shape = (4, 4, self.rows // 4, self.width)
        self.outs = (jax.ShapeDtypeStruct(shape, BF16),) if gather else ()
        self.outs += tuple(outs)
        self.copies = 9 if gather else 6
        self.scratch = [
            pltpu.VMEM((4, self.rows, self.width), BF16),
            pltpu.VMEM((2, self.rows, self.width), BF16),
            pltpu.VMEM((self.rows, self.width), BF16),
            pltpu.VMEM((self.rows, self.width), F32),
            pltpu.VMEM((4, self.rows, 128), F32),
        ]
        self.flops = 8 * self.rows * x.shape[2] * self.width

    def run(self, wire, args, outs, scratch):
        x, w = args[:2]
        part, first, second, summed, stats = scratch
        rows, depth = self.rows, x.shape[2]
        r = rows // 4
        dims = BY_COLS if self.by_cols else PLAIN

        def body(cols):
            tile = w[cols, :] if self.by_cols else w[:, cols]
            low = fast(x[...].reshape(4 * rows, depth), tile, dims).astype(BF16)
            for c in range(4):
                for z in range(4):
                    part[z, c * r : (c + 1) * r, cols] = low[c * rows + z * r : c * rows + z * r + r]

        over_tiles(self.width, body)
        sent = [wire.start(part.at[z], first.at[i], z_partner(1)) for i, z in enumerate((1, 3))]
        yield
        sent[1].wait_recv()

        def add(cols):
            both = part[2, :, cols].astype(F32) + first[1, :, cols].astype(F32)
            part[2, :, cols] = both.astype(BF16)

        over_tiles(self.width, add)
        later = wire.start(part.at[2], second, z_partner(2))
        yield
        sent[0].wait_recv()
        later.wait_recv()

        def finish(cols):
            both = part[0, :, cols].astype(F32) + first[0, :, cols].astype(F32)
            summed[:, cols] = both + second[:, cols].astype(F32)

        over_tiles(self.width, finish)
        rest = outs[1:] if self.gather else outs
        local = self.local(summed, args[2:], rest)
        stats[0] = jnp.broadcast_to(next(local), (rows, 128))
        sums = [
            wire.start(stats.at[0], stats.at[rel], chip_partner(rel)) for rel in range(1, 4)
        ]
        yield
        total_sums = stats[0]
        for rel in range(1, 4):
            sums[rel - 1].wait_recv()
            moved = [stats[rel, (i ^ rel) * r : (i ^ rel) * r + r, :] for i in range(4)]
            total_sums = total_sums + jnp.concatenate(moved, axis=0)
        low = local.send(total_sums[:, 0:1])
        if self.gather:
            gathered = outs[0]
            for c in range(4):
                gathered[c, 0] = low[c * r : (c + 1) * r]
            far = wire.start(gathered.at[:, 0], gathered.at[:, 2], z_partner(2))
            near = wire.start(gathered.at[:, 0], gathered.at[:, 1], z_partner(1))
            yield
            far.wait_recv()
            last = wire.start(gathered.at[:, 2], gathered.at[:, 3], z_partner(1))
            yield
            near.wait_recv()
            last.wait_recv()
            sent += [far, near, last]
        for copy in sent + [later] + sums:
            copy.wait_send()


def together(groups, collective_id):
    partners = sorted({p for g in groups for p in g.partners})

    def kernel(*refs):
        refs = list(refs)

        def take(count):
            got = refs[:count]
            del refs[:count]
            return got

        args = [take(len(g.args)) for g in groups]
        outs = [take(len(g.outs)) for g in groups]
        scratch = [take(len(g.scratch)) for g in groups]
        wires = [Wire(*take(2)) for g in groups]
        barrier = pltpu.get_barrier_semaphore()
        for axis, rel in partners:
            partner = chip_partner(rel) if axis == "dp" else z_partner(rel)
            pl.semaphore_signal(
                barrier, inc=1, device_id=partner, device_id_type=pl.DeviceIdType.MESH
            )
        pl.semaphore_wait(barrier, len(partners))
        running = [
            g.run(wire, a, o, s) for g, wire, a, o, s in zip(groups, wires, args, outs, scratch)
        ]
        while running:
            left = []
            for run in running:
                if next(run, running) is not running:
                    left.append(run)
            running = left

    args = [x for g in groups for x in g.args]
    outs = [x for g in groups for x in g.outs]
    scratch = [x for g in groups for x in g.scratch]
    for g in groups:
        scratch += [pltpu.SemaphoreType.DMA((g.copies,))] * 2
    size = sum(x.size * x.dtype.itemsize for x in args + outs)
    flat = pl.pallas_call(
        kernel,
        out_shape=outs,
        in_specs=[pl.BlockSpec(memory_space=pltpu.VMEM)] * len(args),
        out_specs=[pl.BlockSpec(memory_space=pltpu.VMEM)] * len(outs),
        scratch_shapes=scratch,
        compiler_params=pltpu.CompilerParams(
            collective_id=collective_id, has_side_effects=True, vmem_limit_bytes=58 * 2**20
        ),
        cost_estimate=pl.CostEstimate(
            flops=sum(g.flops for g in groups), bytes_accessed=size, transcendentals=0
        ),
    )(*args)
    results = []
    for g in groups:
        results.append(flat[: len(g.outs)])
        flat = flat[len(g.outs) :]
    return results


def attend_local(qkv, slot, args, outs, scratch):
    cos, sin, allowed = args
    attend_kernel(qkv, cos, sin, allowed, outs[0], slot)


def attend_back_local(d_attended, slot, args, outs, scratch):
    low, cos, sin, allowed = args
    attend_back_kernel(low, d_attended, cos, sin, allowed, slot)


GELU_SCALE = (2.0 / 3.141592653589793) ** 0.5


def feed_local(summed, slot, args, outs, scratch):
    (up,) = args
    gate_up, adapter = outs
    units = slot.shape[1]
    low = summed[:, 2 * units :].astype(BF16)
    adapter[...] = low

    def widen(cols):
        gate_up[:, cols] = summed[:, cols] + fast(low, up[:, cols], PLAIN)

    over_tiles(2 * units, widen)
    tile = 256

    def act(i, carry):
        at = pl.ds(pl.multiple_of(i * tile, 128), tile)
        also = pl.ds(pl.multiple_of(units + i * tile, 128), tile)
        v = gate_up[:, at]
        bent = jnp.tanh(GELU_SCALE * (v + 0.044715 * (v * v * v)))
        slot[:, at] = (0.5 * v * (1.0 + bent) * gate_up[:, also]).astype(BF16)
        return carry

    lax.fori_loop(0, units // tile, act, 0)


def feed_back_local(d_hidden, slot, args, outs, scratch):
    gate_up, up = args
    (adapter,) = scratch
    units = d_hidden.shape[1]
    tile = 256
    adapter[...] = jnp.zeros(adapter.shape, F32)

    def act(i, carry):
        at = pl.ds(pl.multiple_of(i * tile, 128), tile)
        also = pl.ds(pl.multiple_of(units + i * tile, 128), tile)
        v, u, d = gate_up[:, at], gate_up[:, also], d_hidden[:, at]
        bent = jnp.tanh(GELU_SCALE * (v + 0.044715 * (v * v * v)))
        slope = 0.5 * (1.0 + bent) + 0.5 * v * (1.0 - bent * bent) * GELU_SCALE * (
            1.0 + 3.0 * 0.044715 * (v * v)
        )
        d_gate = (d * u * slope).astype(BF16)
        d_up = (d * (0.5 * v * (1.0 + bent))).astype(BF16)
        slot[:, at] = d_gate
        slot[:, also] = d_up
        adapter[...] += fast(d_gate, up[:, at], BY_COLS) + fast(d_up, up[:, also], BY_COLS)
        return carry

    lax.fori_loop(0, units // tile, act, 0)
    slot[:, 2 * units :] = adapter[...].astype(BF16)


def norm_local(width, summed, args, outs):
    base, gain = args
    mid, inverse = outs
    value = base[...] + summed[...]
    mid[...] = value
    squares = yield jnp.sum(value * value, axis=1, keepdims=True)
    inv = lax.rsqrt(squares / width + EPSILON)
    inverse[...] = inv
    yield (value * inv * gain[...]).astype(BF16)


def norm_back_local(width, summed, args, outs):
    value, inverse, gain, skip = args
    d_value, d_gain = outs
    dy = summed[...]
    scaled = dy * gain[...]
    v, inv = value[...], inverse[...]
    weighted = yield jnp.sum(scaled * v, axis=1, keepdims=True)
    d_gain[...] = jnp.sum(dy * v * inv, axis=0, keepdims=True)
    result = scaled * inv - v * (inv * inv * inv * weighted / width) + skip[...]
    d_value[...] = result
    yield result.astype(BF16)


def proj_spread(links, w):
    rows = links.z_ag(w, 0)
    if links.chips == links.n_t:
        blocks = [
            lax.dynamic_index_in_dim(rows, links.chip ^ links.t ^ rel, 0, keepdims=False)
            for rel in range(links.chips)
        ]
    else:
        rows = links.by_index(rows, 0, links.t).reshape(links.chips, -1, w.shape[1])
        blocks = [
            lax.dynamic_index_in_dim(rows, links.chip ^ rel, 0, keepdims=False)
            for rel in range(links.chips)
        ]
    came = jnp.stack(links.chip_a2a(blocks), 0)
    return jnp.stack([came, links.core_swap(came)], 1)


def proj_collect(links, own, other):
    mine = (own + links.core_swap(other).astype(F32)).astype(BF16)
    blocks = [mine[:, rel] for rel in range(links.chips)]
    rows = jnp.stack(links.chip_a2a(blocks), 0)
    if links.chips == links.n_t:
        rows = links.by_index(rows, 0, links.chip ^ links.t)
    else:
        rows = links.by_index(rows, 0, links.chip).reshape(links.n_t, -1, own.shape[2])
        rows = links.by_index(rows, 0, links.t)
    return links.z_rs(rows, 0)


def core_halves(links, x):
    split = x.reshape(x.shape[:-1] + (2, x.shape[-1] // 2))
    return links.by_index(split, x.ndim - 1, links.core).reshape(x.shape)


def enter(links, w, m):
    rows = m.hid.shape[0]
    joined = links.rows_by_t(jnp.concatenate([m.hid, m.emb], axis=1))
    wide = joined.astype(F32)
    m.inverse = lax.rsqrt(jnp.mean(wide * wide, axis=1) + EPSILON)
    half = joined.shape[1] // links.n_dp
    blocks = []
    for rel in range(links.chips):
        at = 2 * (links.chip ^ rel)
        pieces = [
            lax.dynamic_slice_in_dim(joined, (at + (links.core ^ j)) * half, half, axis=1)
            for j in range(2)
        ]
        blocks.append(jnp.concatenate(pieces, axis=1))
    m.joined = jnp.stack(links.chip_a2a(blocks), 0)
    places = jnp.arange(rows, dtype=jnp.int32)
    m.true = layout(m.lens, places)
    _, position, _, allowed = layout(m.lens, links.rows_by_t(places))
    m.allowed_rel = allowed.astype(F32)
    m.cos, m.sin = rope_tables(position)


def attend(links, w, m):
    wide = m.joined.astype(F32) * m.inv_attn[:, :, None]
    m.attn_in = lax.optimization_barrier((wide * w.g_attn).astype(BF16))
    qkv = links.chip_rs(dotl("crd,dn->crn", m.attn_in, w.qkv), 0)
    rows, width = qkv.shape[0], qkv.shape[1] // 3
    outs = (
        jax.ShapeDtypeStruct((rows, 3 * width), BF16),
        jax.ShapeDtypeStruct((rows, width), BF16),
    )
    args = (qkv, m.cos, m.sin, m.allowed_rel)
    m.qkv_low, attended = in_vmem(attend_kernel, outs, args, 4 * rows * rows * width)
    m.attended = links.chip_ag(attended, 0, direct=True)


def z_split(links, x, axis):
    rows = x.shape[axis]
    return x.reshape(x.shape[:axis] + (links.n_t, rows // links.n_t) + x.shape[axis + 1 :])


def z_join(x, axis):
    return x.reshape(x.shape[:axis] + (-1,) + x.shape[axis + 2 :])


def attend_out(links, w, m):
    part = dotl("crn,nd->crd", m.attended, w.out)
    summed = links.z_rs(z_split(links, part, 1), 1)
    rows = summed.shape[1]
    m.joined_z = m.joined[:, :rows].astype(F32)
    m.inv_attn_z = m.inv_attn[:, :rows]
    mid = m.joined_z + summed
    m.mid = mid
    squares = links.chip_sum(jnp.sum(mid * mid, axis=2))
    width = mid.shape[2] * links.chips
    m.inv_mlp = lax.rsqrt(squares / width + EPSILON)
    low = (mid * m.inv_mlp[:, :, None] * w.g_mlp).astype(BF16)
    m.mlp_in = z_join(links.z_ag(low, 1), 1)


def feed(links, w, m):
    summed = links.chip_rs(dotl("crd,dn->crn", m.mlp_in, w.gate_up), 0)
    units = 2 * w.down.shape[0]
    m.adapter = summed[:, units:].astype(BF16)
    gate_up = summed[:, :units] + dotf("ra,an->rn", m.adapter, w.adapter_up)
    activated, m.gate_back = jax.vjp(gated_gelu, gate_up)
    m.hidden = links.chip_ag(activated.astype(BF16), 0, direct=True)


def feed_out(links, w, m):
    part = dotl("crn,nd->crd", m.hidden, w.down)
    summed = links.z_rs(z_split(links, part, 1), 1)
    m.block = (m.mid + summed).astype(BF16)
    m.block = core_halves(links, m.block)
    part = dotl("crd,xydn->xycrn", m.block, w.proj)
    part = links.by_index(links.by_index(part, 1, links.core), 0, links.chip)
    part = z_join(part, 0).transpose(1, 2, 0, 3)
    part = part.reshape(part.shape[:2] + (-1,))
    shared = links.chip_rs(part, 0, direct=True).astype(BF16)
    whole = links.by_index(links.z_ag(shared, 0), 0, links.t)
    shared_full = whole.reshape(-1, whole.shape[2])
    m.mamba_in = m.hid.astype(F32) + shared_full.astype(F32)
    own = z_split(links, m.hid, 0)
    own = lax.dynamic_index_in_dim(own, links.t, 0, keepdims=False)
    m.mamba_in_z = own.astype(F32) + shared.astype(F32)


def mix(links, w, m):
    taps_x, taps_bc, step_bias, decay_log, skip, gate_gain = w.smalls
    segment, _, valid, allowed = m.true
    mamba_in = m.mamba_in
    inverse = lax.rsqrt(jnp.mean(mamba_in * mamba_in, axis=1, keepdims=True) + EPSILON)
    ssm_in = (mamba_in * inverse * w.g_mamba).astype(BF16)
    gate_x = dotf("td,kdc->ktc", ssm_in, w.w_in)
    state_io = dotf("td,dn->tn", ssm_in, w.bc)
    step_raw = dotf("td,dn->tn", ssm_in, w.dt)
    grad_low = m.cot * valid[:, None].astype(BF16)
    d_norm = dotf("tn,in->ti", grad_low, w.mout)
    d_scaled = d_norm * gate_gain
    rows, width = gate_x.shape[1:]
    heads = step_raw.shape[1]
    earlier = [jnp.pad(segment, (j, 0), constant_values=-1)[:rows] for j in range(taps_x.shape[0])]
    same = jnp.stack([(e == segment).astype(F32) for e in earlier], 1)
    skips = jnp.repeat(skip, width // heads)[None, :]
    args = (gate_x, state_io, step_raw, taps_x, taps_bc, step_bias[None, :], decay_log[None, :])
    args += (skips, same, allowed.astype(F32), d_scaled)
    outs = (jax.ShapeDtypeStruct((rows, width), F32), jax.ShapeDtypeStruct((rows, 2), F32))
    gated, sums = in_vmem(mix_kernel, outs, args, 4 * rows * rows * width)
    inner = width * links.n_t
    sums = links.z_sum(sums)
    squares, weighted = sums[:, 0], sums[:, 1]
    row_scale = lax.rsqrt(squares / inner + EPSILON)
    m.gated_norm = (gated * row_scale[:, None] * gate_gain).astype(BF16)
    m.mamba_out = dotl("ti,in->tn", m.gated_norm, w.mout)

    grad_gain = jnp.sum(d_norm * gated * row_scale[:, None], axis=0)
    scales = jnp.stack([row_scale, row_scale**3 * weighted / inner], 1)
    outs = (
        jax.ShapeDtypeStruct(gate_x.shape, BF16),
        jax.ShapeDtypeStruct(state_io.shape, BF16),
        jax.ShapeDtypeStruct(step_raw.shape, F32),
        jax.ShapeDtypeStruct(taps_x.shape, F32),
        jax.ShapeDtypeStruct(taps_bc.shape, F32),
        jax.ShapeDtypeStruct((1, heads), F32),
        jax.ShapeDtypeStruct((1, heads), F32),
        jax.ShapeDtypeStruct((1, width), F32),
    )
    args += (gated, scales)
    grads = in_vmem(mix_back_kernel, outs, args, 16 * rows * rows * width)
    m.gate_x_low, d_state_io, d_step, d_taps_x, d_taps_bc, d_bias, d_decay, d_skip = grads
    d_skip = jnp.sum(d_skip.reshape(heads, width // heads), axis=1)
    m.step_low = d_step.astype(BF16)
    part_in = dotf("ktc,kdc->td", m.gate_x_low, w.w_in) + dotf("tn,dn->td", m.step_low, w.dt)
    terms = jnp.concatenate([part_in.astype(BF16), d_state_io], axis=1)
    m.terms = z_split(links, links.rows_by_t(terms), 0)
    m.ssm_in = ssm_in
    m.ssm_in_z = own_rows(links, ssm_in)
    m.grad_low = grad_low
    m.sums_dp = (d_taps_x, grad_gain, d_bias[0], d_decay[0], d_skip)
    m.d_taps_bc = d_taps_bc


def settle(links, w, m):
    summed = links.z_rs(m.terms, 0)
    model_width = m.mamba_in_z.shape[1]
    m.state_low = summed[:, model_width:].astype(BF16)
    dy = summed[:, :model_width] + dotf("tn,dn->td", m.state_low, w.bc)
    v = m.mamba_in_z
    inv = lax.rsqrt(jnp.mean(v * v, axis=1, keepdims=True) + EPSILON)
    scaled = dy * w.g_mamba
    dv = inv * scaled - v * (inv**3 * jnp.mean(scaled * v, axis=1, keepdims=True))
    grad_g_mamba = jnp.sum(dy * v * inv, axis=0)
    m.sums_all = (m.d_taps_bc, grad_g_mamba)
    m.d_mamba = dv + own_rows(links, m.grad_low).astype(F32)
    m.shared_low = links.chip_ag(m.d_mamba.astype(BF16), 0, direct=True)
    split = m.shared_low.reshape(m.shared_low.shape[:2] + w.proj.shape[:2] + (-1,))
    m.shared_cols = links.by_index(links.by_index(split, 3, links.core), 2, links.chip)
    d_block = core_halves(links, dotf("crxyn,xydn->crd", m.shared_cols, w.proj))
    m.d_block = d_block
    m.mlp_low = z_join(links.z_ag(d_block.astype(BF16), 1), 1)


def own_rows(links, x):
    return lax.dynamic_index_in_dim(z_split(links, x, 0), links.t, 0, keepdims=False)


def finish_output(links, micro):
    terms = jnp.stack([z_split(links, links.rows_by_t(m.mamba_out), 0) for m in micro], 0)
    summed = links.z_rs(terms, 1)
    base = jnp.stack([m.mamba_in_z for m in micro], 0)
    valid = jnp.stack([own_rows(links, m.true[2]) for m in micro], 0)
    low = ((base + summed) * valid[:, :, None].astype(F32)).astype(BF16)
    whole = links.by_index(links.z_ag(low, 1), 1, links.t)
    return z_join(whole, 1)


def feed_back(links, w, m):
    part = dotl("crd,nd->crn", m.mlp_low, w.down)
    d_hidden = links.chip_rs(part, 0)
    (d_gate_up,) = m.gate_back(d_hidden)
    m.gate_up_own = d_gate_up.astype(BF16)
    part = dotl("rn,an->ra", m.gate_up_own, w.adapter_up)
    m.gate_up_low = links.chip_ag(jnp.concatenate([m.gate_up_own, part], 1), 0)


def feed_back_out(links, w, m):
    part = dotl("crn,dn->crd", m.gate_up_low, w.gate_up)
    dy = links.z_rs(z_split(links, part, 1), 1)
    scaled = dy * w.g_mlp
    v, inv = m.mid, m.inv_mlp
    weighted = links.chip_sum(jnp.sum(scaled * v, axis=2))
    width = v.shape[2] * links.chips
    dv = scaled * inv[:, :, None] - v * (inv**3 * weighted / width)[:, :, None]
    m.grad_g_mlp = jnp.sum(dy * v * inv[:, :, None], axis=(0, 1))
    m.d_mid = dv + m.d_block
    m.attn_low = z_join(links.z_ag(m.d_mid.astype(BF16), 1), 1)


def attend_back(links, w, m):
    part = dotl("crd,nd->crn", m.attn_low, w.out)
    d_attended = links.chip_rs(part, 0, direct=True)
    rows, width = d_attended.shape
    outs = (jax.ShapeDtypeStruct((rows, 3 * width), BF16),)
    args = (m.qkv_low, d_attended, m.cos, m.sin, m.allowed_rel)
    (d_qkv,) = in_vmem(attend_back_kernel, outs, args, 10 * rows * rows * width)
    m.d_qkv = links.chip_ag(d_qkv, 0)


def leave(links, w, m):
    part = dotl("crn,dn->crd", m.d_qkv, w.qkv)
    dy = links.z_rs(z_split(links, part, 1), 1)
    scaled = dy * w.g_attn
    v, inv = m.joined_z, m.inv_attn_z
    weighted = links.chip_sum(jnp.sum(scaled * v, axis=2))
    width = v.shape[2] * links.chips
    dv = scaled * inv[:, :, None] - v * (inv**3 * weighted / width)[:, :, None]
    m.grad_g_attn = jnp.sum(dy * v * inv[:, :, None], axis=(0, 1))
    m.d_joined = (dv + m.d_mid).astype(BF16)
    leave_rows(links, m)


def leave_rows(links, m):
    d_joined = m.d_joined.reshape(links.chips, -1, m.d_joined.shape[-1])
    came = jnp.stack(links.chip_a2a([d_joined[rel] for rel in range(links.chips)]), 0)
    rows = came.shape[1]
    came = came.reshape(links.chips, rows, 2, -1)
    came = links.by_index(links.by_index(came, 2, links.core), 0, links.chip)
    came = came.transpose(1, 0, 2, 3).reshape(rows, -1)
    model_width = m.d_mamba.shape[1]
    d_hid = (came[:, :model_width].astype(F32) + m.d_mamba).astype(BF16)
    both = jnp.concatenate([d_hid, came[:, model_width:]], axis=1)
    whole = links.by_index(links.z_ag(both, 0), 0, links.t)
    whole = whole.reshape(-1, both.shape[1])
    m.d_hid, m.d_emb = whole[:, :model_width], whole[:, model_width:]


def sds(shape, dtype=F32):
    return jax.ShapeDtypeStruct(shape, dtype)


def attend_group(links, w, m):
    wide = m.joined.astype(F32) * m.inv_attn[:, :, None]
    m.attn_in = (wide * w.g_attn).astype(BF16)
    rows, width = m.attn_in.shape[1], w.qkv.shape[1]
    args = (m.cos, m.sin, m.allowed_rel)
    outs = (sds((rows, width), BF16),)
    return ByChips(m.attn_in, w.qkv, False, width // 3, attend_local, args, outs)


def attend_out_group(links, w, m):
    r, width = m.joined.shape[1] // links.n_t, m.joined.shape[2]
    m.joined_z = m.joined[:, :r].astype(F32).reshape(-1, width)
    m.inv_attn_z = m.inv_attn[:, :r].reshape(-1, 1)
    outs = (sds(m.joined_z.shape), sds(m.inv_attn_z.shape))
    args = (m.joined_z, w.g_mlp[None, :])
    work = partial(norm_local, width * links.chips)
    return ByTensor(m.attended, w.out, False, work, args, outs)


def feed_group(links, w, m):
    rows, units = m.mlp_in.shape[1], w.down.shape[0]
    outs = (sds((rows, 2 * units)), sds((rows, w.gate_up.shape[1] - 2 * units), BF16))
    args = (w.adapter_up,)
    return ByChips(m.mlp_in, w.gate_up, False, units, feed_local, args, outs)


def feed_back_group(links, w, m):
    args = (m.gate_up, w.adapter_up)
    rank = w.gate_up.shape[1] - m.gate_up.shape[1]
    scratch = (pltpu.VMEM((m.gate_up.shape[0], rank), F32),)
    width = w.gate_up.shape[1]
    return ByChips(m.mlp_low, w.down, True, width, feed_back_local, args, (), scratch)


def feed_back_out_group(links, w, m):
    width = m.mid_z.shape[1]
    args = (m.mid_z, m.inv_mlp, w.g_mlp[None, :], m.d_block.reshape(m.mid_z.shape))
    outs = (sds(m.mid_z.shape), sds((1, width)))
    work = partial(norm_back_local, width * links.chips)
    return ByTensor(m.gate_up_low, w.gate_up, True, work, args, outs)


def attend_back_group(links, w, m):
    args = (m.qkv_low, m.cos, m.sin, m.allowed_rel)
    width = w.qkv.shape[1]
    return ByChips(m.attn_low, w.out, True, width, attend_back_local, args, ())


def leave_group(links, w, m):
    width = m.joined_z.shape[1]
    args = (m.joined_z, m.inv_attn_z, w.g_attn[None, :], m.d_mid)
    outs = (sds(m.joined_z.shape), sds((1, width)))
    work = partial(norm_back_local, width * links.chips)
    return ByTensor(m.d_qkv, w.qkv, True, work, args, outs, gather=False)


def take_attend(m, got):
    m.attended, m.qkv_low = got


def take_attend_out(m, got):
    gathered, m.mid_z, m.inv_mlp = got
    m.mlp_in = z_join(gathered, 1)
    m.mid = m.mid_z.reshape(gathered.shape[0], -1, gathered.shape[3])


def take_feed(m, got):
    m.hidden, m.gate_up, m.adapter = got


def take_feed_back(m, got):
    (m.gate_up_low,) = got
    m.gate_up_own = m.gate_up_low[0, :, : m.gate_up.shape[1]]


def take_feed_back_out(m, got):
    gathered, m.d_mid, d_gain = got
    m.attn_low = z_join(gathered, 1)
    m.grad_g_mlp = d_gain[0]


def take_attend_back(m, got):
    (m.d_qkv,) = got


def take_leave(m, got):
    d_joined, d_gain = got
    m.grad_g_attn = d_gain[0]
    m.d_joined = d_joined.astype(BF16)


def fused(links, w, number, *work):
    groups = [make(links, w, m) for make, _, m in work]
    for (_, taker, m), got in zip(work, together(groups, number)):
        taker(m, got)


ATTEND = (attend_group, take_attend)
ATTEND_OUT = (attend_out_group, take_attend_out)
FEED = (feed_group, take_feed)
FEED_BACK = (feed_back_group, take_feed_back)
FEED_BACK_OUT = (feed_back_out_group, take_feed_back_out)
ATTEND_BACK = (attend_back_group, take_attend_back)
LEAVE = (leave_group, take_leave)


def local(
    hidden,
    embedding,
    lengths,
    query_key_value_weight,
    attention_output_weight,
    attention_gain,
    feedforward_gain,
    gate_up_weight,
    adapter_down,
    adapter_up,
    down_weight,
    shared_projection_weight,
    mixer_gain,
    mixer_input_weight,
    state_map_weight,
    step_weight,
    mixer_output_weight,
    mixer_input_taps,
    state_map_taps,
    step_bias,
    decay_logarithm,
    head_skip_weight,
    gated_norm_gain,
    cotangent,
    n_dp,
    n_t,
):
    links = Links(n_dp, n_t)
    smalls = (
        mixer_input_taps,
        state_map_taps,
        step_bias,
        decay_logarithm,
        head_skip_weight,
        gated_norm_gain,
    )
    micro = [
        SimpleNamespace(
            hid=hidden[b], emb=embedding[b], lens=lengths[b, 0], cot=cotangent[b]
        )
        for b in range(hidden.shape[0])
    ]
    w = SimpleNamespace()
    gains = core_pair(links, jnp.stack([attention_gain, feedforward_gain], 0), 1).astype(F32)
    w.g_attn, w.g_mlp = gains[0], gains[1]
    flat = jnp.concatenate([query_key_value_weight[:, i] for i in range(3)], axis=1)
    w.qkv = lax.optimization_barrier(core_pair(links, flat, 0))
    def stage(work, m):
        with jax.named_scope(f"{work.__name__}_micro{micro.index(m)}"):
            work(links, w, m)

    for m in micro:
        stage(enter, m)
    inverses = jnp.stack([m.inverse for m in micro], 0)
    inverses = jnp.stack(links.chip_a2a([inverses] * links.chips), 1)
    for b, m in enumerate(micro):
        m.inv_attn = inverses[b]
    first = micro[0]
    units = gate_up_weight.shape[2]
    up_own = adapter_up.reshape(adapter_up.shape[0], 2 * units)
    cols = jnp.concatenate([gate_up_weight[:, 0], gate_up_weight[:, 1], adapter_down], axis=1)
    w.out = lax.optimization_barrier(core_pair(links, attention_output_weight, 1))
    w.gate_up = lax.optimization_barrier(core_pair(links, cols, 0))
    w.down = lax.optimization_barrier(core_pair(links, down_weight, 1))
    state_cols, step_cols = state_map_weight.shape[1], step_weight.shape[1]
    packed = jnp.concatenate([state_map_weight, step_weight, mixer_gain[:, None]], axis=1)

    w.smalls = smalls
    def gather_mixer():
        w.adapter_up = lax.all_gather(after(up_own, first.joined), "dp", axis=0, tiled=True)
        w.proj = proj_spread(links, shared_projection_weight)
        whole = lax.all_gather(after(packed, first.attended), "dp", axis=0, tiled=True)
        w.bc = whole[:, :state_cols]
        w.dt = whole[:, state_cols : state_cols + step_cols]
        w.g_mamba = whole[:, state_cols + step_cols].astype(F32)
        shard = after(mixer_input_weight.transpose(1, 0, 2), first.attended)
        w.w_in = lax.all_gather(shard, "dp", axis=1, tiled=True)
        shard = after(mixer_output_weight, first.attended)
        w.mout = lax.all_gather(shard, "dp", axis=1, tiled=True)

    def run(*works):
        for work in works:
            for m in micro:
                stage(work, m)

    if links.chips == 4 and links.n_t == 4 and len(micro) == 2:
        a, b = micro
        fused(links, w, 1, (*ATTEND, a))
        gather_mixer()
        fused(links, w, 2, (*ATTEND, b), (*ATTEND_OUT, a))
        fused(links, w, 3, (*FEED, a), (*ATTEND_OUT, b))
        fused(links, w, 4, (*FEED, b))
        run(feed_out, mix, settle)
        fused(links, w, 5, (*FEED_BACK, a))
        fused(links, w, 6, (*FEED_BACK, b), (*FEED_BACK_OUT, a))
        fused(links, w, 7, (*ATTEND_BACK, a), (*FEED_BACK_OUT, b))
        fused(links, w, 8, (*ATTEND_BACK, b), (*LEAVE, a))
        fused(links, w, 9, (*LEAVE, b))
        for m in micro:
            leave_rows(links, m)
    else:
        run(attend)
        gather_mixer()
        run(attend_out, feed, feed_out, mix, settle)
        run(feed_back, feed_back_out, attend_back, leave)
    with jax.named_scope("outputs"):
        results = finish_output(links, micro)

    def both(get, axis=0):
        return jnp.concatenate([get(m) for m in micro], axis=axis)

    ssm_in = both(lambda m: m.ssm_in)
    grad_in = dotl("td,ktc->kdc", ssm_in, both(lambda m: m.gate_x_low, 1))
    grad_in = lax.psum_scatter(grad_in, "dp", scatter_dimension=1, tiled=True)
    grad_mout = dotl("tn,ti->ni", both(lambda m: m.grad_low), both(lambda m: m.gated_norm))
    grad_mout = lax.psum_scatter(grad_mout, "dp", scatter_dimension=0, tiled=True)
    grad_bc = dotl("td,tn->dn", both(lambda m: m.ssm_in_z), both(lambda m: m.state_low))
    grad_dt = dotl("td,tn->dn", ssm_in, both(lambda m: m.step_low))
    grad_small = jnp.concatenate([grad_bc, grad_dt], axis=1)
    grad_small = lax.psum_scatter(grad_small, "dp", scatter_dimension=0, tiled=True)
    grad_up = dotl("ra,rn->an", both(lambda m: m.adapter), both(lambda m: m.gate_up_own))
    grad_up = lax.psum_scatter(grad_up, "dp", scatter_dimension=0, tiled=True)

    sums_dp = jax.tree.map(lambda *v: total(v), *[m.sums_dp for m in micro])
    sums_all = jax.tree.map(lambda *v: total(v), *[m.sums_all for m in micro])
    flat_all = links.z_sum(jnp.concatenate([v.reshape(-1) for v in sums_all]))
    flat = links.dp_sum(jnp.concatenate([v.reshape(-1) for v in sums_dp] + [flat_all]))
    small_sums = []
    for v in sums_dp + sums_all:
        small_sums.append(flat[: v.size].reshape(v.shape))
        flat = flat[v.size :]
    own_gain = mixer_gain.shape[0]
    grad_g_mamba = lax.dynamic_slice_in_dim(small_sums[6], links.d * own_gain, own_gain)

    g_rows = total([jnp.stack([m.grad_g_attn, m.grad_g_mlp], 0) for m in micro])
    half = g_rows.shape[1] // 2
    g_rows = g_rows[:, :half] + links.core_swap(g_rows[:, half:])
    g_rows = links.z_sum(g_rows)

    def grad(spec, get_a, get_b, axis):
        return core_rs(links, total([dotf(spec, get_a(m), get_b(m)) for m in micro]), axis)

    block = both(lambda m: m.block)
    cols = both(lambda m: m.shared_cols)
    spec = "crd,crxn->dxn"
    grad_proj = proj_collect(
        links, dotf(spec, block, cols[:, :, :, 0]), dotl(spec, block, cols[:, :, :, 1])
    )
    grad_down = grad("crn,crd->nd", lambda m: m.hidden, lambda m: m.mlp_low, 1)
    grad_cols = grad("crd,crn->dn", lambda m: m.mlp_in, lambda m: m.gate_up_low, 0)
    grad_out = grad("crn,crd->nd", lambda m: m.attended, lambda m: m.attn_low, 1)
    grad_qkv = grad("crd,crn->dn", lambda m: m.attn_in, lambda m: m.d_qkv, 0)
    grad_qkv = jnp.stack(jnp.split(grad_qkv, 3, axis=1), 1)
    grad_gate_up = jnp.stack([grad_cols[:, :units], grad_cols[:, units : 2 * units]], 1)
    partial_t = [grad_cols[:, 2 * units :].astype(BF16), grad_small[:, :state_cols]]
    sizes = [v.size for v in partial_t]
    whole_t = links.z_sum(jnp.concatenate([v.reshape(-1, HEAD) for v in partial_t], 0))
    split = sizes[0] // HEAD
    grad_adapter_down = whole_t[:split].reshape(partial_t[0].shape).astype(F32)
    grad_bc = whole_t[split:].reshape(partial_t[1].shape).astype(F32)

    return (
        results,
        jnp.stack([m.d_hid for m in micro]),
        jnp.stack([m.d_emb for m in micro]),
        grad_qkv,
        grad_out,
        g_rows[0],
        g_rows[1],
        grad_gate_up,
        grad_adapter_down,
        grad_up.reshape(adapter_up.shape).astype(F32),
        grad_down,
        grad_proj,
        grad_g_mamba,
        grad_in.transpose(1, 0, 2).astype(F32),
        grad_bc,
        grad_small[:, state_cols:].astype(F32),
        grad_mout.T.astype(F32),
        small_sums[0],
        small_sums[5],
        small_sums[2],
        small_sums[3],
        small_sums[4],
        small_sums[1],
    )


def solution(mesh):
    rows = P(None, "dp", None)
    by_dp = P("dp", None, "tensor")
    by_t = P("tensor", "dp")
    weights = (by_dp, by_t, P("dp"), P("dp"), by_dp, P("dp", None), by_dp, by_t, by_t, P("dp"))
    weights += (by_dp, P("dp", None), P("dp", "tensor"), by_t)
    smalls = (P(None, "tensor"), P(), P("tensor"), P("tensor"), P("tensor"), P("tensor"))
    return jax.shard_map(
        partial(local, n_dp=mesh.shape["dp"], n_t=mesh.shape["tensor"]),
        mesh=mesh,
        in_specs=(rows, rows, rows) + weights + smalls + (rows,),
        out_specs=(rows, rows, rows) + weights + smalls,
        check_vma=False,
    )
```

```python
from functools import partial
from types import SimpleNamespace

import jax
import jax.numpy as jnp
from jax import lax
from jax.experimental import pallas as pl
from jax.experimental.pallas import tpu as pltpu
from jax.sharding import PartitionSpec as P

HEAD = 128
EPSILON = 1e-05
ROPE_BASE = 10000.0
MASKED = -1e30
TOP_PRECISION = lax.Precision.HIGHEST
F32 = jnp.float32
BF16 = jnp.bfloat16


def layout(len_row, places):
    bounds = jnp.cumsum(len_row)[:-1]
    passed = places[:, None] >= bounds[None, :]
    segment = jnp.sum(passed.astype(jnp.int32), axis=1)
    starts = jnp.max(jnp.where(passed, bounds[None, :], 0), axis=1)
    position = places - starts
    valid = segment < bounds.shape[0]
    allowed = (segment[:, None] == segment[None, :]) & (places[None, :] <= places[:, None])
    return (segment, position, valid, allowed)


def rope_tables(position):
    half = HEAD // 2
    frequency = ROPE_BASE ** (-2.0 * jnp.arange(half, dtype=F32) / HEAD)
    angles = position.astype(F32)[:, None] * frequency[None, :]
    cosine, sine = jnp.cos(angles), jnp.sin(angles)
    return jnp.concatenate([cosine, cosine], axis=1), jnp.concatenate([-sine, sine], axis=1)


def rows_down(x, count):
    return x if count == 0 else pltpu.roll(x, count, 0)


def rows_up(x, count):
    return x if count == 0 else pltpu.roll(x, x.shape[0] - count, 0)


def conv_taps(x, taps_ref, same_ref):
    summed = x * taps_ref[0:1, :]
    for j in range(1, taps_ref.shape[0]):
        summed = summed + rows_down(x, j) * same_ref[:, j : j + 1] * taps_ref[j : j + 1, :]
    return summed


def conv_taps_back(x, d_out, taps_ref, same_ref, d_taps_ref, cols):
    d_x = d_out * taps_ref[0:1, cols]
    d_taps_ref[0:1, cols] = jnp.sum(d_out * x, axis=0, keepdims=True)
    for j in range(1, taps_ref.shape[0]):
        kept = d_out * same_ref[:, j : j + 1]
        d_taps_ref[j : j + 1, cols] = jnp.sum(kept * rows_down(x, j), axis=0, keepdims=True)
        d_x = d_x + rows_up(kept * taps_ref[j : j + 1, cols], j)
    return d_x


def exact(a, b, dims):
    return lax.dot_general(
        a, b, (dims, ((), ())), precision=TOP_PRECISION, preferred_element_type=F32
    )


def fast(a, b, dims):
    return lax.dot_general(
        a.astype(BF16), b.astype(BF16), (dims, ((), ())), preferred_element_type=F32
    )


PLAIN = ((1,), (0,))
BY_COLS = ((1,), (1,))
BY_ROWS = ((0,), (0,))


def triangle(rows):
    t = lax.broadcasted_iota(jnp.int32, (rows, rows), 0)
    s = lax.broadcasted_iota(jnp.int32, (rows, rows), 1)
    return t, s


def step_terms(step_ref, bias_ref, decay_ref, rows):
    t, s = triangle(rows)
    raw = step_ref[...] + bias_ref[...]
    step = jnp.maximum(raw, 0.0) + jnp.log1p(jnp.exp(-jnp.abs(raw)))
    log_decay = -step * jnp.exp(decay_ref[...])
    running = exact((s <= t).astype(F32), log_decay, PLAIN)
    running_t = exact(log_decay, (t <= s).astype(F32), BY_ROWS)
    step_t = exact(step, (t == s).astype(F32), BY_ROWS)
    return raw, step, log_decay, running, running_t, step_t


def decayed(running, running_t, h, allowed):
    gap = running[:, h : h + 1] - running_t[h : h + 1, :]
    return jnp.exp(jnp.where(allowed, gap, MASKED))


def mix_kernel(
    gate_ref, state_ref, step_ref, taps_x_ref, taps_bc_ref, bias_ref, decay_ref, skip_ref,
    same_ref, allowed_ref, d_scaled_ref, gated_ref, sums_ref,
):
    rows = state_ref.shape[0]
    size = state_ref.shape[1] // 2
    heads = step_ref.shape[1]
    lanes = 128
    per = lanes * heads // gate_ref.shape[2]
    allowed = allowed_ref[...] > 0.0
    _, _, _, running, running_t, step_t = step_terms(step_ref, bias_ref, decay_ref, rows)
    conv_bc = conv_taps(state_ref[...], taps_bc_ref, same_ref)
    state = conv_bc * jax.nn.sigmoid(conv_bc)
    affinity = exact(state[:, size:], state[:, :size], BY_COLS)
    lane = lax.broadcasted_iota(jnp.int32, (rows, lanes), 1) * per // lanes
    squares = jnp.zeros((rows, lanes), F32)
    weighted = jnp.zeros((rows, lanes), F32)
    for group in range(gate_ref.shape[2] // lanes):
        cols = slice(group * lanes, (group + 1) * lanes)
        x = gate_ref[1, :, cols]
        conv = x * taps_x_ref[0:1, cols]
        for j in range(1, taps_x_ref.shape[0]):
            conv = conv + rows_down(x, j) * same_ref[:, j : j + 1] * taps_x_ref[j : j + 1, cols]
        act = conv * jax.nn.sigmoid(conv)
        mixed = act * skip_ref[0:1, cols]
        for i in range(per):
            h = group * per + i
            mixing = decayed(running, running_t, h, allowed) * affinity * step_t[h : h + 1, :]
            mixed = mixed + jnp.where(lane == i, fast(mixing, act, PLAIN), 0.0)
        z = gate_ref[0, :, cols]
        gated = mixed * (z * jax.nn.sigmoid(z))
        gated_ref[:, cols] = gated
        squares = squares + gated * gated
        weighted = weighted + gated * d_scaled_ref[:, cols]
    sums_ref[:, 0:1] = jnp.sum(squares, axis=1, keepdims=True)
    sums_ref[:, 1:2] = jnp.sum(weighted, axis=1, keepdims=True)


def mix_back_kernel(
    gate_ref, state_ref, step_ref, taps_x_ref, taps_bc_ref, bias_ref, decay_ref, skip_ref,
    same_ref, allowed_ref, d_scaled_ref, gated_ref, scales_ref,
    d_gate_ref, d_state_ref, d_step_ref, d_taps_x_ref, d_taps_bc_ref, d_bias_ref, d_decay_ref,
    d_skip_ref,
):
    rows = state_ref.shape[0]
    size = state_ref.shape[1] // 2
    heads = step_ref.shape[1]
    lanes = 128
    per = lanes * heads // gate_ref.shape[2]
    allowed = allowed_ref[...] > 0.0
    raw, step, log_decay, running, running_t, step_t = step_terms(
        step_ref, bias_ref, decay_ref, rows
    )
    conv_bc = conv_taps(state_ref[...], taps_bc_ref, same_ref)
    sig_bc = jax.nn.sigmoid(conv_bc)
    state = conv_bc * sig_bc
    affinity = exact(state[:, size:], state[:, :size], BY_COLS)
    lane = lax.broadcasted_iota(jnp.int32, (rows, lanes), 1) * per // lanes
    head_lane = lax.broadcasted_iota(jnp.int32, (rows, heads), 1)
    head_row = lax.broadcasted_iota(jnp.int32, (heads, rows), 0)
    d_affinity = jnp.zeros((rows, rows), F32)
    d_run = jnp.zeros((rows, heads), F32)
    d_step_t = jnp.zeros((heads, rows), F32)
    for group in range(gate_ref.shape[2] // lanes):
        cols = slice(group * lanes, (group + 1) * lanes)
        x = gate_ref[1, :, cols]
        conv = x * taps_x_ref[0:1, cols]
        for j in range(1, taps_x_ref.shape[0]):
            conv = conv + rows_down(x, j) * same_ref[:, j : j + 1] * taps_x_ref[j : j + 1, cols]
        sig = jax.nn.sigmoid(conv)
        act = conv * sig
        z = gate_ref[0, :, cols]
        sig_z = jax.nn.sigmoid(z)
        d_gated = d_scaled_ref[:, cols] * scales_ref[:, 0:1] - gated_ref[:, cols] * scales_ref[:, 1:2]
        d_mixed = d_gated * (z * sig_z)
        mixed = act * skip_ref[0:1, cols]
        d_act = d_mixed * skip_ref[0:1, cols]
        d_skip_ref[0:1, cols] = jnp.sum(d_mixed * act, axis=0, keepdims=True)
        for i in range(per):
            h = group * per + i
            decay = decayed(running, running_t, h, allowed)
            weight = affinity * step_t[h : h + 1, :]
            mixing = decay * weight
            mixed = mixed + jnp.where(lane == i, fast(mixing, act, PLAIN), 0.0)
            d_act = d_act + jnp.where(lane == i, fast(mixing, d_mixed, BY_ROWS), 0.0)
            d_mixing = fast(jnp.where(lane == i, d_mixed, 0.0), act, BY_COLS) * decay
            d_affinity = d_affinity + d_mixing * step_t[h : h + 1, :]
            by_aff = d_mixing * affinity
            d_step_t = d_step_t + jnp.where(
                head_row == h, jnp.sum(by_aff, axis=0, keepdims=True), 0.0
            )
            by_gap = jnp.sum(by_aff * step_t[h : h + 1, :], axis=1, keepdims=True)
            d_run = d_run + jnp.where(head_lane == h, by_gap, 0.0)
        d_gate_ref[0, :, cols] = (d_gated * mixed * (sig_z * (1.0 + z * (1.0 - sig_z)))).astype(BF16)
        d_conv = d_act * (sig * (1.0 + conv * (1.0 - sig)))
        d_x = conv_taps_back(x, d_conv, taps_x_ref, same_ref, d_taps_x_ref, cols)
        d_gate_ref[1, :, cols] = d_x.astype(BF16)
    t, s = triangle(rows)
    eye = (t == s).astype(F32)
    d_run = d_run - exact(eye, d_step_t * step_t, BY_COLS)
    d_log = exact((s >= t).astype(F32), d_run, PLAIN)
    d_step = exact(eye, d_step_t, BY_COLS) - jnp.exp(decay_ref[...]) * d_log
    d_raw = d_step * jax.nn.sigmoid(raw)
    d_step_ref[...] = d_raw
    d_bias_ref[...] = jnp.sum(d_raw, axis=0, keepdims=True)
    d_decay_ref[...] = jnp.sum(d_log * log_decay, axis=0, keepdims=True)
    d_b = exact(d_affinity, state[:, size:], BY_ROWS)
    d_c = exact(d_affinity, state[:, :size], PLAIN)
    d_silu = sig_bc * (1.0 + conv_bc * (1.0 - sig_bc))
    for part, d_part in enumerate((d_b, d_c)):
        cols = slice(part * size, (part + 1) * size)
        d_conv = d_part * d_silu[:, cols]
        d_x = conv_taps_back(
            state_ref[:, cols], d_conv, taps_bc_ref, same_ref, d_taps_bc_ref, cols
        )
        d_state_ref[:, cols] = d_x.astype(BF16)


def turned(x, cos_ref, sin_ref, sign):
    return x * cos_ref[...] + pltpu.roll(x, HEAD // 2, 1) * (sign * sin_ref[...])


def probabilities(query, key, allowed):
    scores = fast(query, key, BY_COLS) * HEAD ** (-0.5)
    scores = jnp.where(allowed, scores, MASKED)
    raised = jnp.exp(scores - jnp.max(scores, axis=1, keepdims=True))
    return raised / jnp.sum(raised, axis=1, keepdims=True)


def attend_kernel(qkv_ref, cos_ref, sin_ref, allowed_ref, low_ref, attended_ref):
    allowed = allowed_ref[...] > 0.0
    width = attended_ref.shape[1]
    for h in range(width // HEAD):
        q, k, v = (slice(i * width + h * HEAD, i * width + (h + 1) * HEAD) for i in range(3))
        query = turned(qkv_ref[:, q], cos_ref, sin_ref, 1.0).astype(BF16)
        key = turned(qkv_ref[:, k], cos_ref, sin_ref, 1.0).astype(BF16)
        value = qkv_ref[:, v].astype(BF16)
        low_ref[:, q] = query
        low_ref[:, k] = key
        low_ref[:, v] = value
        probs = probabilities(query, key, allowed)
        attended_ref[:, q] = fast(probs, value, PLAIN).astype(BF16)


def attend_back_kernel(low_ref, d_ref, cos_ref, sin_ref, allowed_ref, d_qkv_ref):
    allowed = allowed_ref[...] > 0.0
    width = d_ref.shape[1]
    for h in range(width // HEAD):
        q, k, v = (slice(i * width + h * HEAD, i * width + (h + 1) * HEAD) for i in range(3))
        query, key, value = low_ref[:, q], low_ref[:, k], low_ref[:, v]
        d_out = d_ref[:, q].astype(BF16)
        probs = probabilities(query, key, allowed)
        d_qkv_ref[:, v] = fast(probs, d_out, BY_ROWS).astype(BF16)
        d_probs = fast(d_out, value, BY_COLS)
        inner = jnp.sum(probs * d_probs, axis=1, keepdims=True)
        d_scores = (probs * (d_probs - inner) * HEAD ** (-0.5)).astype(BF16)
        d_query = fast(d_scores, key, PLAIN)
        d_key = fast(d_scores, query, BY_ROWS)
        d_qkv_ref[:, q] = turned(d_query, cos_ref, sin_ref, -1.0).astype(BF16)
        d_qkv_ref[:, k] = turned(d_key, cos_ref, sin_ref, -1.0).astype(BF16)


def in_vmem(kernel, outs, args, flops):
    size = sum(x.size * x.dtype.itemsize for x in tuple(args) + tuple(outs))
    return pl.pallas_call(
        kernel,
        out_shape=outs,
        in_specs=[pl.BlockSpec(memory_space=pltpu.VMEM)] * len(args),
        out_specs=[pl.BlockSpec(memory_space=pltpu.VMEM)] * len(outs),
        compiler_params=pltpu.CompilerParams(vmem_limit_bytes=40 * 2**20),
        cost_estimate=pl.CostEstimate(flops=flops, bytes_accessed=size, transcendentals=0),
    )(*args)


def gated_gelu(gate_up):
    half = gate_up.shape[1] // 2
    return jax.nn.gelu(gate_up[:, :half], approximate=True) * gate_up[:, half:]


def total(values):
    summed = values[0]
    for value in values[1:]:
        summed = summed + value
    return summed


def after(x, done):
    mark = done[(-1,) * done.ndim].astype(F32)
    return x + jnp.minimum(jnp.abs(mark), 0.0).astype(x.dtype)


class Links:
    def __init__(self, n_dp, n_t):
        self.n_dp = n_dp
        self.n_t = n_t
        self.chips = n_dp // 2
        self.chip_bits = self.chips.bit_length() - 1
        self.z_bits = n_t.bit_length() - 1
        d = lax.axis_index("dp")
        self.d = d
        self.core = d % 2
        self.chip = d // 2
        self.t = lax.axis_index("tensor")

    def core_swap(self, x):
        return lax.ppermute(x, "dp", [(i, i ^ 1) for i in range(self.n_dp)])

    def chip_swap(self, x, rel):
        return lax.ppermute(x, "dp", [(i, i ^ (rel << 1)) for i in range(self.n_dp)])

    def z_swap(self, x, rel):
        return lax.ppermute(x, "tensor", [(i, i ^ rel) for i in range(self.n_t)])

    def row_parts(self, rows):
        count = max(1, min(self.chip_bits, rows // 16))
        units = rows // 16
        edges = [0] + [16 * ((units * (i + 1)) // count) for i in range(count)]
        edges[-1] = rows
        return [(edges[i], edges[i + 1]) for i in range(count)]

    def chip_rs(self, terms, axis, direct=False):
        if direct:
            blocks = [
                lax.index_in_dim(terms, rel, axis, keepdims=False) for rel in range(self.chips)
            ]
            return total([block.astype(F32) for block in self.chip_a2a(blocks)])
        outs = []
        bits = self.chip_bits
        for number, (low, high) in enumerate(self.row_parts(terms.shape[axis + 1])):
            cur = lax.slice_in_dim(terms, low, high, axis=axis + 1)
            cur = cur.reshape(cur.shape[:axis] + (2,) * bits + cur.shape[axis + 1 :])
            left = list(range(bits))[::-1]
            for step in range(bits):
                bit = (number + step) % bits
                at = axis + left.index(bit)
                left.remove(bit)
                keep = lax.index_in_dim(cur, 0, at, keepdims=False)
                send = lax.index_in_dim(cur, 1, at, keepdims=False)
                got = self.chip_swap(send.astype(BF16), 1 << bit)
                cur = keep.astype(F32) + got.astype(F32)
            outs.append(cur)
        return outs[0] if len(outs) == 1 else jnp.concatenate(outs, axis=axis)

    def chip_ag(self, x, axis, direct=False):
        if direct:
            return jnp.stack(self.chip_a2a([x] * self.chips), axis=axis)
        bits = self.chip_bits
        outs = []
        for number, (low, high) in enumerate(self.row_parts(x.shape[axis])):
            blocks = {0: lax.slice_in_dim(x, low, high, axis=axis)}
            for step in range(bits):
                bit = (number + step) % bits
                for rel in list(blocks):
                    blocks[rel | (1 << bit)] = self.chip_swap(blocks[rel], 1 << bit)
            outs.append([blocks[rel] for rel in range(self.chips)])
        merged = []
        for rel in range(self.chips):
            pieces = [part[rel] for part in outs]
            merged.append(pieces[0] if len(pieces) == 1 else jnp.concatenate(pieces, axis=axis))
        return jnp.stack(merged, axis=axis)

    def chip_a2a(self, blocks):
        return [blocks[0]] + [self.chip_swap(blocks[rel], rel) for rel in range(1, self.chips)]

    def chip_sum(self, x):
        total = x
        for rel in range(1, self.chips):
            moved = jnp.stack([x[i ^ rel] for i in range(self.chips)], 0)
            total = total + self.chip_swap(moved, rel)
        return total

    def z_sum(self, x):
        return total([x] + [self.z_swap(x, rel) for rel in range(1, self.n_t)])

    def dp_sum(self, x):
        x = x + self.core_swap(x)
        return total(self.chip_a2a([x] * self.chips))

    def z_rs(self, terms, axis):
        bits = self.z_bits
        cur = terms.reshape(terms.shape[:axis] + (2,) * bits + terms.shape[axis + 1 :])
        left = list(range(bits))[::-1]
        for bit in range(bits):
            at = axis + left.index(bit)
            left.remove(bit)
            keep = lax.index_in_dim(cur, 0, at, keepdims=False)
            send = lax.index_in_dim(cur, 1, at, keepdims=False)
            got = self.z_swap(send.astype(BF16), 1 << bit)
            cur = keep.astype(F32) + got.astype(F32)
        return cur

    def z_ag(self, x, axis):
        blocks = {0: x}
        for bit in range(self.z_bits)[::-1]:
            for rel in list(blocks):
                blocks[rel | (1 << bit)] = self.z_swap(blocks[rel], 1 << bit)
        return jnp.stack([blocks[rel] for rel in range(self.n_t)], axis=axis)

    def dp_order(self, x, axis):
        split = x.reshape(x.shape[:axis] + (self.chips, 2, -1) + x.shape[axis + 1 :])
        split = self.by_index(self.by_index(split, axis + 1, self.core), axis, self.chip)
        return split.reshape(x.shape)

    def by_index(self, x, axis, own):
        count = x.shape[axis]
        return jnp.concatenate(
            [lax.dynamic_slice_in_dim(x, own ^ i, 1, axis=axis) for i in range(count)], axis=axis
        )

    def rows_by_t(self, x):
        rows = x.shape[0]
        split = x.reshape((self.n_t, rows // self.n_t) + x.shape[1:])
        return self.by_index(split, 0, self.t).reshape(x.shape)


def core_pair(links, x, axis):
    return jnp.concatenate([x, links.core_swap(x)], axis=axis)


def core_rs(links, x, axis):
    half = x.shape[axis] // 2
    own = lax.slice_in_dim(x, 0, half, axis=axis)
    other = lax.slice_in_dim(x, half, 2 * half, axis=axis)
    return own + links.core_swap(other.astype(BF16)).astype(F32)


def dotf(spec, a, b):
    return jnp.einsum(spec, a, b, preferred_element_type=F32)


def dotl(spec, a, b):
    return jnp.einsum(spec, a, b, preferred_element_type=F32).astype(BF16)


def flip(index, bit):
    return index + (1 - 2 * ((index // bit) % 2)) * bit


def chip_partner(rel):
    d = lax.axis_index("dp")
    for bit in (1, 2):
        if rel & bit:
            d = flip(d, 2 * bit)
    return {"dp": d}


def z_partner(rel):
    return {"tensor": flip(lax.axis_index("tensor"), rel)}


def core_partner():
    return {"dp": flip(lax.axis_index("dp"), 1)}


def partner_of(axis, rel):
    if axis == "core":
        return core_partner()
    return chip_partner(rel) if axis == "dp" else z_partner(rel)


def xor(a, b):
    return sum(((a // bit + b // bit) % 2) * bit for bit in (1, 2))


def core_order(x):
    half = x.shape[-1] // 2
    turned = jnp.concatenate([x[..., half:], x[..., :half]], axis=-1)
    return jnp.where(lax.axis_index("dp") % 2 == 1, turned, x)


class Wire:
    def __init__(self, send, recv):
        self.send, self.recv, self.used = send, recv, 0

    def start(self, src, dst, partner):
        i = self.used
        self.used += 1
        copy = pltpu.make_async_remote_copy(
            src_ref=src,
            dst_ref=dst,
            send_sem=self.send.at[i],
            recv_sem=self.recv.at[i],
            device_id=partner,
            device_id_type=pl.DeviceIdType.MESH,
        )
        copy.start()
        return copy


TILE = 256


def over_tiles(width, body, offset=0):
    def step(i, carry):
        at = pl.ds(pl.multiple_of(i * TILE, 128), TILE)
        body(at, pl.ds(pl.multiple_of(offset + i * TILE, 128), TILE))
        return carry

    count = width // TILE
    lax.fori_loop(0, count, step, 0)
    if width % TILE:
        low, left = count * TILE, width % TILE
        body(pl.ds(low, left), pl.ds(offset + low, left))


class RowPair:
    def __init__(self, own, other):
        self.args = (own, other)
        self.parts = own.shape[0] if own.ndim == 3 else 1
        self.half, self.cols = own.shape[-2:]
        self.shape = (2 * self.half, self.parts * self.cols)

    def whole(self):
        both = jnp.concatenate(self.args, axis=-2)
        return both if both.ndim == 2 else jnp.concatenate(list(both), axis=1)

    def pick(self, ref, part):
        return ref if self.parts == 1 else ref.at[part]

    def times(self, x, refs, by_cols, store):
        half, cols = self.half, self.cols
        if by_cols:
            for h, ref in enumerate(refs):

                def body(at, to, ref=ref):
                    store(
                        to,
                        total(
                            [
                                fast(x(slice(i * cols, i * cols + cols)), self.pick(ref, i)[at, :], BY_COLS)
                                for i in range(self.parts)
                            ]
                        ),
                    )

                over_tiles(half, body, h * half)
            return
        for i in range(self.parts):

            def body(at, to, i=i):
                own, other = (self.pick(ref, i)[:, at] for ref in refs)
                left, right = x(slice(0, half)), x(slice(half, 2 * half))
                store(to, fast(left, own, PLAIN) + fast(right, other, PLAIN))

            over_tiles(cols, body, i * cols)


class ColPair:
    def __init__(self, own, other):
        self.args = (own, other)
        self.rows, self.half = own.shape
        self.shape = (self.rows, 2 * self.half)

    def whole(self):
        return jnp.concatenate(self.args, axis=1)

    def times(self, x, refs, by_cols, store):
        half = self.half
        if by_cols:
            own, other = refs

            def body(at, to):
                left, right = x(slice(0, half)), x(slice(half, 2 * half))
                store(to, fast(left, own[at, :], BY_COLS) + fast(right, other[at, :], BY_COLS))

            over_tiles(self.rows, body)
            return
        for h, ref in enumerate(refs):

            def body(at, to, ref=ref):
                store(to, fast(x(slice(0, self.rows)), ref[:, at], PLAIN))

            over_tiles(half, body, h * half)


class ByChips:
    copies = 12
    partners = [("dp", 1), ("dp", 2)]

    def __init__(self, x, w, by_cols, out_width, local, args, outs, scratch=()):
        self.by_cols, self.local, self.count = by_cols, local, len(args)
        self.rows = x.shape[1]
        self.width = w.shape[0] if by_cols else w.shape[1]
        self.w = w
        self.args = (x,) + w.args + tuple(args)
        self.outs = (jax.ShapeDtypeStruct((4, self.rows, out_width), BF16),) + tuple(outs)
        self.scratch = chip_scratch(self.rows, self.width)
        self.scratch += [pltpu.VMEM((self.rows, self.width), F32)] + list(scratch)
        self.flops = 8 * self.rows * x.shape[2] * self.width

    def run(self, wire, args, outs, scratch):
        x, w = args[0], args[1:3]
        part, first, second, summed = scratch[:4]
        gathered = outs[0]
        rows = self.rows

        def dot(low, high):
            def left(at):
                return x[low:high, :, at].reshape((high - low) * rows, at.stop - at.start)

            def store(to, value):
                part[low:high, :, to] = value.astype(BF16).reshape(high - low, rows, value.shape[1])

            self.w.times(left, w, self.by_cols, store)

        dot(1, 4)
        yield from chip_sum(wire, part, first, second, summed, lambda: dot(0, 1))
        self.local(summed, gathered.at[0], args[3:], outs[1:], scratch[4:])
        yield from chip_gather(wire, [gathered.at[rel] for rel in range(4)], rows)


def pieces(rows):
    half = rows // 2
    return [(p, slice(p * half, (p + 1) * half), 1 << p, 1 << (1 - p)) for p in range(2)]


def chip_sum(wire, part, first, second, summed, meanwhile=None):
    rows, width = summed.shape
    sent, later = [], []
    for p, at, bit, _ in pieces(rows):
        for i, rel in enumerate((bit, 3)):
            sent.append(wire.start(part.at[rel, at], first.at[p, i], chip_partner(bit)))
    if meanwhile:
        meanwhile()
    yield
    for p, at, _, other in pieces(rows):
        sent[2 * p + 1].wait_recv()

        def add(cols, _, p=p, at=at, other=other):
            both = part[other, at, cols].astype(F32) + first[p, 1, :, cols].astype(F32)
            part[other, at, cols] = both.astype(BF16)

        over_tiles(width, add)
        later.append(wire.start(part.at[other, at], second.at[p], chip_partner(other)))
    yield
    for p, at, _, _ in pieces(rows):
        sent[2 * p].wait_recv()
        later[p].wait_recv()

        def finish(cols, _, p=p, at=at):
            both = part[0, at, cols].astype(F32) + first[p, 0, :, cols].astype(F32)
            summed[at, cols] = both + second[p, :, cols].astype(F32)

        over_tiles(width, finish)
    for copy in sent + later:
        copy.wait_send()


def chip_gather(wire, slots, rows):
    near, far, last = [], [], []
    for _, at, bit, other in pieces(rows):
        near.append(wire.start(slots[0].at[at], slots[bit].at[at], chip_partner(bit)))
        far.append(wire.start(slots[0].at[at], slots[other].at[at], chip_partner(other)))
    yield
    for p, at, bit, other in pieces(rows):
        near[p].wait_recv()
        last.append(wire.start(slots[bit].at[at], slots[3].at[at], chip_partner(other)))
    yield
    for copy in far + last:
        copy.wait_recv()
    for copy in near + far + last:
        copy.wait_send()


def chip_scratch(rows, width):
    half = rows // 2
    return [
        pltpu.VMEM((4, rows, width), BF16),
        pltpu.VMEM((2, 2, half, width), BF16),
        pltpu.VMEM((2, half, width), BF16),
    ]


class GatherDp:
    partners = [("dp", 1), ("dp", 2), ("core", 1)]
    copies = 7
    flops = 0

    def __init__(self, x):
        self.args, self.rows = (x,), x.shape[0]
        self.outs = (jax.ShapeDtypeStruct((4, 2) + x.shape, BF16),)
        self.scratch = []

    def run(self, wire, args, outs, scratch):
        (out,) = outs
        out[0, 0] = args[0][...]
        yield from chip_gather(wire, [out.at[rel, 0] for rel in range(4)], self.rows)
        swap = wire.start(out.at[:, 0], out.at[:, 1], core_partner())
        yield
        swap.wait_recv()
        swap.wait_send()


class ScatterDp:
    partners = GatherDp.partners
    copies = 7
    flops = 0

    def __init__(self, own, other):
        self.args = (own, other)
        shape = own.shape[1:]
        self.outs = (jax.ShapeDtypeStruct(shape, F32),)
        self.scratch = [pltpu.VMEM(own.shape, BF16)] + chip_scratch(*shape)

    def run(self, wire, args, outs, scratch):
        own, other = args
        swapped, part, first, second = scratch
        swap = wire.start(other, swapped, core_partner())
        yield
        swap.wait_recv()
        for rel in range(4):

            def add(cols, _, rel=rel):
                both = own[rel, :, cols].astype(F32) + swapped[rel, :, cols].astype(F32)
                part[rel, :, cols] = both.astype(BF16)

            over_tiles(own.shape[2], add)
        yield from chip_sum(wire, part, first, second, outs[0])
        swap.wait_send()


def tensor_sum(weight, x, w, by_cols, wire, scratch):
    part, first, second, summed = scratch
    rows, width = summed.shape
    r = rows // 4

    def left(at):
        return x[:, :, at].reshape(4 * rows, at.stop - at.start)

    def store(to, value):
        low = value.astype(BF16)
        for c in range(4):
            for z in range(4):
                part[z, c * r : (c + 1) * r, to] = low[c * rows + z * r : c * rows + z * r + r]

    weight.times(left, w, by_cols, store)
    half = width // 2
    halves = [slice(h * half, (h + 1) * half) for h in range(2)]
    sent, later = [], []
    for h in halves:
        for i, z in ((1, 3), (0, 1)):
            sent.append(wire.start(part.at[z, :, h], first.at[i, :, h], z_partner(1)))
    yield
    for n, h in enumerate(halves):
        sent[2 * n].wait_recv()

        def add(_, cols):
            both = part[2, :, cols].astype(F32) + first[1, :, cols].astype(F32)
            part[2, :, cols] = both.astype(BF16)

        over_tiles(half, add, n * half)
        later.append(wire.start(part.at[2, :, h], second.at[:, h], z_partner(2)))
    yield
    for n in range(2):
        sent[2 * n + 1].wait_recv()
        later[n].wait_recv()

        def finish(_, cols):
            both = part[0, :, cols].astype(F32) + first[0, :, cols].astype(F32)
            summed[:, cols] = both + second[:, cols].astype(F32)

        over_tiles(half, finish, n * half)
    for copy in sent + later:
        copy.wait_send()


def sum_scratch(rows, width):
    return [
        pltpu.VMEM((4, rows, width), BF16),
        pltpu.VMEM((2, rows, width), BF16),
        pltpu.VMEM((rows, width), BF16),
        pltpu.VMEM((rows, width), F32),
    ]


def true_slots(ref):
    t = lax.axis_index("tensor")
    own = [ref.at[xor(t, rel)] for rel in range(4)]
    return own, [None, own[0], own[0], own[2]]


def tensor_gather(wire, slots, there=None):
    there = there or slots
    far = wire.start(slots[0], there[2], z_partner(2))
    near = wire.start(slots[0], there[1], z_partner(1))
    yield
    far.wait_recv()
    last = wire.start(slots[2], there[3], z_partner(1))
    yield
    near.wait_recv()
    last.wait_recv()
    for copy in (far, near, last):
        copy.wait_send()


class ByTensor:
    copies = 9
    partners = [("tensor", 1), ("tensor", 2), ("dp", 1), ("dp", 2), ("dp", 3)]

    def __init__(self, x, w, by_cols, local, args, outs, gather=True):
        self.by_cols, self.local, self.gather = by_cols, local, gather
        self.rows = x.shape[1]
        self.width = w.shape[0] if by_cols else w.shape[1]
        self.w = w
        self.args = (x,) + w.args + tuple(args)
        shape = (4, 4, self.rows // 4, self.width)
        self.outs = (jax.ShapeDtypeStruct(shape, BF16),) if gather else ()
        self.outs += tuple(outs)
        self.copies = 12 if gather else 9
        self.scratch = sum_scratch(self.rows, self.width)
        self.scratch += [pltpu.VMEM((4, self.rows, 128), F32)]
        self.flops = 8 * self.rows * x.shape[2] * self.width

    def run(self, wire, args, outs, scratch):
        summed, stats = scratch[3:5]
        rows = self.rows
        r = rows // 4
        yield from tensor_sum(self.w, args[0], args[1:3], self.by_cols, wire, scratch[:4])
        rest = outs[1:] if self.gather else outs[:1]
        local = self.local(summed, args[3:7], rest)
        stats[0] = jnp.broadcast_to(next(local), (rows, 128))
        sums = [
            wire.start(stats.at[0], stats.at[rel], chip_partner(rel)) for rel in range(1, 4)
        ]
        yield
        total_sums = stats[0]
        for rel in range(1, 4):
            sums[rel - 1].wait_recv()
            moved = [stats[rel, (i ^ rel) * r : (i ^ rel) * r + r, :] for i in range(4)]
            total_sums = total_sums + jnp.concatenate(moved, axis=0)
        low = local.send(total_sums[:, 0:1])
        if self.gather:
            gathered = outs[0]
            for c in range(4):
                gathered[c, 0] = low[c * r : (c + 1) * r]
            far = wire.start(gathered.at[:, 0], gathered.at[:, 2], z_partner(2))
            near = wire.start(gathered.at[:, 0], gathered.at[:, 1], z_partner(1))
            yield
            far.wait_recv()
            last = wire.start(gathered.at[:, 2], gathered.at[:, 3], z_partner(1))
            yield
            near.wait_recv()
            last.wait_recv()
            sums += [far, near, last]
        else:
            yield from self.tail(wire, low, args, outs, scratch)
        for copy in sums:
            copy.wait_send()


class Leave(ByTensor):
    def __init__(self, x, w, local, args, d_gain, theirs):
        super().__init__(x, w, True, local, args, (d_gain,), gather=False)
        r = self.rows // 4
        self.args += (theirs,)
        self.outs += (jax.ShapeDtypeStruct((4, r, 4 * self.width), BF16),)
        self.copies = 15
        self.scratch += [pltpu.VMEM((4, r, self.width), BF16)] * 2
        self.scratch += [pltpu.VMEM((r, 4 * self.width), BF16)]

    def tail(self, wire, low, args, outs, scratch):
        theirs, out = args[-1], outs[-1]
        mine, came, block_ref = scratch[5:]
        r, width = self.rows // 4, self.width
        half = width // 2
        d, t = lax.axis_index("dp"), lax.axis_index("tensor")
        for c in range(4):
            mine[c] = low[c * r : (c + 1) * r]
        sent = [
            wire.start(mine.at[rel], came.at[rel], chip_partner(rel)) for rel in range(1, 4)
        ]
        yield
        for rel in range(4):
            if rel:
                sent[rel - 1].wait_recv()
            block = (came if rel else mine)[rel].astype(F32)
            for j in range(2):
                at = 2 * xor(d // 2, rel) + (d + j) % 2
                at = pl.ds(pl.multiple_of(at * half, 128), half)
                low = block[:, j * half : (j + 1) * half] + theirs[:, at]
                block_ref[:, at] = low.astype(BF16)
        out[t] = block_ref[...]
        yield from tensor_gather(wire, *true_slots(out))
        for copy in sent:
            copy.wait_send()


class FeedOut:
    partners = [("tensor", 1), ("tensor", 2), ("dp", 1), ("dp", 2), ("dp", 3)]
    copies = 12

    def __init__(self, x, w, mid, proj):
        self.w = w
        self.rows, self.width = x.shape[1], w.shape[1]
        self.cols = proj.shape[3]
        r = self.rows // 4
        self.args = (x,) + w.args + (mid, proj)
        wide = 8 * self.cols
        self.outs = (
            jax.ShapeDtypeStruct((self.rows, self.width), BF16),
            jax.ShapeDtypeStruct((4, r, wide), BF16),
            jax.ShapeDtypeStruct((r, wide), BF16),
        )
        self.scratch = sum_scratch(self.rows, self.width)
        self.scratch += [pltpu.VMEM((4, r, wide), BF16)] * 2
        self.flops = 8 * self.rows * x.shape[2] * self.width

    def run(self, wire, args, outs, scratch):
        mid, proj = args[3:]
        block, gathered, own = outs
        summed, part, came = scratch[3:]
        r = self.rows // 4
        d = lax.axis_index("dp")
        yield from tensor_sum(self.w, args[0], args[1:3], False, wire, scratch[:4])
        block[...] = core_order((mid[...] + summed[...]).astype(BF16))
        for x in range(4):
            for y in range(2):
                at = 2 * xor(d // 2, x) + (d + y) % 2
                at = pl.ds(pl.multiple_of(at * self.cols, 128), self.cols)
                value = fast(block[...], proj[x, y], PLAIN).astype(BF16)
                part[:, :, at] = value.reshape(4, r, self.cols)
        sent = [
            wire.start(part.at[rel], came.at[rel], chip_partner(rel)) for rel in range(1, 4)
        ]
        yield
        shared = part[0].astype(F32)
        for rel in range(1, 4):
            sent[rel - 1].wait_recv()
            shared = shared + came[rel].astype(F32)
        own[...] = shared.astype(BF16)
        gathered[lax.axis_index("tensor")] = own[...]
        yield from tensor_gather(wire, *true_slots(gathered))
        for copy in sent:
            copy.wait_send()


class Settle:
    partners = [("tensor", 1), ("tensor", 2), ("dp", 1), ("dp", 2), ("dp", 3)]
    copies = 9

    def __init__(self, terms, bc, mamba_in, gain, grad, proj):
        self.args = (terms, bc, mamba_in, gain, grad, proj)
        r, wide = mamba_in.shape
        self.r, self.wide, self.cols = r, wide, proj.shape[3]
        states, width = terms.shape[2] - wide, proj.shape[2]
        self.outs = (
            jax.ShapeDtypeStruct((4, 4, r, width), BF16),
            jax.ShapeDtypeStruct((4, r, wide), BF16),
            jax.ShapeDtypeStruct((r, wide), F32),
            jax.ShapeDtypeStruct((r, states), BF16),
            jax.ShapeDtypeStruct((4 * r, width), F32),
            jax.ShapeDtypeStruct((1, wide), F32),
        )
        self.scratch = [
            pltpu.VMEM((2, r, terms.shape[2]), BF16),
            pltpu.VMEM((r, terms.shape[2]), BF16),
            pltpu.VMEM((r, terms.shape[2]), BF16),
        ]
        self.flops = 16 * r * wide * width

    def run(self, wire, args, outs, scratch):
        terms, bc, mamba_in, gain, grad, proj = args
        gathered, shared, d_mamba, state, d_block, d_gain = outs
        first, middle, second = scratch
        wide = self.wide
        d = lax.axis_index("dp")
        sent = [wire.start(terms.at[z], first.at[i], z_partner(1)) for i, z in enumerate((1, 3))]
        yield
        sent[1].wait_recv()
        middle[...] = (terms[2].astype(F32) + first[1].astype(F32)).astype(BF16)
        sent.append(wire.start(middle, second, z_partner(2)))
        yield
        sent[0].wait_recv()
        sent[2].wait_recv()
        summed = terms[0].astype(F32) + first[0].astype(F32) + second[...].astype(F32)
        state[...] = summed[:, wide:].astype(BF16)
        dy = summed[:, :wide] + fast(state[...], bc[...], BY_COLS)
        v = mamba_in[...]
        inv = lax.rsqrt(jnp.mean(v * v, axis=1, keepdims=True) + EPSILON)
        scaled = dy * gain[...]
        inner = jnp.mean(scaled * v, axis=1, keepdims=True)
        d_gain[...] = jnp.sum(dy * v * inv, axis=0, keepdims=True)
        d_mamba[...] = inv * scaled - v * (inv * inv * inv * inner) + grad[...].astype(F32)
        shared[0] = d_mamba[...].astype(BF16)
        more = [
            wire.start(shared.at[0], shared.at[rel], chip_partner(rel)) for rel in range(1, 4)
        ]
        yield
        for copy in more:
            copy.wait_recv()
        result = None
        for x in range(4):
            for y in range(2):
                at = 2 * xor(d // 2, x) + (d + y) % 2
                at = pl.ds(pl.multiple_of(at * self.cols, 128), self.cols)
                left = shared[:, :, at].reshape(4 * self.r, self.cols)
                value = fast(left, proj[x, y], BY_COLS)
                result = value if result is None else result + value
        d_block[...] = core_order(result)
        for c in range(4):
            gathered[c, 0] = d_block[c * self.r : (c + 1) * self.r].astype(BF16)
        yield from tensor_gather(wire, [gathered.at[:, i] for i in range(4)])
        for copy in sent + more:
            copy.wait_send()


class Spread:
    partners = [("tensor", 1), ("tensor", 2), ("dp", 1), ("dp", 2), ("dp", 3), ("core", 1)]
    copies = 7
    flops = 0

    def __init__(self, w):
        self.args = (w,)
        self.outs = (jax.ShapeDtypeStruct((4, 2) + w.shape, BF16),)
        self.scratch = [pltpu.VMEM((4,) + w.shape, BF16)]

    def run(self, wire, args, outs, scratch):
        (out,), (rows,) = outs, scratch
        rows[0] = args[0][...]
        yield from tensor_gather(wire, [rows.at[i] for i in range(4)])
        here = xor(lax.axis_index("dp") // 2, lax.axis_index("tensor"))
        sent = [
            wire.start(rows.at[xor(here, rel)], out.at[rel, 0], chip_partner(rel))
            for rel in range(1, 4)
        ]
        out[0, 0] = rows[here]
        yield
        for copy in sent:
            copy.wait_recv()
        sent.append(wire.start(out.at[:, 0], out.at[:, 1], core_partner()))
        yield
        sent[3].wait_recv()
        for copy in sent:
            copy.wait_send()


class Collect:
    partners = Spread.partners
    copies = 7
    flops = 0

    def __init__(self, own, other):
        self.args = (own, other)
        shape = own.shape[1:]
        self.outs = (jax.ShapeDtypeStruct(shape, F32),)
        self.scratch = [pltpu.VMEM((4,) + shape, BF16)] * 3
        self.scratch += [pltpu.VMEM((2,) + shape, BF16), pltpu.VMEM(shape, BF16)]

    def run(self, wire, args, outs, scratch):
        own, other = args
        (out,) = outs
        swapped, mine, came, first, second = scratch
        rows = own.shape[1]
        tile = 128
        sent = [wire.start(other, swapped, core_partner())]
        yield
        sent[0].wait_recv()
        for rel in range(4):

            def add(i, carry, rel=rel):
                at = pl.ds(pl.multiple_of(i * tile, tile), tile)
                both = own[rel, at, :] + swapped[rel, at, :].astype(F32)
                (mine if rel else came)[rel, at, :] = both.astype(BF16)
                return carry

            lax.fori_loop(0, rows // tile, add, 0)
            if rel:
                sent.append(wire.start(mine.at[rel], came.at[rel], chip_partner(rel)))
        yield
        for copy in sent[1:]:
            copy.wait_recv()
        here = xor(lax.axis_index("dp") // 2, lax.axis_index("tensor"))
        at = [xor(here, z) for z in range(4)]
        more = [wire.start(came.at[at[z]], first.at[i], z_partner(1)) for i, z in enumerate((1, 3))]
        yield
        more[1].wait_recv()

        def middle(i, carry):
            to = pl.ds(pl.multiple_of(i * tile, tile), tile)
            both = came[at[2], to, :].astype(F32) + first[1, to, :].astype(F32)
            swapped[0, to, :] = both.astype(BF16)
            return carry

        lax.fori_loop(0, rows // tile, middle, 0)
        more.append(wire.start(swapped.at[0], second, z_partner(2)))
        yield
        more[0].wait_recv()
        more[2].wait_recv()

        def finish(i, carry):
            to = pl.ds(pl.multiple_of(i * tile, tile), tile)
            both = came[at[0], to, :].astype(F32) + first[0, to, :].astype(F32)
            out[to, :] = both + second[to, :].astype(F32)
            return carry

        lax.fori_loop(0, rows // tile, finish, 0)
        for copy in sent + more:
            copy.wait_send()


class Outputs:
    partners = [("tensor", 1), ("tensor", 2)]
    copies = 6
    flops = 0

    def __init__(self, terms, base, valid):
        self.args = (terms, base, valid)
        self.outs = (jax.ShapeDtypeStruct(terms.shape, BF16),)
        shape = terms.shape[1:]
        self.scratch = [pltpu.VMEM((2,) + shape, BF16), pltpu.VMEM(shape, BF16)]
        self.scratch += [pltpu.VMEM(shape, BF16)]

    def run(self, wire, args, outs, scratch):
        terms, base, valid = args
        (gathered,) = outs
        first, middle, second = scratch
        sent = [wire.start(terms.at[z], first.at[i], z_partner(1)) for i, z in enumerate((1, 3))]
        yield
        sent[1].wait_recv()
        middle[...] = (terms[2].astype(F32) + first[1].astype(F32)).astype(BF16)
        sent.append(wire.start(middle, second, z_partner(2)))
        yield
        sent[0].wait_recv()
        sent[2].wait_recv()
        summed = terms[0].astype(F32) + first[0].astype(F32) + second[...].astype(F32)
        gathered[lax.axis_index("tensor")] = ((base[...] + summed) * valid[...]).astype(BF16)
        yield from tensor_gather(wire, *true_slots(gathered))
        for copy in sent:
            copy.wait_send()


class Enter:
    partners = [("dp", 1), ("dp", 2), ("dp", 3)]
    copies = 9
    flops = 0

    def __init__(self, hid, emb, gain):
        self.args = (hid, emb, gain)
        self.rows, self.half = hid.shape[0], gain.shape[1] // 2
        rows, width = self.rows, gain.shape[1]
        self.outs = (
            jax.ShapeDtypeStruct((4, rows, width), BF16),
            jax.ShapeDtypeStruct((rows, width), F32),
            jax.ShapeDtypeStruct((rows, 1), F32),
        )
        self.scratch = [
            pltpu.VMEM((rows, 4 * width), BF16),
            pltpu.VMEM((4, rows, width), BF16),
            pltpu.VMEM((4, rows, 128), F32),
        ]

    def run(self, wire, args, outs, scratch):
        hid, emb, gain = args
        attn_in, joined_z, inv_z = outs
        joined, came, stats = scratch
        rows, half = self.rows, self.half
        r, wide = rows // 4, hid.shape[1]
        d, t = lax.axis_index("dp"), lax.axis_index("tensor")
        for i in range(4):
            at = pl.ds(pl.multiple_of(xor(t, i) * r, r), r)
            to = slice(i * r, (i + 1) * r)
            left, right = hid[at, :], emb[at, :]
            joined[to, :wide] = left
            joined[to, wide:] = right
            left, right = left.astype(F32), right.astype(F32)
            squares = jnp.sum(left * left, axis=1, keepdims=True)
            squares = squares + jnp.sum(right * right, axis=1, keepdims=True)
            inverse = lax.rsqrt(squares / (2 * wide) + EPSILON)
            stats[0, to, :] = jnp.broadcast_to(inverse, (r, 128))
        sent = []
        for rel in (3, 1, 2):
            sent.append(wire.start(stats.at[0], stats.at[rel], chip_partner(rel)))
        for rel in (3, 1, 2, 0):
            for j in range(2):
                at = 2 * xor(d // 2, rel) + (d + j) % 2
                at = pl.ds(pl.multiple_of(at * half, 128), half)
                to = slice(j * half, (j + 1) * half)
                if rel:
                    src, dst = joined.at[:, at], came.at[rel, :, to]
                    sent.append(wire.start(src, dst, chip_partner(rel)))
                else:
                    came[0, :, to] = joined[:, at]
        yield
        for copy in sent:
            copy.wait_recv()
        for c in range(4):
            block = came[c].astype(F32)
            inverse = stats[c][:, 0:1]
            attn_in[c] = (block * inverse * gain[...]).astype(BF16)
            joined_z[c * r : (c + 1) * r] = block[:r]
            inv_z[c * r : (c + 1) * r] = inverse[:r]
        for copy in sent:
            copy.wait_send()


class WeightGrad:
    partners = [("core", 1)]
    copies = 1

    def __init__(self, a, b, by_rows, parts=1):
        self.count, self.by_rows, self.parts = len(a), by_rows, parts
        self.args = tuple(a) + tuple(b)
        self.height, self.width = a[0].shape[2], b[0].shape[2]
        if by_rows:
            self.height //= 2
        else:
            self.width //= 2
        self.cols = self.width // parts
        shape = (self.height, self.cols)
        shape = (parts,) + shape if parts > 1 else shape
        self.outs = (jax.ShapeDtypeStruct(shape, F32),)
        self.step = min(self.height, 512)
        self.scratch = [pltpu.VMEM(shape, BF16)] * 2
        self.scratch += [pltpu.VMEM((self.count, self.step, 4 * a[0].shape[1]), BF16)]
        self.flops = 4 * self.count * a[0].shape[1] * self.height * self.width * 2

    def run(self, wire, args, outs, scratch):
        (out,) = outs
        other, got, turned = scratch
        a, b = args[: self.count], args[self.count :]
        step = self.step
        tokens = 4 * a[0].shape[1]

        def work(half, ref):
            row, col = (half * self.height, 0) if self.by_rows else (0, half * self.width)
            for low in range(0, self.height, step):
                rows = slice(row + low, row + low + step)
                for i, x in enumerate(a):
                    turned[i] = x[:, :, rows].reshape(tokens, step).T
                for part in range(self.parts):
                    to_ref = ref if self.parts == 1 else ref.at[part]

                    def body(to, at, low=low, to_ref=to_ref):
                        terms = [
                            fast(turned[i], y[:, :, at].reshape(tokens, at.size), PLAIN)
                            for i, y in enumerate(b)
                        ]
                        to_ref[low : low + step, to] = total(terms).astype(to_ref.dtype)

                    over_tiles(self.cols, body, col + part * self.cols)
                    yield

        yield
        yield from work(1, other)
        swap = wire.start(other, got, core_partner())
        yield from work(0, out)
        swap.wait_recv()
        for part in range(self.parts):
            to_ref, got_ref = (out, got) if self.parts == 1 else (out.at[part], got.at[part])

            def add(cols, _, to_ref=to_ref, got_ref=got_ref):
                to_ref[:, cols] += got_ref[:, cols].astype(F32)

            over_tiles(self.cols, add)
        swap.wait_send()


def together(groups, collective_id):
    partners = sorted({p for g in groups for p in g.partners})

    def kernel(*refs):
        refs = list(refs)

        def take(count):
            got = refs[:count]
            del refs[:count]
            return got

        args = [take(len(g.args)) for g in groups]
        outs = [take(len(g.outs)) for g in groups]
        scratch = [take(len(g.scratch)) for g in groups]
        wires = [Wire(*take(2)) for g in groups]
        barrier = pltpu.get_barrier_semaphore()
        for axis, rel in partners:
            pl.semaphore_signal(
                barrier,
                inc=1,
                device_id=partner_of(axis, rel),
                device_id_type=pl.DeviceIdType.MESH,
            )
        pl.semaphore_wait(barrier, len(partners))
        running = [
            g.run(wire, a, o, s) for g, wire, a, o, s in zip(groups, wires, args, outs, scratch)
        ]
        while running:
            left = []
            for run in running:
                if next(run, running) is not running:
                    left.append(run)
            running = left

    args = [x for g in groups for x in g.args]
    outs = [x for g in groups for x in g.outs]
    scratch = [x for g in groups for x in g.scratch]
    for g in groups:
        scratch += [pltpu.SemaphoreType.DMA((g.copies,))] * 2
    size = sum(x.size * x.dtype.itemsize for x in args + outs)
    flat = pl.pallas_call(
        kernel,
        out_shape=outs,
        in_specs=[pl.BlockSpec(memory_space=pltpu.VMEM)] * len(args),
        out_specs=[pl.BlockSpec(memory_space=pltpu.VMEM)] * len(outs),
        scratch_shapes=scratch,
        compiler_params=pltpu.CompilerParams(
            collective_id=collective_id, has_side_effects=True, vmem_limit_bytes=62 * 2**20
        ),
        cost_estimate=pl.CostEstimate(
            flops=sum(g.flops for g in groups), bytes_accessed=size, transcendentals=0
        ),
    )(*args)
    results = []
    for g in groups:
        results.append(flat[: len(g.outs)])
        flat = flat[len(g.outs) :]
    return results


def attend_local(qkv, slot, args, outs, scratch):
    cos, sin, allowed = args
    attend_kernel(qkv, cos, sin, allowed, outs[0], slot)


def attend_back_local(d_attended, slot, args, outs, scratch):
    low, cos, sin, allowed = args
    attend_back_kernel(low, d_attended, cos, sin, allowed, slot)


GELU_SCALE = (2.0 / 3.141592653589793) ** 0.5


def feed_local(summed, slot, args, outs, scratch):
    (up,) = args
    gate_up, adapter = outs
    units = slot.shape[1]
    low = summed[:, 2 * units :].astype(BF16)
    adapter[...] = low

    def widen(cols, _):
        gate_up[:, cols] = summed[:, cols] + fast(low, up[:, cols], PLAIN)

    over_tiles(2 * units, widen)
    tile = 256

    def act(i, carry):
        at = pl.ds(pl.multiple_of(i * tile, 128), tile)
        also = pl.ds(pl.multiple_of(units + i * tile, 128), tile)
        v = gate_up[:, at]
        bent = jnp.tanh(GELU_SCALE * (v + 0.044715 * (v * v * v)))
        slot[:, at] = (0.5 * v * (1.0 + bent) * gate_up[:, also]).astype(BF16)
        return carry

    lax.fori_loop(0, units // tile, act, 0)


def feed_back_local(d_hidden, slot, args, outs, scratch):
    gate_up, up = args
    (adapter,) = scratch
    units = d_hidden.shape[1]
    tile = 256
    adapter[...] = jnp.zeros(adapter.shape, F32)

    def act(i, carry):
        at = pl.ds(pl.multiple_of(i * tile, 128), tile)
        also = pl.ds(pl.multiple_of(units + i * tile, 128), tile)
        v, u, d = gate_up[:, at], gate_up[:, also], d_hidden[:, at]
        bent = jnp.tanh(GELU_SCALE * (v + 0.044715 * (v * v * v)))
        slope = 0.5 * (1.0 + bent) + 0.5 * v * (1.0 - bent * bent) * GELU_SCALE * (
            1.0 + 3.0 * 0.044715 * (v * v)
        )
        d_gate = (d * u * slope).astype(BF16)
        d_up = (d * (0.5 * v * (1.0 + bent))).astype(BF16)
        slot[:, at] = d_gate
        slot[:, also] = d_up
        adapter[...] += fast(d_gate, up[:, at], BY_COLS) + fast(d_up, up[:, also], BY_COLS)
        return carry

    lax.fori_loop(0, units // tile, act, 0)
    slot[:, 2 * units :] = adapter[...].astype(BF16)


def norm_local(width, summed, args, outs):
    base, gain = args
    mid, inverse = outs
    value = base[...] + summed[...]
    mid[...] = value
    squares = yield jnp.sum(value * value, axis=1, keepdims=True)
    inv = lax.rsqrt(squares / width + EPSILON)
    inverse[...] = inv
    yield (value * inv * gain[...]).astype(BF16)


def norm_back_local(width, summed, args, outs):
    value, inverse, gain, skip = args
    d_gain = outs[-1]
    dy = summed[...]
    scaled = dy * gain[...]
    v, inv = value[...], inverse[...]
    weighted = yield jnp.sum(scaled * v, axis=1, keepdims=True)
    d_gain[...] = jnp.sum(dy * v * inv, axis=0, keepdims=True)
    result = scaled * inv - v * (inv * inv * inv * weighted / width) + skip[...]
    if len(outs) == 2:
        outs[0][...] = result
    yield result.astype(BF16)


def proj_spread(links, w):
    rows = links.z_ag(w, 0)
    if links.chips == links.n_t:
        blocks = [
            lax.dynamic_index_in_dim(rows, links.chip ^ links.t ^ rel, 0, keepdims=False)
            for rel in range(links.chips)
        ]
    else:
        rows = links.by_index(rows, 0, links.t).reshape(links.chips, -1, w.shape[1])
        blocks = [
            lax.dynamic_index_in_dim(rows, links.chip ^ rel, 0, keepdims=False)
            for rel in range(links.chips)
        ]
    came = jnp.stack(links.chip_a2a(blocks), 0)
    return jnp.stack([came, links.core_swap(came)], 1)


def proj_collect(links, own, other):
    mine = (own + links.core_swap(other).astype(F32)).astype(BF16)
    blocks = [mine[rel] for rel in range(links.chips)]
    rows = jnp.stack(links.chip_a2a(blocks), 0)
    if links.chips == links.n_t:
        rows = links.by_index(rows, 0, links.chip ^ links.t)
    else:
        rows = links.by_index(rows, 0, links.chip).reshape(links.n_t, -1, own.shape[2])
        rows = links.by_index(rows, 0, links.t)
    return links.z_rs(rows, 0)


def core_halves(links, x):
    split = x.reshape(x.shape[:-1] + (2, x.shape[-1] // 2))
    return links.by_index(split, x.ndim - 1, links.core).reshape(x.shape)


def enter(links, w, m):
    rows = m.hid.shape[0]
    joined = links.rows_by_t(jnp.concatenate([m.hid, m.emb], axis=1))
    wide = joined.astype(F32)
    m.inverse = lax.rsqrt(jnp.mean(wide * wide, axis=1) + EPSILON)
    half = joined.shape[1] // links.n_dp
    blocks = []
    for rel in range(links.chips):
        at = 2 * (links.chip ^ rel)
        pieces = [
            lax.dynamic_slice_in_dim(joined, (at + (links.core ^ j)) * half, half, axis=1)
            for j in range(2)
        ]
        blocks.append(jnp.concatenate(pieces, axis=1))
    m.joined = jnp.stack(links.chip_a2a(blocks), 0)
    places = jnp.arange(rows, dtype=jnp.int32)
    m.true = layout(m.lens, places)
    _, position, _, allowed = layout(m.lens, links.rows_by_t(places))
    m.allowed_rel = allowed.astype(F32)
    m.cos, m.sin = rope_tables(position)


def attend(links, w, m):
    wide = m.joined.astype(F32) * m.inv_attn[:, :, None]
    m.attn_in = lax.optimization_barrier((wide * w.g_attn).astype(BF16))
    qkv = links.chip_rs(dotl("crd,dn->crn", m.attn_in, w.qkv), 0)
    rows, width = qkv.shape[0], qkv.shape[1] // 3
    outs = (
        jax.ShapeDtypeStruct((rows, 3 * width), BF16),
        jax.ShapeDtypeStruct((rows, width), BF16),
    )
    args = (qkv, m.cos, m.sin, m.allowed_rel)
    m.qkv_low, attended = in_vmem(attend_kernel, outs, args, 4 * rows * rows * width)
    m.attended = links.chip_ag(attended, 0, direct=True)


def z_split(links, x, axis):
    rows = x.shape[axis]
    return x.reshape(x.shape[:axis] + (links.n_t, rows // links.n_t) + x.shape[axis + 1 :])


def z_join(x, axis):
    return x.reshape(x.shape[:axis] + (-1,) + x.shape[axis + 2 :])


def attend_out(links, w, m):
    part = dotl("crn,nd->crd", m.attended, w.out)
    summed = links.z_rs(z_split(links, part, 1), 1)
    rows = summed.shape[1]
    m.joined_z = m.joined[:, :rows].astype(F32)
    m.inv_attn_z = m.inv_attn[:, :rows]
    mid = m.joined_z + summed
    m.mid = mid
    squares = links.chip_sum(jnp.sum(mid * mid, axis=2))
    width = mid.shape[2] * links.chips
    m.inv_mlp = lax.rsqrt(squares / width + EPSILON)
    low = (mid * m.inv_mlp[:, :, None] * w.g_mlp).astype(BF16)
    m.mlp_in = z_join(links.z_ag(low, 1), 1)


def feed(links, w, m):
    summed = links.chip_rs(dotl("crd,dn->crn", m.mlp_in, w.gate_up), 0)
    units = 2 * w.down.shape[0]
    m.adapter = summed[:, units:].astype(BF16)
    gate_up = summed[:, :units] + dotf("ra,an->rn", m.adapter, w.adapter_up)
    activated, m.gate_back = jax.vjp(gated_gelu, gate_up)
    m.hidden = links.chip_ag(activated.astype(BF16), 0, direct=True)


def feed_out(links, w, m):
    part = dotl("crn,nd->crd", m.hidden, w.down)
    summed = links.z_rs(z_split(links, part, 1), 1)
    m.block = (m.mid + summed).astype(BF16)
    m.block = core_halves(links, m.block)
    part = dotl("crd,xydn->xycrn", m.block, w.proj)
    part = links.by_index(links.by_index(part, 1, links.core), 0, links.chip)
    part = z_join(part, 0).transpose(1, 2, 0, 3)
    part = part.reshape(part.shape[:2] + (-1,))
    shared = links.chip_rs(part, 0, direct=True).astype(BF16)
    whole = links.by_index(links.z_ag(shared, 0), 0, links.t)
    shared_full = whole.reshape(-1, whole.shape[2])
    m.mamba_in = m.hid.astype(F32) + shared_full.astype(F32)
    own = z_split(links, m.hid, 0)
    own = lax.dynamic_index_in_dim(own, links.t, 0, keepdims=False)
    m.mamba_in_z = own.astype(F32) + shared.astype(F32)


def mix(links, w, m):
    taps_x, taps_bc, step_bias, decay_log, skip, gate_gain = w.smalls
    segment, _, valid, allowed = m.true
    mamba_in = m.mamba_in
    inverse = lax.rsqrt(jnp.mean(mamba_in * mamba_in, axis=1, keepdims=True) + EPSILON)
    ssm_in = (mamba_in * inverse * w.g_mamba).astype(BF16)
    gate_x = dotf("td,kdc->ktc", ssm_in, w.w_in)
    state_io = dotf("td,dn->tn", ssm_in, w.bc)
    step_raw = dotf("td,dn->tn", ssm_in, w.dt)
    grad_low = m.cot * valid[:, None].astype(BF16)
    d_norm = dotf("tn,in->ti", grad_low, w.mout)
    d_scaled = d_norm * gate_gain
    rows, width = gate_x.shape[1:]
    heads = step_raw.shape[1]
    earlier = [jnp.pad(segment, (j, 0), constant_values=-1)[:rows] for j in range(taps_x.shape[0])]
    same = jnp.stack([(e == segment).astype(F32) for e in earlier], 1)
    skips = jnp.repeat(skip, width // heads)[None, :]
    args = (gate_x, state_io, step_raw, taps_x, taps_bc, step_bias[None, :], decay_log[None, :])
    args += (skips, same, allowed.astype(F32), d_scaled)
    outs = (jax.ShapeDtypeStruct((rows, width), F32), jax.ShapeDtypeStruct((rows, 2), F32))
    gated, sums = in_vmem(mix_kernel, outs, args, 4 * rows * rows * width)
    inner = width * links.n_t
    sums = links.z_sum(sums)
    squares, weighted = sums[:, 0], sums[:, 1]
    row_scale = lax.rsqrt(squares / inner + EPSILON)
    m.gated_norm = (gated * row_scale[:, None] * gate_gain).astype(BF16)
    m.mamba_out = dotl("ti,in->tn", m.gated_norm, w.mout)

    grad_gain = jnp.sum(d_norm * gated * row_scale[:, None], axis=0)
    scales = jnp.stack([row_scale, row_scale**3 * weighted / inner], 1)
    outs = (
        jax.ShapeDtypeStruct(gate_x.shape, BF16),
        jax.ShapeDtypeStruct(state_io.shape, BF16),
        jax.ShapeDtypeStruct(step_raw.shape, F32),
        jax.ShapeDtypeStruct(taps_x.shape, F32),
        jax.ShapeDtypeStruct(taps_bc.shape, F32),
        jax.ShapeDtypeStruct((1, heads), F32),
        jax.ShapeDtypeStruct((1, heads), F32),
        jax.ShapeDtypeStruct((1, width), F32),
    )
    args += (gated, scales)
    grads = in_vmem(mix_back_kernel, outs, args, 16 * rows * rows * width)
    m.gate_x_low, d_state_io, d_step, d_taps_x, d_taps_bc, d_bias, d_decay, d_skip = grads
    d_skip = jnp.sum(d_skip.reshape(heads, width // heads), axis=1)
    m.step_low = d_step.astype(BF16)
    part_in = dotf("ktc,kdc->td", m.gate_x_low, w.w_in) + dotf("tn,dn->td", m.step_low, w.dt)
    terms = jnp.concatenate([part_in.astype(BF16), d_state_io], axis=1)
    m.terms = z_split(links, links.rows_by_t(terms), 0)
    m.ssm_in = ssm_in
    m.ssm_in_z = own_rows(links, ssm_in)
    m.grad_low = grad_low
    m.sums_dp = (d_taps_x, grad_gain, d_bias[0], d_decay[0], d_skip)
    m.d_taps_bc = d_taps_bc


def settle(links, w, m):
    summed = links.z_rs(m.terms, 0)
    model_width = m.mamba_in_z.shape[1]
    m.state_low = summed[:, model_width:].astype(BF16)
    dy = summed[:, :model_width] + dotf("tn,dn->td", m.state_low, w.bc)
    v = m.mamba_in_z
    inv = lax.rsqrt(jnp.mean(v * v, axis=1, keepdims=True) + EPSILON)
    scaled = dy * w.g_mamba
    dv = inv * scaled - v * (inv**3 * jnp.mean(scaled * v, axis=1, keepdims=True))
    grad_g_mamba = jnp.sum(dy * v * inv, axis=0)
    m.sums_all = (m.d_taps_bc, grad_g_mamba)
    m.d_mamba = dv + own_rows(links, m.grad_low).astype(F32)
    m.shared_low = links.chip_ag(m.d_mamba.astype(BF16), 0, direct=True)
    split = m.shared_low.reshape(m.shared_low.shape[:2] + w.proj.shape[:2] + (-1,))
    m.shared_cols = links.by_index(links.by_index(split, 3, links.core), 2, links.chip)
    d_block = core_halves(links, dotf("crxyn,xydn->crd", m.shared_cols, w.proj))
    m.d_block = d_block
    m.mlp_low = z_join(links.z_ag(d_block.astype(BF16), 1), 1)


def own_rows(links, x):
    return lax.dynamic_index_in_dim(z_split(links, x, 0), links.t, 0, keepdims=False)


def finish_output(links, micro):
    terms = jnp.stack([z_split(links, links.rows_by_t(m.mamba_out), 0) for m in micro], 0)
    summed = links.z_rs(terms, 1)
    base = jnp.stack([m.mamba_in_z for m in micro], 0)
    valid = jnp.stack([own_rows(links, m.true[2]) for m in micro], 0)
    low = ((base + summed) * valid[:, :, None].astype(F32)).astype(BF16)
    whole = links.by_index(links.z_ag(low, 1), 1, links.t)
    return z_join(whole, 1)


def feed_back(links, w, m):
    part = dotl("crd,nd->crn", m.mlp_low, w.down)
    d_hidden = links.chip_rs(part, 0)
    (d_gate_up,) = m.gate_back(d_hidden)
    m.gate_up_own = d_gate_up.astype(BF16)
    part = dotl("rn,an->ra", m.gate_up_own, w.adapter_up)
    m.gate_up_low = links.chip_ag(jnp.concatenate([m.gate_up_own, part], 1), 0)


def feed_back_out(links, w, m):
    part = dotl("crn,dn->crd", m.gate_up_low, w.gate_up)
    dy = links.z_rs(z_split(links, part, 1), 1)
    scaled = dy * w.g_mlp
    v, inv = m.mid, m.inv_mlp
    weighted = links.chip_sum(jnp.sum(scaled * v, axis=2))
    width = v.shape[2] * links.chips
    dv = scaled * inv[:, :, None] - v * (inv**3 * weighted / width)[:, :, None]
    m.grad_g_mlp = jnp.sum(dy * v * inv[:, :, None], axis=(0, 1))
    m.d_mid = dv + m.d_block
    m.attn_low = z_join(links.z_ag(m.d_mid.astype(BF16), 1), 1)


def attend_back(links, w, m):
    part = dotl("crd,nd->crn", m.attn_low, w.out)
    d_attended = links.chip_rs(part, 0, direct=True)
    rows, width = d_attended.shape
    outs = (jax.ShapeDtypeStruct((rows, 3 * width), BF16),)
    args = (m.qkv_low, d_attended, m.cos, m.sin, m.allowed_rel)
    (d_qkv,) = in_vmem(attend_back_kernel, outs, args, 10 * rows * rows * width)
    m.d_qkv = links.chip_ag(d_qkv, 0)


def leave(links, w, m):
    part = dotl("crn,dn->crd", m.d_qkv, w.qkv)
    dy = links.z_rs(z_split(links, part, 1), 1)
    scaled = dy * w.g_attn
    v, inv = m.joined_z, m.inv_attn_z
    weighted = links.chip_sum(jnp.sum(scaled * v, axis=2))
    width = v.shape[2] * links.chips
    dv = scaled * inv[:, :, None] - v * (inv**3 * weighted / width)[:, :, None]
    m.grad_g_attn = jnp.sum(dy * v * inv[:, :, None], axis=(0, 1))
    m.d_joined = (dv + m.d_mid).astype(BF16)
    leave_rows(links, m)


def leave_rows(links, m):
    d_joined = m.d_joined.reshape(links.chips, -1, m.d_joined.shape[-1])
    came = jnp.stack(links.chip_a2a([d_joined[rel] for rel in range(links.chips)]), 0)
    rows = came.shape[1]
    came = came.reshape(links.chips, rows, 2, -1)
    came = links.by_index(links.by_index(came, 2, links.core), 0, links.chip)
    came = came.transpose(1, 0, 2, 3).reshape(rows, -1)
    model_width = m.d_mamba.shape[1]
    d_hid = (came[:, :model_width].astype(F32) + m.d_mamba).astype(BF16)
    both = jnp.concatenate([d_hid, came[:, model_width:]], axis=1)
    whole = links.by_index(links.z_ag(both, 0), 0, links.t)
    whole = whole.reshape(-1, both.shape[1])
    m.d_hid, m.d_emb = whole[:, :model_width], whole[:, model_width:]


def sds(shape, dtype=F32):
    return jax.ShapeDtypeStruct(shape, dtype)


def mixer_rows(links, m):
    whole = m.shared_all.reshape(-1, m.shared_all.shape[2])
    m.mamba_in = m.hid.astype(F32) + whole.astype(F32)
    m.mamba_in_z = own_rows(links, m.hid).astype(F32) + m.shared_z.astype(F32)


def projection_grads(links, micro):
    block = jnp.concatenate([m.block for m in micro], axis=0)
    low = jnp.concatenate([m.shared_low for m in micro], axis=0)
    cols = links.dp_order(low, 2).reshape(low.shape[:2] + (links.chips, 2, -1))
    spec = "crd,crxn->xdn"
    return dotf(spec, block, cols[:, :, :, 0]), dotl(spec, block, cols[:, :, :, 1])


def enter_group(links, w, m):
    rows = m.hid.shape[0]
    places = jnp.arange(rows, dtype=jnp.int32)
    m.true = layout(m.lens, places)
    _, position, _, allowed = layout(m.lens, links.rows_by_t(places))
    m.allowed_rel = allowed.astype(F32)
    m.cos, m.sin = rope_tables(position)
    return Enter(m.hid, m.emb, w.g_attn[None, :])


def take_enter(m, got):
    m.attn_in, m.joined_z, m.inv_attn_z = got


def attend_group(links, w, m):
    rows, width = m.attn_in.shape[1], w.qkv_pair.shape[1]
    args = (m.cos, m.sin, m.allowed_rel)
    outs = (sds((rows, width), BF16),)
    return ByChips(m.attn_in, w.qkv_pair, False, width // 3, attend_local, args, outs)


def attend_out_group(links, w, m):
    width = m.joined_z.shape[1]
    outs = (sds(m.joined_z.shape), sds(m.inv_attn_z.shape))
    args = (m.joined_z, w.g_mlp[None, :])
    work = partial(norm_local, width * links.chips)
    return ByTensor(m.attended, w.out_pair, False, work, args, outs)


def feed_group(links, w, m):
    rows, units = m.mlp_in.shape[1], w.down_pair.shape[0]
    outs = (sds((rows, 2 * units)), sds((rows, w.gate_up_pair.shape[1] - 2 * units), BF16))
    args = (w.adapter_up,)
    return ByChips(m.mlp_in, w.gate_up_pair, False, units, feed_local, args, outs)


def feed_back_group(links, w, m):
    args = (m.gate_up, w.adapter_up)
    rank = w.gate_up_pair.shape[1] - m.gate_up.shape[1]
    scratch = (pltpu.VMEM((m.gate_up.shape[0], rank), F32),)
    width = w.gate_up_pair.shape[1]
    return ByChips(m.mlp_low, w.down_pair, True, width, feed_back_local, args, (), scratch)


def feed_back_out_group(links, w, m):
    width = m.mid_z.shape[1]
    args = (m.mid_z, m.inv_mlp, w.g_mlp[None, :], m.d_block.reshape(m.mid_z.shape))
    outs = (sds(m.mid_z.shape), sds((1, width)))
    work = partial(norm_back_local, width * links.chips)
    return ByTensor(m.gate_up_low, w.gate_up_pair, True, work, args, outs)


def attend_back_group(links, w, m):
    args = (m.qkv_low, m.cos, m.sin, m.allowed_rel)
    width = w.qkv_pair.shape[1]
    return ByChips(m.attn_low, w.out_pair, True, width, attend_back_local, args, ())


def leave_group(links, w, m):
    width = m.joined_z.shape[1]
    args = (m.joined_z, m.inv_attn_z, w.g_attn[None, :], m.d_mid)
    work = partial(norm_back_local, width * links.chips)
    theirs = jnp.concatenate([m.d_mamba, jnp.zeros_like(m.d_mamba)], axis=1)
    return Leave(m.d_qkv, w.qkv_pair, work, args, sds((1, width)), theirs)


def feed_out_group(links, w, m):
    return FeedOut(m.hidden, w.down_pair, m.mid_z, w.proj)


def settle_group(links, w, m):
    grad = own_rows(links, m.grad_low)
    return Settle(m.terms, w.bc, m.mamba_in_z, w.g_mamba[None, :], grad, w.proj)


def spread_group(links, w, m):
    return Spread(w.proj_own)


def outputs_group(links, w, micro):
    terms = [z_split(links, links.rows_by_t(m.mamba_out), 0) for m in micro]
    base = [m.mamba_in_z for m in micro]
    valid = [own_rows(links, m.true[2])[:, None].astype(F32) for m in micro]
    args = (jnp.concatenate(terms, 1), jnp.concatenate(base, 0), jnp.concatenate(valid, 0))
    return Outputs(*args)


def take_feed_out(m, got):
    m.block, m.shared_all, m.shared_z = got
    m.block = m.block.reshape(4, -1, m.block.shape[1])


def take_settle(m, got):
    gathered, m.shared_low, m.d_mamba, m.state_low, d_block, d_gain = got
    m.mlp_low = z_join(gathered, 1)
    m.d_block = d_block
    m.sums_all = (m.d_taps_bc, d_gain[0])


def take_attend(m, got):
    m.attended, m.qkv_low = got


def take_attend_out(m, got):
    gathered, m.mid_z, m.inv_mlp = got
    m.mlp_in = z_join(gathered, 1)
    m.mid = m.mid_z.reshape(gathered.shape[0], -1, gathered.shape[3])


def take_feed(m, got):
    m.hidden, m.gate_up, m.adapter = got


def take_feed_back(m, got):
    (m.gate_up_low,) = got
    m.gate_up_own = m.gate_up_low[0, :, : m.gate_up.shape[1]]


def take_feed_back_out(m, got):
    gathered, m.d_mid, d_gain = got
    m.attn_low = z_join(gathered, 1)
    m.grad_g_mlp = d_gain[0]


def take_attend_back(m, got):
    (m.d_qkv,) = got


def take_leave(m, got):
    d_gain, m.left = got
    m.grad_g_attn = d_gain[0]


def fused(links, w, number, *work):
    groups = [make(links, w, m) for make, _, m in work]
    for (_, taker, m), got in zip(work, together(groups, number)):
        taker(m, got)


ENTER = (enter_group, take_enter)
ATTEND = (attend_group, take_attend)
ATTEND_OUT = (attend_out_group, take_attend_out)
FEED = (feed_group, take_feed)
FEED_BACK = (feed_back_group, take_feed_back)
FEED_BACK_OUT = (feed_back_out_group, take_feed_back_out)
ATTEND_BACK = (attend_back_group, take_attend_back)
LEAVE = (leave_group, take_leave)
FEED_OUT = (feed_out_group, take_feed_out)
SETTLE = (settle_group, take_settle)


WEIGHT_GRADS = {
    "down": ("crn,crd->nd", "hidden", "mlp_low", False, 1),
    "gate_up": ("crd,crn->dn", "mlp_in", "gate_up_low", True, 1),
    "out": ("crn,crd->nd", "attended", "attn_low", False, 1),
    "qkv": ("crd,crn->dn", "attn_in", "d_qkv", True, 3),
}


def local(
    hidden,
    embedding,
    lengths,
    query_key_value_weight,
    attention_output_weight,
    attention_gain,
    feedforward_gain,
    gate_up_weight,
    adapter_down,
    adapter_up,
    down_weight,
    shared_projection_weight,
    mixer_gain,
    mixer_input_weight,
    state_map_weight,
    step_weight,
    mixer_output_weight,
    mixer_input_taps,
    state_map_taps,
    step_bias,
    decay_logarithm,
    head_skip_weight,
    gated_norm_gain,
    cotangent,
    n_dp,
    n_t,
):
    links = Links(n_dp, n_t)
    smalls = (
        mixer_input_taps,
        state_map_taps,
        step_bias,
        decay_logarithm,
        head_skip_weight,
        gated_norm_gain,
    )
    micro = [
        SimpleNamespace(
            hid=hidden[b], emb=embedding[b], lens=lengths[b, 0], cot=cotangent[b]
        )
        for b in range(hidden.shape[0])
    ]
    w = SimpleNamespace()
    gains = core_pair(links, jnp.stack([attention_gain, feedforward_gain], 0), 1).astype(F32)
    w.g_attn, w.g_mlp = gains[0], gains[1]
    parts = query_key_value_weight.transpose(1, 0, 2)
    w.qkv_pair = RowPair(parts, links.core_swap(parts))
    def stage(work, m):
        with jax.named_scope(f"{work.__name__}_micro{micro.index(m)}"):
            work(links, w, m)

    units = gate_up_weight.shape[2]
    up_own = adapter_up.reshape(adapter_up.shape[0], 2 * units)
    cols = jnp.concatenate([gate_up_weight[:, 0], gate_up_weight[:, 1], adapter_down], axis=1)
    w.out_pair = ColPair(attention_output_weight, links.core_swap(attention_output_weight))
    w.gate_up_pair = RowPair(cols, links.core_swap(cols))
    w.down_pair = ColPair(down_weight, links.core_swap(down_weight))
    w.proj_own = shared_projection_weight
    state_cols, step_cols = state_map_weight.shape[1], step_weight.shape[1]
    packed = jnp.concatenate([state_map_weight, step_weight, mixer_gain[:, None]], axis=1)

    w.smalls = smalls
    def gather_mixer():
        w.adapter_up = lax.all_gather(after(up_own, w.begun), "dp", axis=0, tiled=True)
        whole = lax.all_gather(after(packed, w.begun), "dp", axis=0, tiled=True)
        w.bc = whole[:, :state_cols]
        w.dt = whole[:, state_cols : state_cols + step_cols]
        w.g_mamba = whole[:, state_cols + step_cols].astype(F32)
        shard = after(mixer_input_weight.transpose(1, 0, 2), w.begun)
        w.w_in = lax.all_gather(shard, "dp", axis=1, tiled=True)
        shard = after(mixer_output_weight, w.begun)
        w.mout = lax.all_gather(shard, "dp", axis=1, tiled=True)

    def run(*works):
        for work in works:
            for m in micro:
                stage(work, m)

    def both(get, axis=0):
        return jnp.concatenate([get(m) for m in micro], axis=axis)

    def mixer_grads(done=None):
        ssm_in = both(lambda m: m.ssm_in)
        grad_in = dotl("td,ktc->kdc", ssm_in, both(lambda m: m.gate_x_low, 1))
        begun = grad_in
        grad_in = grad_in if done is None else after(grad_in, done)
        grad_in = lax.psum_scatter(grad_in, "dp", scatter_dimension=1, tiled=True)
        grad_mout = dotl("tn,ti->ni", both(lambda m: m.grad_low), both(lambda m: m.gated_norm))
        grad_mout = grad_mout if done is None else after(grad_mout, done)
        grad_mout = lax.psum_scatter(grad_mout, "dp", scatter_dimension=0, tiled=True)
        grad_bc = dotl("td,tn->dn", both(lambda m: m.ssm_in_z), both(lambda m: m.state_low))
        grad_dt = dotl("td,tn->dn", ssm_in, both(lambda m: m.step_low))
        grad_small = jnp.concatenate([grad_bc, grad_dt], axis=1)
        grad_small = lax.psum_scatter(grad_small, "dp", scatter_dimension=0, tiled=True)
        grad_up = dotl("ra,rn->an", both(lambda m: m.adapter), both(lambda m: m.gate_up_own))
        grad_up = lax.psum_scatter(grad_up, "dp", scatter_dimension=0, tiled=True)
        return begun, grad_in, grad_mout, grad_small, grad_up

    def weight_grad(name):
        _, a, b, by_rows, parts = WEIGHT_GRADS[name]

        def make(*_):
            return WeightGrad([getattr(m, a) for m in micro], [getattr(m, b) for m in micro], by_rows, parts)

        return (make, lambda _, got: setattr(w, "grad_" + name, got[0]), None)

    if links.chips == 4 and links.n_t == 4 and len(micro) == 2:
        a, b = micro
        spread = (spread_group, lambda _, got: setattr(w, "proj", got[0]), None)
        fused(links, w, 1, (*ENTER, a))
        fused(links, w, 2, (*ATTEND, a), spread, (*ENTER, b))
        w.begun = a.attended
        gather_mixer()
        fused(links, w, 3, (*ATTEND_OUT, a), (*ATTEND, b))
        fused(links, w, 4, (*FEED, a), (*ATTEND_OUT, b))
        fused(links, w, 5, (*FEED, b), (*FEED_OUT, a))
        mixer_rows(links, a)
        stage(mix, a)
        fused(links, w, 6, (*FEED_OUT, b), (*SETTLE, a))
        mixer_rows(links, b)
        stage(mix, b)
        outputs = (outputs_group, lambda _, got: setattr(w, "results", got[0]), micro)
        fused(links, w, 7, (*FEED_BACK, a), (*SETTLE, b), outputs)
        collect = (lambda *_: Collect(*projection_grads(links, micro)), lambda _, got: setattr(w, "grad_proj", got[0]), None)
        fused(links, w, 8, (*FEED_BACK_OUT, a), (*FEED_BACK, b))
        fused(links, w, 9, (*FEED_BACK_OUT, b), (*ATTEND_BACK, a), weight_grad("gate_up"))
        fused(links, w, 10, (*LEAVE, a), (*ATTEND_BACK, b), weight_grad("down"))
        mixed = mixer_grads(b.d_qkv)
        fused(links, w, 11, (*LEAVE, b), weight_grad("qkv"), weight_grad("out"), collect)
        grad_down, grad_cols, grad_out = w.grad_down, w.grad_gate_up, w.grad_out
        grad_qkv = w.grad_qkv.transpose(1, 0, 2)
        grad_proj = w.grad_proj
        for m in micro:
            m.d_hid, m.d_emb = jnp.split(m.left.reshape(-1, m.left.shape[2]), 2, axis=1)
        results = w.results.reshape(links.n_t, len(micro), -1, w.results.shape[2])
        results = z_join(results.transpose(1, 0, 2, 3), 1)
    else:
        for m in micro:
            stage(enter, m)
        inverses = jnp.stack([m.inverse for m in micro], 0)
        inverses = jnp.stack(links.chip_a2a([inverses] * links.chips), 1)
        for b, m in enumerate(micro):
            m.inv_attn = inverses[b]
        w.qkv, w.out = w.qkv_pair.whole(), w.out_pair.whole()
        w.gate_up, w.down = w.gate_up_pair.whole(), w.down_pair.whole()
        w.proj = proj_spread(links, shared_projection_weight)
        run(attend)
        w.begun = micro[0].attended
        gather_mixer()
        run(attend_out, feed, feed_out, mix, settle)
        run(feed_back, feed_back_out, attend_back, leave)
        results = finish_output(links, micro)
        grad_proj = proj_collect(links, *projection_grads(links, micro))
        mixed = mixer_grads()

        def grad(name, axis):
            spec, a, b = WEIGHT_GRADS[name][:3]
            terms = [dotf(spec, getattr(m, a), getattr(m, b)) for m in micro]
            return core_rs(links, total(terms), axis)

        grad_down, grad_cols, grad_out = grad("down", 1), grad("gate_up", 0), grad("out", 1)
        grad_qkv = jnp.stack(jnp.split(grad("qkv", 0), 3, axis=1), 1)
    _, grad_in, grad_mout, grad_small, grad_up = mixed
    sums_dp = jax.tree.map(lambda *v: total(v), *[m.sums_dp for m in micro])
    sums_all = jax.tree.map(lambda *v: total(v), *[m.sums_all for m in micro])
    flat_all = links.z_sum(jnp.concatenate([v.reshape(-1) for v in sums_all]))
    flat = links.dp_sum(jnp.concatenate([v.reshape(-1) for v in sums_dp] + [flat_all]))
    small_sums = []
    for v in sums_dp + sums_all:
        small_sums.append(flat[: v.size].reshape(v.shape))
        flat = flat[v.size :]
    own_gain = mixer_gain.shape[0]
    grad_g_mamba = lax.dynamic_slice_in_dim(small_sums[6], links.d * own_gain, own_gain)

    g_rows = total([jnp.stack([m.grad_g_attn, m.grad_g_mlp], 0) for m in micro])
    half = g_rows.shape[1] // 2
    g_rows = g_rows[:, :half] + links.core_swap(g_rows[:, half:])
    g_rows = links.z_sum(g_rows)

    grad_gate_up = jnp.stack([grad_cols[:, :units], grad_cols[:, units : 2 * units]], 1)
    partial_t = [grad_cols[:, 2 * units :].astype(BF16), grad_small[:, :state_cols]]
    sizes = [v.size for v in partial_t]
    whole_t = links.z_sum(jnp.concatenate([v.reshape(-1, HEAD) for v in partial_t], 0))
    split = sizes[0] // HEAD
    grad_adapter_down = whole_t[:split].reshape(partial_t[0].shape).astype(F32)
    grad_bc = whole_t[split:].reshape(partial_t[1].shape).astype(F32)

    return (
        results,
        jnp.stack([m.d_hid for m in micro]),
        jnp.stack([m.d_emb for m in micro]),
        grad_qkv,
        grad_out,
        g_rows[0],
        g_rows[1],
        grad_gate_up,
        grad_adapter_down,
        grad_up.reshape(adapter_up.shape).astype(F32),
        grad_down,
        grad_proj,
        grad_g_mamba,
        grad_in.transpose(1, 0, 2).astype(F32),
        grad_bc,
        grad_small[:, state_cols:].astype(F32),
        grad_mout.T.astype(F32),
        small_sums[0],
        small_sums[5],
        small_sums[2],
        small_sums[3],
        small_sums[4],
        small_sums[1],
    )


def solution(mesh):
    rows = P(None, "dp", None)
    by_dp = P("dp", None, "tensor")
    by_t = P("tensor", "dp")
    weights = (by_dp, by_t, P("dp"), P("dp"), by_dp, P("dp", None), by_dp, by_t, by_t, P("dp"))
    weights += (by_dp, P("dp", None), P("dp", "tensor"), by_t)
    smalls = (P(None, "tensor"), P(), P("tensor"), P("tensor"), P("tensor"), P("tensor"))
    return jax.shard_map(
        partial(local, n_dp=mesh.shape["dp"], n_t=mesh.shape["tensor"]),
        mesh=mesh,
        in_specs=(rows, rows, rows) + weights + smalls + (rows,),
        out_specs=(rows, rows, rows) + weights + smalls,
        check_vma=False,
    )
```

```python
from functools import partial
from types import SimpleNamespace

import jax
import jax.numpy as jnp
from jax import lax
from jax.experimental import pallas as pl
from jax.experimental.pallas import tpu as pltpu
from jax.sharding import PartitionSpec as P

HEAD = 128
EPSILON = 1e-05
ROPE_BASE = 10000.0
MASKED = -1e30
TOP_PRECISION = lax.Precision.HIGHEST
F32 = jnp.float32
BF16 = jnp.bfloat16


def layout(len_row, places):
    bounds = jnp.cumsum(len_row)[:-1]
    passed = places[:, None] >= bounds[None, :]
    segment = jnp.sum(passed.astype(jnp.int32), axis=1)
    starts = jnp.max(jnp.where(passed, bounds[None, :], 0), axis=1)
    position = places - starts
    valid = segment < bounds.shape[0]
    allowed = (segment[:, None] == segment[None, :]) & (places[None, :] <= places[:, None])
    return (segment, position, valid, allowed)


def rope_tables(position):
    half = HEAD // 2
    frequency = ROPE_BASE ** (-2.0 * jnp.arange(half, dtype=F32) / HEAD)
    angles = position.astype(F32)[:, None] * frequency[None, :]
    cosine, sine = jnp.cos(angles), jnp.sin(angles)
    return jnp.concatenate([cosine, cosine], axis=1), jnp.concatenate([-sine, sine], axis=1)


def rows_down(x, count):
    return x if count == 0 else pltpu.roll(x, count, 0)


def rows_up(x, count):
    return x if count == 0 else pltpu.roll(x, x.shape[0] - count, 0)


def conv_taps(x, taps_ref, same_ref):
    summed = x * taps_ref[0:1, :]
    for j in range(1, taps_ref.shape[0]):
        summed = summed + rows_down(x, j) * same_ref[:, j : j + 1] * taps_ref[j : j + 1, :]
    return summed


def conv_taps_back(x, d_out, taps_ref, same_ref, d_taps_ref, cols):
    d_x = d_out * taps_ref[0:1, cols]
    d_taps_ref[0:1, cols] = jnp.sum(d_out * x, axis=0, keepdims=True)
    for j in range(1, taps_ref.shape[0]):
        kept = d_out * same_ref[:, j : j + 1]
        d_taps_ref[j : j + 1, cols] = jnp.sum(kept * rows_down(x, j), axis=0, keepdims=True)
        d_x = d_x + rows_up(kept * taps_ref[j : j + 1, cols], j)
    return d_x


def exact(a, b, dims):
    return lax.dot_general(
        a, b, (dims, ((), ())), precision=TOP_PRECISION, preferred_element_type=F32
    )


def fast(a, b, dims):
    return lax.dot_general(
        a.astype(BF16), b.astype(BF16), (dims, ((), ())), preferred_element_type=F32
    )


PLAIN = ((1,), (0,))
BY_COLS = ((1,), (1,))
BY_ROWS = ((0,), (0,))


def triangle(rows):
    t = lax.broadcasted_iota(jnp.int32, (rows, rows), 0)
    s = lax.broadcasted_iota(jnp.int32, (rows, rows), 1)
    return t, s


def step_terms(step_ref, bias_ref, decay_ref, rows):
    t, s = triangle(rows)
    raw = step_ref[...] + bias_ref[...]
    step = jnp.maximum(raw, 0.0) + jnp.log1p(jnp.exp(-jnp.abs(raw)))
    log_decay = -step * jnp.exp(decay_ref[...])
    running = exact((s <= t).astype(F32), log_decay, PLAIN)
    running_t = exact(log_decay, (t <= s).astype(F32), BY_ROWS)
    step_t = exact(step, (t == s).astype(F32), BY_ROWS)
    return raw, step, log_decay, running, running_t, step_t


def decayed(running, running_t, h, allowed):
    gap = running[:, h : h + 1] - running_t[h : h + 1, :]
    return jnp.exp(jnp.where(allowed, gap, MASKED))


def mix_kernel(
    gate_ref, state_ref, step_ref, taps_x_ref, taps_bc_ref, bias_ref, decay_ref, skip_ref,
    same_ref, allowed_ref, d_scaled_ref, gated_ref, sums_ref,
):
    rows = state_ref.shape[0]
    size = state_ref.shape[1] // 2
    heads = step_ref.shape[1]
    lanes = 128
    per = lanes * heads // gate_ref.shape[2]
    allowed = allowed_ref[...] > 0.0
    _, _, _, running, running_t, step_t = step_terms(step_ref, bias_ref, decay_ref, rows)
    conv_bc = conv_taps(state_ref[...], taps_bc_ref, same_ref)
    state = conv_bc * jax.nn.sigmoid(conv_bc)
    affinity = exact(state[:, size:], state[:, :size], BY_COLS)
    lane = lax.broadcasted_iota(jnp.int32, (rows, lanes), 1) * per // lanes
    squares = jnp.zeros((rows, lanes), F32)
    weighted = jnp.zeros((rows, lanes), F32)
    for group in range(gate_ref.shape[2] // lanes):
        cols = slice(group * lanes, (group + 1) * lanes)
        x = gate_ref[1, :, cols]
        conv = x * taps_x_ref[0:1, cols]
        for j in range(1, taps_x_ref.shape[0]):
            conv = conv + rows_down(x, j) * same_ref[:, j : j + 1] * taps_x_ref[j : j + 1, cols]
        act = conv * jax.nn.sigmoid(conv)
        mixed = act * skip_ref[0:1, cols]
        for i in range(per):
            h = group * per + i
            mixing = decayed(running, running_t, h, allowed) * affinity * step_t[h : h + 1, :]
            mixed = mixed + jnp.where(lane == i, fast(mixing, act, PLAIN), 0.0)
        z = gate_ref[0, :, cols]
        gated = mixed * (z * jax.nn.sigmoid(z))
        gated_ref[:, cols] = gated
        squares = squares + gated * gated
        weighted = weighted + gated * d_scaled_ref[:, cols]
    sums_ref[:, 0:1] = jnp.sum(squares, axis=1, keepdims=True)
    sums_ref[:, 1:2] = jnp.sum(weighted, axis=1, keepdims=True)


def mix_back_kernel(
    gate_ref, state_ref, step_ref, taps_x_ref, taps_bc_ref, bias_ref, decay_ref, skip_ref,
    same_ref, allowed_ref, d_scaled_ref, gated_ref, scales_ref,
    d_gate_ref, d_state_ref, d_step_ref, d_taps_x_ref, d_taps_bc_ref, d_bias_ref, d_decay_ref,
    d_skip_ref,
):
    rows = state_ref.shape[0]
    size = state_ref.shape[1] // 2
    heads = step_ref.shape[1]
    lanes = 128
    per = lanes * heads // gate_ref.shape[2]
    allowed = allowed_ref[...] > 0.0
    raw, step, log_decay, running, running_t, step_t = step_terms(
        step_ref, bias_ref, decay_ref, rows
    )
    conv_bc = conv_taps(state_ref[...], taps_bc_ref, same_ref)
    sig_bc = jax.nn.sigmoid(conv_bc)
    state = conv_bc * sig_bc
    affinity = exact(state[:, size:], state[:, :size], BY_COLS)
    lane = lax.broadcasted_iota(jnp.int32, (rows, lanes), 1) * per // lanes
    head_lane = lax.broadcasted_iota(jnp.int32, (rows, heads), 1)
    head_row = lax.broadcasted_iota(jnp.int32, (heads, rows), 0)
    d_affinity = jnp.zeros((rows, rows), F32)
    d_run = jnp.zeros((rows, heads), F32)
    d_step_t = jnp.zeros((heads, rows), F32)
    for group in range(gate_ref.shape[2] // lanes):
        cols = slice(group * lanes, (group + 1) * lanes)
        x = gate_ref[1, :, cols]
        conv = x * taps_x_ref[0:1, cols]
        for j in range(1, taps_x_ref.shape[0]):
            conv = conv + rows_down(x, j) * same_ref[:, j : j + 1] * taps_x_ref[j : j + 1, cols]
        sig = jax.nn.sigmoid(conv)
        act = conv * sig
        z = gate_ref[0, :, cols]
        sig_z = jax.nn.sigmoid(z)
        d_gated = d_scaled_ref[:, cols] * scales_ref[:, 0:1] - gated_ref[:, cols] * scales_ref[:, 1:2]
        d_mixed = d_gated * (z * sig_z)
        mixed = act * skip_ref[0:1, cols]
        d_act = d_mixed * skip_ref[0:1, cols]
        d_skip_ref[0:1, cols] = jnp.sum(d_mixed * act, axis=0, keepdims=True)
        for i in range(per):
            h = group * per + i
            decay = decayed(running, running_t, h, allowed)
            weight = affinity * step_t[h : h + 1, :]
            mixing = decay * weight
            mixed = mixed + jnp.where(lane == i, fast(mixing, act, PLAIN), 0.0)
            d_act = d_act + jnp.where(lane == i, fast(mixing, d_mixed, BY_ROWS), 0.0)
            d_mixing = fast(jnp.where(lane == i, d_mixed, 0.0), act, BY_COLS) * decay
            d_affinity = d_affinity + d_mixing * step_t[h : h + 1, :]
            by_aff = d_mixing * affinity
            d_step_t = d_step_t + jnp.where(
                head_row == h, jnp.sum(by_aff, axis=0, keepdims=True), 0.0
            )
            by_gap = jnp.sum(by_aff * step_t[h : h + 1, :], axis=1, keepdims=True)
            d_run = d_run + jnp.where(head_lane == h, by_gap, 0.0)
        d_gate_ref[0, :, cols] = (d_gated * mixed * (sig_z * (1.0 + z * (1.0 - sig_z)))).astype(BF16)
        d_conv = d_act * (sig * (1.0 + conv * (1.0 - sig)))
        d_x = conv_taps_back(x, d_conv, taps_x_ref, same_ref, d_taps_x_ref, cols)
        d_gate_ref[1, :, cols] = d_x.astype(BF16)
    t, s = triangle(rows)
    eye = (t == s).astype(F32)
    d_run = d_run - exact(eye, d_step_t * step_t, BY_COLS)
    d_log = exact((s >= t).astype(F32), d_run, PLAIN)
    d_step = exact(eye, d_step_t, BY_COLS) - jnp.exp(decay_ref[...]) * d_log
    d_raw = d_step * jax.nn.sigmoid(raw)
    d_step_ref[...] = d_raw
    d_bias_ref[...] = jnp.sum(d_raw, axis=0, keepdims=True)
    d_decay_ref[...] = jnp.sum(d_log * log_decay, axis=0, keepdims=True)
    d_b = exact(d_affinity, state[:, size:], BY_ROWS)
    d_c = exact(d_affinity, state[:, :size], PLAIN)
    d_silu = sig_bc * (1.0 + conv_bc * (1.0 - sig_bc))
    for part, d_part in enumerate((d_b, d_c)):
        cols = slice(part * size, (part + 1) * size)
        d_conv = d_part * d_silu[:, cols]
        d_x = conv_taps_back(
            state_ref[:, cols], d_conv, taps_bc_ref, same_ref, d_taps_bc_ref, cols
        )
        d_state_ref[:, cols] = d_x.astype(BF16)


def turned(x, cos_ref, sin_ref, sign):
    return x * cos_ref[...] + pltpu.roll(x, HEAD // 2, 1) * (sign * sin_ref[...])


def probabilities(query, key, allowed):
    scores = fast(query, key, BY_COLS) * HEAD ** (-0.5)
    scores = jnp.where(allowed, scores, MASKED)
    raised = jnp.exp(scores - jnp.max(scores, axis=1, keepdims=True))
    return raised / jnp.sum(raised, axis=1, keepdims=True)


def attend_kernel(qkv_ref, cos_ref, sin_ref, allowed_ref, low_ref, attended_ref):
    allowed = allowed_ref[...] > 0.0
    width = attended_ref.shape[1]
    for h in range(width // HEAD):
        q, k, v = (slice(i * width + h * HEAD, i * width + (h + 1) * HEAD) for i in range(3))
        query = turned(qkv_ref[:, q], cos_ref, sin_ref, 1.0).astype(BF16)
        key = turned(qkv_ref[:, k], cos_ref, sin_ref, 1.0).astype(BF16)
        value = qkv_ref[:, v].astype(BF16)
        low_ref[:, q] = query
        low_ref[:, k] = key
        low_ref[:, v] = value
        probs = probabilities(query, key, allowed)
        attended_ref[:, q] = fast(probs, value, PLAIN).astype(BF16)


def attend_back_kernel(low_ref, d_ref, cos_ref, sin_ref, allowed_ref, d_qkv_ref):
    allowed = allowed_ref[...] > 0.0
    width = d_ref.shape[1]
    for h in range(width // HEAD):
        q, k, v = (slice(i * width + h * HEAD, i * width + (h + 1) * HEAD) for i in range(3))
        query, key, value = low_ref[:, q], low_ref[:, k], low_ref[:, v]
        d_out = d_ref[:, q].astype(BF16)
        probs = probabilities(query, key, allowed)
        d_qkv_ref[:, v] = fast(probs, d_out, BY_ROWS).astype(BF16)
        d_probs = fast(d_out, value, BY_COLS)
        inner = jnp.sum(probs * d_probs, axis=1, keepdims=True)
        d_scores = (probs * (d_probs - inner) * HEAD ** (-0.5)).astype(BF16)
        d_query = fast(d_scores, key, PLAIN)
        d_key = fast(d_scores, query, BY_ROWS)
        d_qkv_ref[:, q] = turned(d_query, cos_ref, sin_ref, -1.0).astype(BF16)
        d_qkv_ref[:, k] = turned(d_key, cos_ref, sin_ref, -1.0).astype(BF16)


def in_vmem(kernel, outs, args, flops):
    size = sum(x.size * x.dtype.itemsize for x in tuple(args) + tuple(outs))
    return pl.pallas_call(
        kernel,
        out_shape=outs,
        in_specs=[pl.BlockSpec(memory_space=pltpu.VMEM)] * len(args),
        out_specs=[pl.BlockSpec(memory_space=pltpu.VMEM)] * len(outs),
        compiler_params=pltpu.CompilerParams(vmem_limit_bytes=40 * 2**20),
        cost_estimate=pl.CostEstimate(flops=flops, bytes_accessed=size, transcendentals=0),
    )(*args)


def gated_gelu(gate_up):
    half = gate_up.shape[1] // 2
    return jax.nn.gelu(gate_up[:, :half], approximate=True) * gate_up[:, half:]


def total(values):
    summed = values[0]
    for value in values[1:]:
        summed = summed + value
    return summed


def after(x, done):
    mark = done[(-1,) * done.ndim].astype(F32)
    return x + jnp.minimum(jnp.abs(mark), 0.0).astype(x.dtype)


class Links:
    def __init__(self, n_dp, n_t):
        self.n_dp = n_dp
        self.n_t = n_t
        self.chips = n_dp // 2
        self.chip_bits = self.chips.bit_length() - 1
        self.z_bits = n_t.bit_length() - 1
        d = lax.axis_index("dp")
        self.d = d
        self.core = d % 2
        self.chip = d // 2
        self.t = lax.axis_index("tensor")

    def core_swap(self, x):
        return lax.ppermute(x, "dp", [(i, i ^ 1) for i in range(self.n_dp)])

    def chip_swap(self, x, rel):
        return lax.ppermute(x, "dp", [(i, i ^ (rel << 1)) for i in range(self.n_dp)])

    def z_swap(self, x, rel):
        return lax.ppermute(x, "tensor", [(i, i ^ rel) for i in range(self.n_t)])

    def row_parts(self, rows):
        count = max(1, min(self.chip_bits, rows // 16))
        units = rows // 16
        edges = [0] + [16 * ((units * (i + 1)) // count) for i in range(count)]
        edges[-1] = rows
        return [(edges[i], edges[i + 1]) for i in range(count)]

    def chip_rs(self, terms, axis, direct=False):
        if direct:
            blocks = [
                lax.index_in_dim(terms, rel, axis, keepdims=False) for rel in range(self.chips)
            ]
            return total([block.astype(F32) for block in self.chip_a2a(blocks)])
        outs = []
        bits = self.chip_bits
        for number, (low, high) in enumerate(self.row_parts(terms.shape[axis + 1])):
            cur = lax.slice_in_dim(terms, low, high, axis=axis + 1)
            cur = cur.reshape(cur.shape[:axis] + (2,) * bits + cur.shape[axis + 1 :])
            left = list(range(bits))[::-1]
            for step in range(bits):
                bit = (number + step) % bits
                at = axis + left.index(bit)
                left.remove(bit)
                keep = lax.index_in_dim(cur, 0, at, keepdims=False)
                send = lax.index_in_dim(cur, 1, at, keepdims=False)
                got = self.chip_swap(send.astype(BF16), 1 << bit)
                cur = keep.astype(F32) + got.astype(F32)
            outs.append(cur)
        return outs[0] if len(outs) == 1 else jnp.concatenate(outs, axis=axis)

    def chip_ag(self, x, axis, direct=False):
        if direct:
            return jnp.stack(self.chip_a2a([x] * self.chips), axis=axis)
        bits = self.chip_bits
        outs = []
        for number, (low, high) in enumerate(self.row_parts(x.shape[axis])):
            blocks = {0: lax.slice_in_dim(x, low, high, axis=axis)}
            for step in range(bits):
                bit = (number + step) % bits
                for rel in list(blocks):
                    blocks[rel | (1 << bit)] = self.chip_swap(blocks[rel], 1 << bit)
            outs.append([blocks[rel] for rel in range(self.chips)])
        merged = []
        for rel in range(self.chips):
            pieces = [part[rel] for part in outs]
            merged.append(pieces[0] if len(pieces) == 1 else jnp.concatenate(pieces, axis=axis))
        return jnp.stack(merged, axis=axis)

    def chip_a2a(self, blocks):
        return [blocks[0]] + [self.chip_swap(blocks[rel], rel) for rel in range(1, self.chips)]

    def chip_sum(self, x):
        total = x
        for rel in range(1, self.chips):
            moved = jnp.stack([x[i ^ rel] for i in range(self.chips)], 0)
            total = total + self.chip_swap(moved, rel)
        return total

    def z_sum(self, x):
        return total([x] + [self.z_swap(x, rel) for rel in range(1, self.n_t)])

    def dp_sum(self, x):
        x = x + self.core_swap(x)
        return total(self.chip_a2a([x] * self.chips))

    def z_rs(self, terms, axis):
        bits = self.z_bits
        cur = terms.reshape(terms.shape[:axis] + (2,) * bits + terms.shape[axis + 1 :])
        left = list(range(bits))[::-1]
        for bit in range(bits):
            at = axis + left.index(bit)
            left.remove(bit)
            keep = lax.index_in_dim(cur, 0, at, keepdims=False)
            send = lax.index_in_dim(cur, 1, at, keepdims=False)
            got = self.z_swap(send.astype(BF16), 1 << bit)
            cur = keep.astype(F32) + got.astype(F32)
        return cur

    def z_ag(self, x, axis):
        blocks = {0: x}
        for bit in range(self.z_bits)[::-1]:
            for rel in list(blocks):
                blocks[rel | (1 << bit)] = self.z_swap(blocks[rel], 1 << bit)
        return jnp.stack([blocks[rel] for rel in range(self.n_t)], axis=axis)

    def dp_order(self, x, axis):
        split = x.reshape(x.shape[:axis] + (self.chips, 2, -1) + x.shape[axis + 1 :])
        split = self.by_index(self.by_index(split, axis + 1, self.core), axis, self.chip)
        return split.reshape(x.shape)

    def by_index(self, x, axis, own):
        count = x.shape[axis]
        return jnp.concatenate(
            [lax.dynamic_slice_in_dim(x, own ^ i, 1, axis=axis) for i in range(count)], axis=axis
        )

    def rows_by_t(self, x):
        rows = x.shape[0]
        split = x.reshape((self.n_t, rows // self.n_t) + x.shape[1:])
        return self.by_index(split, 0, self.t).reshape(x.shape)


def core_pair(links, x, axis):
    return jnp.concatenate([x, links.core_swap(x)], axis=axis)


def core_rs(links, x, axis):
    half = x.shape[axis] // 2
    own = lax.slice_in_dim(x, 0, half, axis=axis)
    other = lax.slice_in_dim(x, half, 2 * half, axis=axis)
    return own + links.core_swap(other.astype(BF16)).astype(F32)


def dotf(spec, a, b):
    return jnp.einsum(spec, a, b, preferred_element_type=F32)


def dotl(spec, a, b):
    return jnp.einsum(spec, a, b, preferred_element_type=F32).astype(BF16)


def flip(index, bit):
    return index + (1 - 2 * ((index // bit) % 2)) * bit


def chip_partner(rel):
    d = lax.axis_index("dp")
    for bit in (1, 2):
        if rel & bit:
            d = flip(d, 2 * bit)
    return {"dp": d}


def z_partner(rel):
    t = lax.axis_index("tensor")
    for bit in (1, 2):
        if rel & bit:
            t = flip(t, bit)
    return {"tensor": t}


def core_partner():
    return {"dp": flip(lax.axis_index("dp"), 1)}


def partner_of(axis, rel):
    if axis == "core":
        return core_partner()
    return chip_partner(rel) if axis == "dp" else z_partner(rel)


def xor(a, b):
    return sum(((a // bit + b // bit) % 2) * bit for bit in (1, 2))


def core_order(x):
    half = x.shape[-1] // 2
    turned = jnp.concatenate([x[..., half:], x[..., :half]], axis=-1)
    return jnp.where(lax.axis_index("dp") % 2 == 1, turned, x)


class Wire:
    def __init__(self, send, recv):
        self.send, self.recv, self.used = send, recv, 0

    def start(self, src, dst, partner):
        i = self.used
        self.used += 1
        copy = pltpu.make_async_remote_copy(
            src_ref=src,
            dst_ref=dst,
            send_sem=self.send.at[i],
            recv_sem=self.recv.at[i],
            device_id=partner,
            device_id_type=pl.DeviceIdType.MESH,
        )
        copy.start()
        return copy


TILE = 256


def over_tiles(width, body, *offsets):
    offsets = (0,) + (offsets or (0,))

    def step(i, carry):
        starts = [pl.multiple_of(offset + i * TILE, 128) for offset in offsets]
        body(*[pl.ds(start, TILE) for start in starts])
        return carry

    count = width // TILE
    lax.fori_loop(0, count, step, 0)
    if width % TILE:
        body(*[pl.ds(offset + count * TILE, width % TILE) for offset in offsets])


class RowPair:
    def __init__(self, own, other):
        self.args = (own, other)
        self.parts = own.shape[0] if own.ndim == 3 else 1
        self.half, self.cols = own.shape[-2:]
        self.shape = (2 * self.half, self.parts * self.cols)

    def whole(self):
        both = jnp.concatenate(self.args, axis=-2)
        return both if both.ndim == 2 else jnp.concatenate(list(both), axis=1)

    def pick(self, ref, part):
        return ref if self.parts == 1 else ref.at[part]

    def chunks(self, by_cols):
        if by_cols:
            return [(0, self.half), (self.half, self.half)]
        if self.parts > 1:
            return [(i * self.cols, self.cols) for i in range(self.parts)]
        low = self.cols // 2 // TILE * TILE
        return [(0, low), (low, self.cols - low)]

    def times(self, x, refs, by_cols, store, chunk):
        half, cols = self.half, self.cols
        start, width = self.chunks(by_cols)[chunk]
        if by_cols:
            ref = refs[chunk]

            def body(at, to):
                terms = [
                    fast(x(slice(i * cols, i * cols + cols)), self.pick(ref, i)[at, :], BY_COLS)
                    for i in range(self.parts)
                ]
                store(to, total(terms))

            over_tiles(width, body, start)
            return
        part, low = (chunk, 0) if self.parts > 1 else (0, start)

        def body(_, at, to):
            own, other = (self.pick(ref, part)[:, at] for ref in refs)
            left, right = x(slice(0, half)), x(slice(half, 2 * half))
            store(to, fast(left, own, PLAIN) + fast(right, other, PLAIN))

        over_tiles(width, body, low, start)


class ColPair:
    def __init__(self, own, other):
        self.args = (own, other)
        self.rows, self.half = own.shape
        self.shape = (self.rows, 2 * self.half)

    def whole(self):
        return jnp.concatenate(self.args, axis=1)

    def chunks(self, by_cols):
        width = self.rows // 2 if by_cols else self.half
        return [(0, width), (width, width)]

    def times(self, x, refs, by_cols, store, chunk):
        half = self.half
        start, width = self.chunks(by_cols)[chunk]
        if by_cols:
            own, other = refs

            def body(_, at):
                left, right = x(slice(0, half)), x(slice(half, 2 * half))
                store(at, fast(left, own[at, :], BY_COLS) + fast(right, other[at, :], BY_COLS))

            over_tiles(width, body, start)
            return
        ref = refs[chunk]

        def body(at, to):
            store(to, fast(x(slice(0, self.rows)), ref[:, at], PLAIN))

        over_tiles(width, body, start)


class ByChips:
    partners = [("dp", 1), ("dp", 2)]

    def __init__(self, x, w, by_cols, out_width, local, args, outs, scratch=()):
        self.by_cols, self.local, self.count = by_cols, local, len(args)
        self.rows = x.shape[1]
        self.width = w.shape[0] if by_cols else w.shape[1]
        self.w = w
        self.args = (x,) + w.args + tuple(args)
        self.outs = (jax.ShapeDtypeStruct((4, self.rows, out_width), BF16),) + tuple(outs)
        self.chunks = w.chunks(by_cols)
        self.copies = 6 * len(self.chunks) + 12
        self.scratch = chip_scratch(self.rows, self.width)
        self.scratch += [pltpu.VMEM((self.rows, self.width), F32)] + list(scratch)
        self.flops = 8 * self.rows * x.shape[2] * self.width

    def run(self, wire, args, outs, scratch):
        x, w = args[0], args[1:3]
        part, first, second, summed = scratch[:4]
        gathered = outs[0]
        rows = self.rows

        def dot(low, high, chunk):
            def left(at):
                return x[low:high, :, at].reshape((high - low) * rows, at.stop - at.start)

            def store(to, value):
                part[low:high, :, to] = value.astype(BF16).reshape(high - low, rows, value.shape[1])

            self.w.times(left, w, self.by_cols, store, chunk)

        yield from chip_sum(wire, part, first, second, summed, self.chunks, dot)
        self.local(summed, gathered.at[0], args[3:], outs[1:], scratch[4:])
        yield from chip_gather(wire, gathered)


def pieces(rows):
    half = rows // 2
    return [(p, slice(p * half, (p + 1) * half), 1 << p, 1 << (1 - p)) for p in range(2)]


def chip_sum(wire, part, first, second, summed, chunks, dot):
    halves = pieces(summed.shape[0])
    sent, later = {}, {}
    for n, (start, width) in enumerate(chunks):
        cols = slice(start, start + width)
        dot(1, 4, n)
        for p, at, bit, _ in halves:
            for i, rel in ((1, 3), (0, bit)):
                src, dst = part.at[rel, at, cols], first.at[p, i, :, cols]
                sent[n, p, i] = wire.start(src, dst, chip_partner(bit))
        yield
    for n in range(len(chunks)):
        dot(0, 1, n)
    for n, (start, width) in enumerate(chunks):
        cols = slice(start, start + width)
        for p, at, _, other in halves:
            sent[n, p, 1].wait_recv()

            def add(_, cols, p=p, at=at, other=other):
                both = part[other, at, cols].astype(F32) + first[p, 1, :, cols].astype(F32)
                part[other, at, cols] = both.astype(BF16)

            over_tiles(width, add, start)
            src, dst = part.at[other, at, cols], second.at[p, :, cols]
            later[n, p] = wire.start(src, dst, chip_partner(other))
        yield
    for n, (start, width) in enumerate(chunks):
        for p, at, _, _ in halves:
            sent[n, p, 0].wait_recv()
            later[n, p].wait_recv()

            def finish(_, cols, p=p, at=at):
                both = part[0, at, cols].astype(F32) + first[p, 0, :, cols].astype(F32)
                summed[at, cols] = both + second[p, :, cols].astype(F32)

            over_tiles(width, finish, start)
    for copy in list(sent.values()) + list(later.values()):
        copy.wait_send()


def chip_gather(wire, out):
    _, rows, width = out.shape
    low = width // 2 // 128 * 128
    ranges = [slice(0, low), slice(low, width)]
    near, far, last = {}, [], []
    for n, cols in enumerate(ranges):
        for p, at, bit, other in pieces(rows):
            src = out.at[0, at, cols]
            near[n, p] = wire.start(src, out.at[bit, at, cols], chip_partner(bit))
            far.append(wire.start(src, out.at[other, at, cols], chip_partner(other)))
    yield
    for n, cols in enumerate(ranges):
        for p, at, bit, other in pieces(rows):
            near[n, p].wait_recv()
            src, dst = out.at[bit, at, cols], out.at[3, at, cols]
            last.append(wire.start(src, dst, chip_partner(other)))
        yield
    for copy in far + last:
        copy.wait_recv()
    for copy in list(near.values()) + far + last:
        copy.wait_send()


def chip_scratch(rows, width):
    half = rows // 2
    return [
        pltpu.VMEM((4, rows, width), BF16),
        pltpu.VMEM((2, 2, half, width), BF16),
        pltpu.VMEM((2, half, width), BF16),
    ]


def tensor_sum(weight, x, w, by_cols, wire, scratch):
    part, first, second, summed = scratch
    rows, width = summed.shape
    r = rows // 4

    def left(at):
        return x[:, :, at].reshape(4 * rows, at.stop - at.start)

    def store(to, value):
        low = value.astype(BF16)
        for c in range(4):
            for z in range(4):
                part[z, c * r : (c + 1) * r, to] = low[c * rows + z * r : c * rows + z * r + r]

    half = width // 2
    halves = [slice(h * half, (h + 1) * half) for h in range(2)]
    sent, later = [], []
    for n, h in enumerate(halves):
        weight.times(left, w, by_cols, store, n)
        for i, z in ((1, 3), (0, 1)):
            sent.append(wire.start(part.at[z, :, h], first.at[i, :, h], z_partner(1)))
        yield
    for n, h in enumerate(halves):
        sent[2 * n].wait_recv()

        def add(_, cols):
            both = part[2, :, cols].astype(F32) + first[1, :, cols].astype(F32)
            part[2, :, cols] = both.astype(BF16)

        over_tiles(half, add, n * half)
        later.append(wire.start(part.at[2, :, h], second.at[:, h], z_partner(2)))
        yield
    for n in range(2):
        sent[2 * n + 1].wait_recv()
        later[n].wait_recv()

        def finish(_, cols):
            both = part[0, :, cols].astype(F32) + first[0, :, cols].astype(F32)
            summed[:, cols] = both + second[:, cols].astype(F32)

        over_tiles(half, finish, n * half)
    for copy in sent + later:
        copy.wait_send()


def sum_scratch(rows, width):
    return [
        pltpu.VMEM((4, rows, width), BF16),
        pltpu.VMEM((2, rows, width), BF16),
        pltpu.VMEM((rows, width), BF16),
        pltpu.VMEM((rows, width), F32),
    ]


def true_slots(ref):
    t = lax.axis_index("tensor")
    own = [ref.at[xor(t, rel)] for rel in range(4)]
    return own, [None, own[0], own[0], own[2]]


def tensor_gather(wire, slots, there=None):
    there = there or slots
    far = wire.start(slots[0], there[2], z_partner(2))
    near = wire.start(slots[0], there[1], z_partner(1))
    yield
    far.wait_recv()
    last = wire.start(slots[2], there[3], z_partner(1))
    yield
    near.wait_recv()
    last.wait_recv()
    for copy in (far, near, last):
        copy.wait_send()


class ByTensor:
    copies = 9
    partners = [("tensor", 1), ("tensor", 2), ("dp", 1), ("dp", 2), ("dp", 3)]

    def __init__(self, x, w, by_cols, local, args, outs, gather=True):
        self.by_cols, self.local, self.gather = by_cols, local, gather
        self.rows = x.shape[1]
        self.width = w.shape[0] if by_cols else w.shape[1]
        self.w = w
        self.args = (x,) + w.args + tuple(args)
        shape = (4, 4, self.rows // 4, self.width)
        self.outs = (jax.ShapeDtypeStruct(shape, BF16),) if gather else ()
        self.outs += tuple(outs)
        self.copies = 12 if gather else 9
        self.scratch = sum_scratch(self.rows, self.width)
        self.scratch += [pltpu.VMEM((4, self.rows, 128), F32)]
        self.flops = 8 * self.rows * x.shape[2] * self.width

    def run(self, wire, args, outs, scratch):
        summed, stats = scratch[3:5]
        rows = self.rows
        r = rows // 4
        yield from tensor_sum(self.w, args[0], args[1:3], self.by_cols, wire, scratch[:4])
        rest = outs[1:] if self.gather else outs[:1]
        local = self.local(summed, args[3:7], rest)
        stats[0] = jnp.broadcast_to(next(local), (rows, 128))
        sums = [
            wire.start(stats.at[0], stats.at[rel], chip_partner(rel)) for rel in range(1, 4)
        ]
        yield
        total_sums = stats[0]
        for rel in range(1, 4):
            sums[rel - 1].wait_recv()
            moved = [stats[rel, (i ^ rel) * r : (i ^ rel) * r + r, :] for i in range(4)]
            total_sums = total_sums + jnp.concatenate(moved, axis=0)
        low = local.send(total_sums[:, 0:1])
        if self.gather:
            gathered = outs[0]
            for c in range(4):
                gathered[c, 0] = low[c * r : (c + 1) * r]
            far = wire.start(gathered.at[:, 0], gathered.at[:, 2], z_partner(2))
            near = wire.start(gathered.at[:, 0], gathered.at[:, 1], z_partner(1))
            yield
            far.wait_recv()
            last = wire.start(gathered.at[:, 2], gathered.at[:, 3], z_partner(1))
            yield
            near.wait_recv()
            last.wait_recv()
            sums += [far, near, last]
        else:
            yield from self.tail(wire, low, args, outs, scratch)
        for copy in sums:
            copy.wait_send()


class Leave(ByTensor):
    def __init__(self, x, w, local, args, d_gain, theirs):
        super().__init__(x, w, True, local, args, (d_gain,), gather=False)
        r = self.rows // 4
        self.args += (theirs,)
        self.outs += (jax.ShapeDtypeStruct((4, r, 4 * self.width), BF16),)
        self.copies = 15
        self.scratch += [pltpu.VMEM((4, r, self.width), BF16)] * 2
        self.scratch += [pltpu.VMEM((r, 4 * self.width), BF16)]

    def tail(self, wire, low, args, outs, scratch):
        theirs, out = args[-1], outs[-1]
        mine, came, block_ref = scratch[5:]
        r, width = self.rows // 4, self.width
        half = width // 2
        d, t = lax.axis_index("dp"), lax.axis_index("tensor")
        for c in range(4):
            mine[c] = low[c * r : (c + 1) * r]
        sent = [
            wire.start(mine.at[rel], came.at[rel], chip_partner(rel)) for rel in range(1, 4)
        ]
        yield
        for rel in range(4):
            if rel:
                sent[rel - 1].wait_recv()
            block = (came if rel else mine)[rel].astype(F32)
            for j in range(2):
                at = 2 * xor(d // 2, rel) + (d + j) % 2
                at = pl.ds(pl.multiple_of(at * half, 128), half)
                low = block[:, j * half : (j + 1) * half] + theirs[:, at]
                block_ref[:, at] = low.astype(BF16)
        out[t] = block_ref[...]
        yield from tensor_gather(wire, *true_slots(out))
        for copy in sent:
            copy.wait_send()


class FeedOut:
    partners = [("tensor", 1), ("tensor", 2), ("dp", 1), ("dp", 2), ("dp", 3)]
    copies = 12

    def __init__(self, x, w, mid, proj):
        self.w = w
        self.rows, self.width = x.shape[1], w.shape[1]
        self.cols = proj.shape[3]
        r = self.rows // 4
        self.args = (x,) + w.args + (mid, proj)
        wide = 8 * self.cols
        self.outs = (
            jax.ShapeDtypeStruct((self.rows, self.width), BF16),
            jax.ShapeDtypeStruct((4, r, wide), BF16),
            jax.ShapeDtypeStruct((r, wide), BF16),
        )
        self.scratch = sum_scratch(self.rows, self.width)
        self.scratch += [pltpu.VMEM((4, r, wide), BF16)] * 2
        self.flops = 8 * self.rows * x.shape[2] * self.width

    def run(self, wire, args, outs, scratch):
        mid, proj = args[3:]
        block, gathered, own = outs
        summed, part, came = scratch[3:]
        r = self.rows // 4
        d = lax.axis_index("dp")
        yield from tensor_sum(self.w, args[0], args[1:3], False, wire, scratch[:4])
        block[...] = core_order((mid[...] + summed[...]).astype(BF16))
        for x in range(4):
            for y in range(2):
                at = 2 * xor(d // 2, x) + (d + y) % 2
                at = pl.ds(pl.multiple_of(at * self.cols, 128), self.cols)
                value = fast(block[...], proj[x, y], PLAIN).astype(BF16)
                part[:, :, at] = value.reshape(4, r, self.cols)
        sent = [
            wire.start(part.at[rel], came.at[rel], chip_partner(rel)) for rel in range(1, 4)
        ]
        yield
        shared = part[0].astype(F32)
        for rel in range(1, 4):
            sent[rel - 1].wait_recv()
            shared = shared + came[rel].astype(F32)
        own[...] = shared.astype(BF16)
        gathered[lax.axis_index("tensor")] = own[...]
        yield from tensor_gather(wire, *true_slots(gathered))
        for copy in sent:
            copy.wait_send()


class Settle:
    partners = [("tensor", 1), ("tensor", 2), ("dp", 1), ("dp", 2), ("dp", 3)]
    copies = 9

    def __init__(self, terms, bc, mamba_in, gain, grad, proj):
        self.args = (terms, bc, mamba_in, gain, grad, proj)
        r, wide = mamba_in.shape
        self.r, self.wide, self.cols = r, wide, proj.shape[3]
        states, width = terms.shape[2] - wide, proj.shape[2]
        self.outs = (
            jax.ShapeDtypeStruct((4, 4, r, width), BF16),
            jax.ShapeDtypeStruct((4, r, wide), BF16),
            jax.ShapeDtypeStruct((r, wide), F32),
            jax.ShapeDtypeStruct((r, states), BF16),
            jax.ShapeDtypeStruct((4 * r, width), F32),
            jax.ShapeDtypeStruct((1, wide), F32),
        )
        self.scratch = [
            pltpu.VMEM((2, r, terms.shape[2]), BF16),
            pltpu.VMEM((r, terms.shape[2]), BF16),
            pltpu.VMEM((r, terms.shape[2]), BF16),
        ]
        self.flops = 16 * r * wide * width

    def run(self, wire, args, outs, scratch):
        terms, bc, mamba_in, gain, grad, proj = args
        gathered, shared, d_mamba, state, d_block, d_gain = outs
        first, middle, second = scratch
        wide = self.wide
        d = lax.axis_index("dp")
        sent = [wire.start(terms.at[z], first.at[i], z_partner(1)) for i, z in enumerate((1, 3))]
        yield
        sent[1].wait_recv()
        middle[...] = (terms[2].astype(F32) + first[1].astype(F32)).astype(BF16)
        sent.append(wire.start(middle, second, z_partner(2)))
        yield
        sent[0].wait_recv()
        sent[2].wait_recv()
        summed = terms[0].astype(F32) + first[0].astype(F32) + second[...].astype(F32)
        state[...] = summed[:, wide:].astype(BF16)
        dy = summed[:, :wide] + fast(state[...], bc[...], BY_COLS)
        v = mamba_in[...]
        inv = lax.rsqrt(jnp.mean(v * v, axis=1, keepdims=True) + EPSILON)
        scaled = dy * gain[...]
        inner = jnp.mean(scaled * v, axis=1, keepdims=True)
        d_gain[...] = jnp.sum(dy * v * inv, axis=0, keepdims=True)
        d_mamba[...] = inv * scaled - v * (inv * inv * inv * inner) + grad[...].astype(F32)
        shared[0] = d_mamba[...].astype(BF16)
        more = [
            wire.start(shared.at[0], shared.at[rel], chip_partner(rel)) for rel in range(1, 4)
        ]
        yield
        for copy in more:
            copy.wait_recv()
        result = None
        for x in range(4):
            for y in range(2):
                at = 2 * xor(d // 2, x) + (d + y) % 2
                at = pl.ds(pl.multiple_of(at * self.cols, 128), self.cols)
                left = shared[:, :, at].reshape(4 * self.r, self.cols)
                value = fast(left, proj[x, y], BY_COLS)
                result = value if result is None else result + value
        d_block[...] = core_order(result)
        for c in range(4):
            gathered[c, 0] = d_block[c * self.r : (c + 1) * self.r].astype(BF16)
        yield from tensor_gather(wire, [gathered.at[:, i] for i in range(4)])
        for copy in sent + more:
            copy.wait_send()


class Spread:
    every = 2

    partners = [("tensor", 1), ("tensor", 2), ("dp", 1), ("dp", 2), ("dp", 3), ("core", 1)]
    copies = 7
    flops = 0

    def __init__(self, w):
        self.args = (w,)
        self.outs = (jax.ShapeDtypeStruct((4, 2) + w.shape, BF16),)
        self.scratch = [pltpu.VMEM((4,) + w.shape, BF16)]

    def run(self, wire, args, outs, scratch):
        (out,), (rows,) = outs, scratch
        rows[0] = args[0][...]
        yield from tensor_gather(wire, [rows.at[i] for i in range(4)])
        here = xor(lax.axis_index("dp") // 2, lax.axis_index("tensor"))
        sent = [
            wire.start(rows.at[xor(here, rel)], out.at[rel, 0], chip_partner(rel))
            for rel in range(1, 4)
        ]
        out[0, 0] = rows[here]
        yield
        for copy in sent:
            copy.wait_recv()
        sent.append(wire.start(out.at[:, 0], out.at[:, 1], core_partner()))
        yield
        sent[3].wait_recv()
        for copy in sent:
            copy.wait_send()


class Collect:
    every = 2

    partners = Spread.partners
    copies = 7
    flops = 0

    def __init__(self, own, other):
        self.args = (own, other)
        shape = own.shape[1:]
        self.outs = (jax.ShapeDtypeStruct(shape, F32),)
        self.scratch = [pltpu.VMEM((4,) + shape, BF16)] * 3
        self.scratch += [pltpu.VMEM((2,) + shape, BF16), pltpu.VMEM(shape, BF16)]

    def run(self, wire, args, outs, scratch):
        own, other = args
        (out,) = outs
        swapped, mine, came, first, second = scratch
        rows = own.shape[1]
        tile = 128
        sent = [wire.start(other, swapped, core_partner())]
        yield
        sent[0].wait_recv()
        for rel in range(4):

            def add(i, carry, rel=rel):
                at = pl.ds(pl.multiple_of(i * tile, tile), tile)
                both = own[rel, at, :] + swapped[rel, at, :].astype(F32)
                (mine if rel else came)[rel, at, :] = both.astype(BF16)
                return carry

            lax.fori_loop(0, rows // tile, add, 0)
            if rel:
                sent.append(wire.start(mine.at[rel], came.at[rel], chip_partner(rel)))
        yield
        for copy in sent[1:]:
            copy.wait_recv()
        here = xor(lax.axis_index("dp") // 2, lax.axis_index("tensor"))
        at = [xor(here, z) for z in range(4)]
        more = [wire.start(came.at[at[z]], first.at[i], z_partner(1)) for i, z in enumerate((1, 3))]
        yield
        more[1].wait_recv()

        def middle(i, carry):
            to = pl.ds(pl.multiple_of(i * tile, tile), tile)
            both = came[at[2], to, :].astype(F32) + first[1, to, :].astype(F32)
            swapped[0, to, :] = both.astype(BF16)
            return carry

        lax.fori_loop(0, rows // tile, middle, 0)
        more.append(wire.start(swapped.at[0], second, z_partner(2)))
        yield
        more[0].wait_recv()
        more[2].wait_recv()

        def finish(i, carry):
            to = pl.ds(pl.multiple_of(i * tile, tile), tile)
            both = came[at[0], to, :].astype(F32) + first[0, to, :].astype(F32)
            out[to, :] = both + second[to, :].astype(F32)
            return carry

        lax.fori_loop(0, rows // tile, finish, 0)
        for copy in sent + more:
            copy.wait_send()


class Outputs:
    partners = [("tensor", 1), ("tensor", 2)]
    copies = 6
    flops = 0

    def __init__(self, terms, base, valid):
        self.args = (terms, base, valid)
        self.outs = (jax.ShapeDtypeStruct(terms.shape, BF16),)
        shape = terms.shape[1:]
        self.scratch = [pltpu.VMEM((2,) + shape, BF16), pltpu.VMEM(shape, BF16)]
        self.scratch += [pltpu.VMEM(shape, BF16)]

    def run(self, wire, args, outs, scratch):
        terms, base, valid = args
        (gathered,) = outs
        first, middle, second = scratch
        sent = [wire.start(terms.at[z], first.at[i], z_partner(1)) for i, z in enumerate((1, 3))]
        yield
        sent[1].wait_recv()
        middle[...] = (terms[2].astype(F32) + first[1].astype(F32)).astype(BF16)
        sent.append(wire.start(middle, second, z_partner(2)))
        yield
        sent[0].wait_recv()
        sent[2].wait_recv()
        summed = terms[0].astype(F32) + first[0].astype(F32) + second[...].astype(F32)
        gathered[lax.axis_index("tensor")] = ((base[...] + summed) * valid[...]).astype(BF16)
        yield from tensor_gather(wire, *true_slots(gathered))
        for copy in sent:
            copy.wait_send()


class SmallSum:
    partners = [("tensor", 1), ("tensor", 2), ("tensor", 3)]
    partners += [("dp", 1), ("dp", 2), ("dp", 3), ("core", 1)]
    copies = 7
    flops = 0

    def __init__(self, x, rows_all):
        self.args, self.rows_all = (x,), rows_all
        self.outs = (jax.ShapeDtypeStruct(x.shape, F32),)
        self.scratch = [pltpu.VMEM(x.shape, F32)] * 3
        self.scratch += [pltpu.VMEM((3,) + x.shape, F32), pltpu.VMEM((3, rows_all, 128), F32)]

    def run(self, wire, args, outs, scratch):
        (x,), (out,) = args, outs
        from_core, mine, whole, from_chips, from_z = scratch
        top = slice(0, self.rows_all)
        swap = wire.start(x, from_core, core_partner())
        yield
        swap.wait_recv()
        mine[...] = x[...] + from_core[...]
        sent = [
            wire.start(mine, from_chips.at[rel - 1], chip_partner(rel)) for rel in range(1, 4)
        ]
        yield
        for copy in sent:
            copy.wait_recv()
        whole[...] = total([mine[...]] + [from_chips[i] for i in range(3)])
        more = [
            wire.start(whole.at[top], from_z.at[rel - 1], z_partner(rel)) for rel in range(1, 4)
        ]
        yield
        for copy in more:
            copy.wait_recv()
        out[...] = whole[...]
        out[top] = total([whole[top]] + [from_z[i] for i in range(3)])
        for copy in [swap] + sent + more:
            copy.wait_send()


class Enter:
    partners = [("dp", 1), ("dp", 2), ("dp", 3)]
    copies = 9
    flops = 0

    def __init__(self, hid, emb, gain):
        self.args = (hid, emb, gain)
        self.rows, self.half = hid.shape[0], gain.shape[1] // 2
        rows, width = self.rows, gain.shape[1]
        self.outs = (
            jax.ShapeDtypeStruct((4, rows, width), BF16),
            jax.ShapeDtypeStruct((rows, width), F32),
            jax.ShapeDtypeStruct((rows, 1), F32),
        )
        self.scratch = [
            pltpu.VMEM((rows, 4 * width), BF16),
            pltpu.VMEM((4, rows, width), BF16),
            pltpu.VMEM((4, rows, 128), F32),
        ]

    def run(self, wire, args, outs, scratch):
        hid, emb, gain = args
        attn_in, joined_z, inv_z = outs
        joined, came, stats = scratch
        rows, half = self.rows, self.half
        r, wide = rows // 4, hid.shape[1]
        d, t = lax.axis_index("dp"), lax.axis_index("tensor")
        for i in range(4):
            at = pl.ds(pl.multiple_of(xor(t, i) * r, r), r)
            to = slice(i * r, (i + 1) * r)
            left, right = hid[at, :], emb[at, :]
            joined[to, :wide] = left
            joined[to, wide:] = right
            left, right = left.astype(F32), right.astype(F32)
            squares = jnp.sum(left * left, axis=1, keepdims=True)
            squares = squares + jnp.sum(right * right, axis=1, keepdims=True)
            inverse = lax.rsqrt(squares / (2 * wide) + EPSILON)
            stats[0, to, :] = jnp.broadcast_to(inverse, (r, 128))
        sent = []
        for rel in (3, 1, 2):
            sent.append(wire.start(stats.at[0], stats.at[rel], chip_partner(rel)))
        for rel in (3, 1, 2, 0):
            for j in range(2):
                at = 2 * xor(d // 2, rel) + (d + j) % 2
                at = pl.ds(pl.multiple_of(at * half, 128), half)
                to = slice(j * half, (j + 1) * half)
                if rel:
                    src, dst = joined.at[:, at], came.at[rel, :, to]
                    sent.append(wire.start(src, dst, chip_partner(rel)))
                else:
                    came[0, :, to] = joined[:, at]
        yield
        for copy in sent:
            copy.wait_recv()
        for c in range(4):
            block = came[c].astype(F32)
            inverse = stats[c][:, 0:1]
            attn_in[c] = (block * inverse * gain[...]).astype(BF16)
            joined_z[c * r : (c + 1) * r] = block[:r]
            inv_z[c * r : (c + 1) * r] = inverse[:r]
        for copy in sent:
            copy.wait_send()


class WeightGrad:
    partners = [("core", 1)]
    copies = 1

    def __init__(self, a, b, by_rows, parts=1):
        self.count, self.by_rows, self.parts = len(a), by_rows, parts
        self.args = tuple(a) + tuple(b)
        self.height, self.width = a[0].shape[2], b[0].shape[2]
        if by_rows:
            self.height //= 2
        else:
            self.width //= 2
        self.cols = self.width // parts
        shape = (self.height, self.cols)
        shape = (parts,) + shape if parts > 1 else shape
        self.outs = (jax.ShapeDtypeStruct(shape, F32),)
        self.step = min(self.height, 512)
        self.scratch = [pltpu.VMEM(shape, BF16)] * 2
        self.scratch += [pltpu.VMEM((self.count, self.step, 4 * a[0].shape[1]), BF16)]
        self.flops = 4 * self.count * a[0].shape[1] * self.height * self.width * 2

    def run(self, wire, args, outs, scratch):
        (out,) = outs
        other, got, turned = scratch
        a, b = args[: self.count], args[self.count :]
        step = self.step
        tokens = 4 * a[0].shape[1]

        def work(half, ref):
            row, col = (half * self.height, 0) if self.by_rows else (0, half * self.width)
            for low in range(0, self.height, step):
                rows = slice(row + low, row + low + step)
                for i, x in enumerate(a):
                    turned[i] = x[:, :, rows].reshape(tokens, step).T
                for part in range(self.parts):
                    to_ref = ref if self.parts == 1 else ref.at[part]

                    def body(to, at, low=low, to_ref=to_ref):
                        terms = [
                            fast(turned[i], y[:, :, at].reshape(tokens, at.size), PLAIN)
                            for i, y in enumerate(b)
                        ]
                        to_ref[low : low + step, to] = total(terms).astype(to_ref.dtype)

                    over_tiles(self.cols, body, col + part * self.cols)
                    yield

        yield
        yield from work(1, other)
        swap = wire.start(other, got, core_partner())
        yield from work(0, out)
        swap.wait_recv()
        for part in range(self.parts):
            to_ref, got_ref = (out, got) if self.parts == 1 else (out.at[part], got.at[part])

            def add(cols, _, to_ref=to_ref, got_ref=got_ref):
                to_ref[:, cols] += got_ref[:, cols].astype(F32)

            over_tiles(self.cols, add)
        swap.wait_send()


def together(groups, collective_id):
    partners = sorted({p for g in groups for p in g.partners})

    def kernel(*refs):
        refs = list(refs)

        def take(count):
            got = refs[:count]
            del refs[:count]
            return got

        args = [take(len(g.args)) for g in groups]
        outs = [take(len(g.outs)) for g in groups]
        scratch = [take(len(g.scratch)) for g in groups]
        wires = [Wire(*take(2)) for g in groups]
        barrier = pltpu.get_barrier_semaphore()
        for axis, rel in partners:
            pl.semaphore_signal(
                barrier,
                inc=1,
                device_id=partner_of(axis, rel),
                device_id_type=pl.DeviceIdType.MESH,
            )
        pl.semaphore_wait(barrier, len(partners))
        running = [
            (g, g.run(wire, a, o, s))
            for g, wire, a, o, s in zip(groups, wires, args, outs, scratch)
        ]
        turn = 0
        while running:
            left = []
            slow_alone = all(getattr(g, "every", 1) > 1 for g, _ in running)
            for g, run in running:
                waits = turn % getattr(g, "every", 1) and not slow_alone
                if waits or next(run, running) is not running:
                    left.append((g, run))
            running = left
            turn += 1

    args = [x for g in groups for x in g.args]
    outs = [x for g in groups for x in g.outs]
    scratch = [x for g in groups for x in g.scratch]
    for g in groups:
        scratch += [pltpu.SemaphoreType.DMA((g.copies,))] * 2
    size = sum(x.size * x.dtype.itemsize for x in args + outs)
    flat = pl.pallas_call(
        kernel,
        out_shape=outs,
        in_specs=[pl.BlockSpec(memory_space=pltpu.VMEM)] * len(args),
        out_specs=[pl.BlockSpec(memory_space=pltpu.VMEM)] * len(outs),
        scratch_shapes=scratch,
        compiler_params=pltpu.CompilerParams(
            collective_id=collective_id, has_side_effects=True, vmem_limit_bytes=62 * 2**20
        ),
        cost_estimate=pl.CostEstimate(
            flops=sum(g.flops for g in groups), bytes_accessed=size, transcendentals=0
        ),
    )(*args)
    results = []
    for g in groups:
        results.append(flat[: len(g.outs)])
        flat = flat[len(g.outs) :]
    return results


def attend_local(qkv, slot, args, outs, scratch):
    cos, sin, allowed = args
    attend_kernel(qkv, cos, sin, allowed, outs[0], slot)


def attend_back_local(d_attended, slot, args, outs, scratch):
    low, cos, sin, allowed = args
    attend_back_kernel(low, d_attended, cos, sin, allowed, slot)


GELU_SCALE = (2.0 / 3.141592653589793) ** 0.5


def feed_local(summed, slot, args, outs, scratch):
    (up,) = args
    gate_up, adapter = outs
    units = slot.shape[1]
    low = summed[:, 2 * units :].astype(BF16)
    adapter[...] = low

    def widen(cols, _):
        gate_up[:, cols] = summed[:, cols] + fast(low, up[:, cols], PLAIN)

    over_tiles(2 * units, widen)
    tile = 256

    def act(i, carry):
        at = pl.ds(pl.multiple_of(i * tile, 128), tile)
        also = pl.ds(pl.multiple_of(units + i * tile, 128), tile)
        v = gate_up[:, at]
        bent = jnp.tanh(GELU_SCALE * (v + 0.044715 * (v * v * v)))
        slot[:, at] = (0.5 * v * (1.0 + bent) * gate_up[:, also]).astype(BF16)
        return carry

    lax.fori_loop(0, units // tile, act, 0)


def feed_back_local(d_hidden, slot, args, outs, scratch):
    gate_up, up = args
    (adapter,) = scratch
    units = d_hidden.shape[1]
    tile = 256
    adapter[...] = jnp.zeros(adapter.shape, F32)

    def act(i, carry):
        at = pl.ds(pl.multiple_of(i * tile, 128), tile)
        also = pl.ds(pl.multiple_of(units + i * tile, 128), tile)
        v, u, d = gate_up[:, at], gate_up[:, also], d_hidden[:, at]
        bent = jnp.tanh(GELU_SCALE * (v + 0.044715 * (v * v * v)))
        slope = 0.5 * (1.0 + bent) + 0.5 * v * (1.0 - bent * bent) * GELU_SCALE * (
            1.0 + 3.0 * 0.044715 * (v * v)
        )
        d_gate = (d * u * slope).astype(BF16)
        d_up = (d * (0.5 * v * (1.0 + bent))).astype(BF16)
        slot[:, at] = d_gate
        slot[:, also] = d_up
        adapter[...] += fast(d_gate, up[:, at], BY_COLS) + fast(d_up, up[:, also], BY_COLS)
        return carry

    lax.fori_loop(0, units // tile, act, 0)
    slot[:, 2 * units :] = adapter[...].astype(BF16)


def norm_local(width, summed, args, outs):
    base, gain = args
    mid, inverse = outs
    value = base[...] + summed[...]
    mid[...] = value
    squares = yield jnp.sum(value * value, axis=1, keepdims=True)
    inv = lax.rsqrt(squares / width + EPSILON)
    inverse[...] = inv
    yield (value * inv * gain[...]).astype(BF16)


def norm_back_local(width, summed, args, outs):
    value, inverse, gain, skip = args
    d_gain = outs[-1]
    dy = summed[...]
    scaled = dy * gain[...]
    v, inv = value[...], inverse[...]
    weighted = yield jnp.sum(scaled * v, axis=1, keepdims=True)
    d_gain[...] = jnp.sum(dy * v * inv, axis=0, keepdims=True)
    result = scaled * inv - v * (inv * inv * inv * weighted / width) + skip[...]
    if len(outs) == 2:
        outs[0][...] = result
    yield result.astype(BF16)


def proj_spread(links, w):
    rows = links.z_ag(w, 0)
    if links.chips == links.n_t:
        blocks = [
            lax.dynamic_index_in_dim(rows, links.chip ^ links.t ^ rel, 0, keepdims=False)
            for rel in range(links.chips)
        ]
    else:
        rows = links.by_index(rows, 0, links.t).reshape(links.chips, -1, w.shape[1])
        blocks = [
            lax.dynamic_index_in_dim(rows, links.chip ^ rel, 0, keepdims=False)
            for rel in range(links.chips)
        ]
    came = jnp.stack(links.chip_a2a(blocks), 0)
    return jnp.stack([came, links.core_swap(came)], 1)


def proj_collect(links, own, other):
    mine = (own + links.core_swap(other).astype(F32)).astype(BF16)
    blocks = [mine[rel] for rel in range(links.chips)]
    rows = jnp.stack(links.chip_a2a(blocks), 0)
    if links.chips == links.n_t:
        rows = links.by_index(rows, 0, links.chip ^ links.t)
    else:
        rows = links.by_index(rows, 0, links.chip).reshape(links.n_t, -1, own.shape[2])
        rows = links.by_index(rows, 0, links.t)
    return links.z_rs(rows, 0)


def core_halves(links, x):
    split = x.reshape(x.shape[:-1] + (2, x.shape[-1] // 2))
    return links.by_index(split, x.ndim - 1, links.core).reshape(x.shape)


def enter(links, w, m):
    rows = m.hid.shape[0]
    joined = links.rows_by_t(jnp.concatenate([m.hid, m.emb], axis=1))
    wide = joined.astype(F32)
    m.inverse = lax.rsqrt(jnp.mean(wide * wide, axis=1) + EPSILON)
    half = joined.shape[1] // links.n_dp
    blocks = []
    for rel in range(links.chips):
        at = 2 * (links.chip ^ rel)
        pieces = [
            lax.dynamic_slice_in_dim(joined, (at + (links.core ^ j)) * half, half, axis=1)
            for j in range(2)
        ]
        blocks.append(jnp.concatenate(pieces, axis=1))
    m.joined = jnp.stack(links.chip_a2a(blocks), 0)
    places = jnp.arange(rows, dtype=jnp.int32)
    m.true = layout(m.lens, places)
    _, position, _, allowed = layout(m.lens, links.rows_by_t(places))
    m.allowed_rel = allowed.astype(F32)
    m.cos, m.sin = rope_tables(position)


def attend(links, w, m):
    wide = m.joined.astype(F32) * m.inv_attn[:, :, None]
    m.attn_in = lax.optimization_barrier((wide * w.g_attn).astype(BF16))
    qkv = links.chip_rs(dotl("crd,dn->crn", m.attn_in, w.qkv), 0)
    rows, width = qkv.shape[0], qkv.shape[1] // 3
    outs = (
        jax.ShapeDtypeStruct((rows, 3 * width), BF16),
        jax.ShapeDtypeStruct((rows, width), BF16),
    )
    args = (qkv, m.cos, m.sin, m.allowed_rel)
    m.qkv_low, attended = in_vmem(attend_kernel, outs, args, 4 * rows * rows * width)
    m.attended = links.chip_ag(attended, 0, direct=True)


def z_split(links, x, axis):
    rows = x.shape[axis]
    return x.reshape(x.shape[:axis] + (links.n_t, rows // links.n_t) + x.shape[axis + 1 :])


def z_join(x, axis):
    return x.reshape(x.shape[:axis] + (-1,) + x.shape[axis + 2 :])


def attend_out(links, w, m):
    part = dotl("crn,nd->crd", m.attended, w.out)
    summed = links.z_rs(z_split(links, part, 1), 1)
    rows = summed.shape[1]
    m.joined_z = m.joined[:, :rows].astype(F32)
    m.inv_attn_z = m.inv_attn[:, :rows]
    mid = m.joined_z + summed
    m.mid = mid
    squares = links.chip_sum(jnp.sum(mid * mid, axis=2))
    width = mid.shape[2] * links.chips
    m.inv_mlp = lax.rsqrt(squares / width + EPSILON)
    low = (mid * m.inv_mlp[:, :, None] * w.g_mlp).astype(BF16)
    m.mlp_in = z_join(links.z_ag(low, 1), 1)


def feed(links, w, m):
    summed = links.chip_rs(dotl("crd,dn->crn", m.mlp_in, w.gate_up), 0)
    units = 2 * w.down.shape[0]
    m.adapter = summed[:, units:].astype(BF16)
    gate_up = summed[:, :units] + dotf("ra,an->rn", m.adapter, w.adapter_up)
    activated, m.gate_back = jax.vjp(gated_gelu, gate_up)
    m.hidden = links.chip_ag(activated.astype(BF16), 0, direct=True)


def feed_out(links, w, m):
    part = dotl("crn,nd->crd", m.hidden, w.down)
    summed = links.z_rs(z_split(links, part, 1), 1)
    m.block = (m.mid + summed).astype(BF16)
    m.block = core_halves(links, m.block)
    part = dotl("crd,xydn->xycrn", m.block, w.proj)
    part = links.by_index(links.by_index(part, 1, links.core), 0, links.chip)
    part = z_join(part, 0).transpose(1, 2, 0, 3)
    part = part.reshape(part.shape[:2] + (-1,))
    shared = links.chip_rs(part, 0, direct=True).astype(BF16)
    whole = links.by_index(links.z_ag(shared, 0), 0, links.t)
    shared_full = whole.reshape(-1, whole.shape[2])
    m.mamba_in = m.hid.astype(F32) + shared_full.astype(F32)
    own = z_split(links, m.hid, 0)
    own = lax.dynamic_index_in_dim(own, links.t, 0, keepdims=False)
    m.mamba_in_z = own.astype(F32) + shared.astype(F32)


def mix(links, w, m):
    taps_x, taps_bc, step_bias, decay_log, skip, gate_gain = w.smalls
    segment, _, valid, allowed = m.true
    mamba_in = m.mamba_in
    inverse = lax.rsqrt(jnp.mean(mamba_in * mamba_in, axis=1, keepdims=True) + EPSILON)
    ssm_in = (mamba_in * inverse * w.g_mamba).astype(BF16)
    gate_x = dotf("td,kdc->ktc", ssm_in, w.w_in)
    state_io = dotf("td,dn->tn", ssm_in, w.bc)
    step_raw = dotf("td,dn->tn", ssm_in, w.dt)
    grad_low = m.cot * valid[:, None].astype(BF16)
    d_norm = dotf("tn,in->ti", grad_low, w.mout)
    d_scaled = d_norm * gate_gain
    rows, width = gate_x.shape[1:]
    heads = step_raw.shape[1]
    earlier = [jnp.pad(segment, (j, 0), constant_values=-1)[:rows] for j in range(taps_x.shape[0])]
    same = jnp.stack([(e == segment).astype(F32) for e in earlier], 1)
    skips = jnp.repeat(skip, width // heads)[None, :]
    args = (gate_x, state_io, step_raw, taps_x, taps_bc, step_bias[None, :], decay_log[None, :])
    args += (skips, same, allowed.astype(F32), d_scaled)
    outs = (jax.ShapeDtypeStruct((rows, width), F32), jax.ShapeDtypeStruct((rows, 2), F32))
    gated, sums = in_vmem(mix_kernel, outs, args, 4 * rows * rows * width)
    inner = width * links.n_t
    sums = links.z_sum(sums)
    squares, weighted = sums[:, 0], sums[:, 1]
    row_scale = lax.rsqrt(squares / inner + EPSILON)
    m.gated_norm = (gated * row_scale[:, None] * gate_gain).astype(BF16)
    m.mamba_out = dotl("ti,in->tn", m.gated_norm, w.mout)

    grad_gain = jnp.sum(d_norm * gated * row_scale[:, None], axis=0)
    scales = jnp.stack([row_scale, row_scale**3 * weighted / inner], 1)
    outs = (
        jax.ShapeDtypeStruct(gate_x.shape, BF16),
        jax.ShapeDtypeStruct(state_io.shape, BF16),
        jax.ShapeDtypeStruct(step_raw.shape, F32),
        jax.ShapeDtypeStruct(taps_x.shape, F32),
        jax.ShapeDtypeStruct(taps_bc.shape, F32),
        jax.ShapeDtypeStruct((1, heads), F32),
        jax.ShapeDtypeStruct((1, heads), F32),
        jax.ShapeDtypeStruct((1, width), F32),
    )
    args += (gated, scales)
    grads = in_vmem(mix_back_kernel, outs, args, 16 * rows * rows * width)
    m.gate_x_low, d_state_io, d_step, d_taps_x, d_taps_bc, d_bias, d_decay, d_skip = grads
    d_skip = jnp.sum(d_skip.reshape(heads, width // heads), axis=1)
    m.step_low = d_step.astype(BF16)
    part_in = dotf("ktc,kdc->td", m.gate_x_low, w.w_in) + dotf("tn,dn->td", m.step_low, w.dt)
    terms = jnp.concatenate([part_in.astype(BF16), d_state_io], axis=1)
    m.terms = z_split(links, links.rows_by_t(terms), 0)
    m.ssm_in = ssm_in
    m.ssm_in_z = own_rows(links, ssm_in)
    m.grad_low = grad_low
    m.sums_dp = (d_taps_x, grad_gain, d_bias[0], d_decay[0], d_skip)
    m.d_taps_bc = d_taps_bc


def settle(links, w, m):
    summed = links.z_rs(m.terms, 0)
    model_width = m.mamba_in_z.shape[1]
    m.state_low = summed[:, model_width:].astype(BF16)
    dy = summed[:, :model_width] + dotf("tn,dn->td", m.state_low, w.bc)
    v = m.mamba_in_z
    inv = lax.rsqrt(jnp.mean(v * v, axis=1, keepdims=True) + EPSILON)
    scaled = dy * w.g_mamba
    dv = inv * scaled - v * (inv**3 * jnp.mean(scaled * v, axis=1, keepdims=True))
    grad_g_mamba = jnp.sum(dy * v * inv, axis=0)
    m.sums_all = (m.d_taps_bc, grad_g_mamba)
    m.d_mamba = dv + own_rows(links, m.grad_low).astype(F32)
    m.shared_low = links.chip_ag(m.d_mamba.astype(BF16), 0, direct=True)
    split = m.shared_low.reshape(m.shared_low.shape[:2] + w.proj.shape[:2] + (-1,))
    m.shared_cols = links.by_index(links.by_index(split, 3, links.core), 2, links.chip)
    d_block = core_halves(links, dotf("crxyn,xydn->crd", m.shared_cols, w.proj))
    m.d_block = d_block
    m.mlp_low = z_join(links.z_ag(d_block.astype(BF16), 1), 1)


def own_rows(links, x):
    return lax.dynamic_index_in_dim(z_split(links, x, 0), links.t, 0, keepdims=False)


def finish_output(links, micro):
    terms = jnp.stack([z_split(links, links.rows_by_t(m.mamba_out), 0) for m in micro], 0)
    summed = links.z_rs(terms, 1)
    base = jnp.stack([m.mamba_in_z for m in micro], 0)
    valid = jnp.stack([own_rows(links, m.true[2]) for m in micro], 0)
    low = ((base + summed) * valid[:, :, None].astype(F32)).astype(BF16)
    whole = links.by_index(links.z_ag(low, 1), 1, links.t)
    return z_join(whole, 1)


def feed_back(links, w, m):
    part = dotl("crd,nd->crn", m.mlp_low, w.down)
    d_hidden = links.chip_rs(part, 0)
    (d_gate_up,) = m.gate_back(d_hidden)
    m.gate_up_own = d_gate_up.astype(BF16)
    part = dotl("rn,an->ra", m.gate_up_own, w.adapter_up)
    m.gate_up_low = links.chip_ag(jnp.concatenate([m.gate_up_own, part], 1), 0)


def feed_back_out(links, w, m):
    part = dotl("crn,dn->crd", m.gate_up_low, w.gate_up)
    dy = links.z_rs(z_split(links, part, 1), 1)
    scaled = dy * w.g_mlp
    v, inv = m.mid, m.inv_mlp
    weighted = links.chip_sum(jnp.sum(scaled * v, axis=2))
    width = v.shape[2] * links.chips
    dv = scaled * inv[:, :, None] - v * (inv**3 * weighted / width)[:, :, None]
    m.grad_g_mlp = jnp.sum(dy * v * inv[:, :, None], axis=(0, 1))
    m.d_mid = dv + m.d_block
    m.attn_low = z_join(links.z_ag(m.d_mid.astype(BF16), 1), 1)


def attend_back(links, w, m):
    part = dotl("crd,nd->crn", m.attn_low, w.out)
    d_attended = links.chip_rs(part, 0, direct=True)
    rows, width = d_attended.shape
    outs = (jax.ShapeDtypeStruct((rows, 3 * width), BF16),)
    args = (m.qkv_low, d_attended, m.cos, m.sin, m.allowed_rel)
    (d_qkv,) = in_vmem(attend_back_kernel, outs, args, 10 * rows * rows * width)
    m.d_qkv = links.chip_ag(d_qkv, 0)


def leave(links, w, m):
    part = dotl("crn,dn->crd", m.d_qkv, w.qkv)
    dy = links.z_rs(z_split(links, part, 1), 1)
    scaled = dy * w.g_attn
    v, inv = m.joined_z, m.inv_attn_z
    weighted = links.chip_sum(jnp.sum(scaled * v, axis=2))
    width = v.shape[2] * links.chips
    dv = scaled * inv[:, :, None] - v * (inv**3 * weighted / width)[:, :, None]
    m.grad_g_attn = jnp.sum(dy * v * inv[:, :, None], axis=(0, 1))
    m.d_joined = (dv + m.d_mid).astype(BF16)
    leave_rows(links, m)


def leave_rows(links, m):
    d_joined = m.d_joined.reshape(links.chips, -1, m.d_joined.shape[-1])
    came = jnp.stack(links.chip_a2a([d_joined[rel] for rel in range(links.chips)]), 0)
    rows = came.shape[1]
    came = came.reshape(links.chips, rows, 2, -1)
    came = links.by_index(links.by_index(came, 2, links.core), 0, links.chip)
    came = came.transpose(1, 0, 2, 3).reshape(rows, -1)
    model_width = m.d_mamba.shape[1]
    d_hid = (came[:, :model_width].astype(F32) + m.d_mamba).astype(BF16)
    both = jnp.concatenate([d_hid, came[:, model_width:]], axis=1)
    whole = links.by_index(links.z_ag(both, 0), 0, links.t)
    whole = whole.reshape(-1, both.shape[1])
    m.d_hid, m.d_emb = whole[:, :model_width], whole[:, model_width:]


def sds(shape, dtype=F32):
    return jax.ShapeDtypeStruct(shape, dtype)


def mixer_rows(links, m):
    whole = m.shared_all.reshape(-1, m.shared_all.shape[2])
    m.mamba_in = m.hid.astype(F32) + whole.astype(F32)
    m.mamba_in_z = own_rows(links, m.hid).astype(F32) + m.shared_z.astype(F32)


def projection_grads(links, micro):
    block = jnp.concatenate([m.block for m in micro], axis=0)
    low = jnp.concatenate([m.shared_low for m in micro], axis=0)
    cols = links.dp_order(low, 2).reshape(low.shape[:2] + (links.chips, 2, -1))
    spec = "crd,crxn->xdn"
    return dotf(spec, block, cols[:, :, :, 0]), dotl(spec, block, cols[:, :, :, 1])


def enter_group(links, w, m):
    rows = m.hid.shape[0]
    places = jnp.arange(rows, dtype=jnp.int32)
    m.true = layout(m.lens, places)
    _, position, _, allowed = layout(m.lens, links.rows_by_t(places))
    m.allowed_rel = allowed.astype(F32)
    m.cos, m.sin = rope_tables(position)
    return Enter(m.hid, m.emb, w.g_attn[None, :])


def take_enter(m, got):
    m.attn_in, m.joined_z, m.inv_attn_z = got


def attend_group(links, w, m):
    rows, width = m.attn_in.shape[1], w.qkv_pair.shape[1]
    args = (m.cos, m.sin, m.allowed_rel)
    outs = (sds((rows, width), BF16),)
    return ByChips(m.attn_in, w.qkv_pair, False, width // 3, attend_local, args, outs)


def attend_out_group(links, w, m):
    width = m.joined_z.shape[1]
    outs = (sds(m.joined_z.shape), sds(m.inv_attn_z.shape))
    args = (m.joined_z, w.g_mlp[None, :])
    work = partial(norm_local, width * links.chips)
    return ByTensor(m.attended, w.out_pair, False, work, args, outs)


def feed_group(links, w, m):
    rows, units = m.mlp_in.shape[1], w.down_pair.shape[0]
    outs = (sds((rows, 2 * units)), sds((rows, w.gate_up_pair.shape[1] - 2 * units), BF16))
    args = (w.adapter_up,)
    return ByChips(m.mlp_in, w.gate_up_pair, False, units, feed_local, args, outs)


def feed_back_group(links, w, m):
    args = (m.gate_up, w.adapter_up)
    rank = w.gate_up_pair.shape[1] - m.gate_up.shape[1]
    scratch = (pltpu.VMEM((m.gate_up.shape[0], rank), F32),)
    width = w.gate_up_pair.shape[1]
    return ByChips(m.mlp_low, w.down_pair, True, width, feed_back_local, args, (), scratch)


def feed_back_out_group(links, w, m):
    width = m.mid_z.shape[1]
    args = (m.mid_z, m.inv_mlp, w.g_mlp[None, :], m.d_block.reshape(m.mid_z.shape))
    outs = (sds(m.mid_z.shape), sds((1, width)))
    work = partial(norm_back_local, width * links.chips)
    return ByTensor(m.gate_up_low, w.gate_up_pair, True, work, args, outs)


def attend_back_group(links, w, m):
    args = (m.qkv_low, m.cos, m.sin, m.allowed_rel)
    width = w.qkv_pair.shape[1]
    return ByChips(m.attn_low, w.out_pair, True, width, attend_back_local, args, ())


def leave_group(links, w, m):
    width = m.joined_z.shape[1]
    args = (m.joined_z, m.inv_attn_z, w.g_attn[None, :], m.d_mid)
    work = partial(norm_back_local, width * links.chips)
    theirs = jnp.concatenate([m.d_mamba, jnp.zeros_like(m.d_mamba)], axis=1)
    return Leave(m.d_qkv, w.qkv_pair, work, args, sds((1, width)), theirs)


def feed_out_group(links, w, m):
    return FeedOut(m.hidden, w.down_pair, m.mid_z, w.proj)


def settle_group(links, w, m):
    grad = own_rows(links, m.grad_low)
    return Settle(m.terms, w.bc, m.mamba_in_z, w.g_mamba[None, :], grad, w.proj)


def spread_group(links, w, m):
    return Spread(w.proj_own)


def outputs_group(links, w, micro):
    terms = [z_split(links, links.rows_by_t(m.mamba_out), 0) for m in micro]
    base = [m.mamba_in_z for m in micro]
    valid = [own_rows(links, m.true[2])[:, None].astype(F32) for m in micro]
    args = (jnp.concatenate(terms, 1), jnp.concatenate(base, 0), jnp.concatenate(valid, 0))
    return Outputs(*args)


def take_feed_out(m, got):
    m.block, m.shared_all, m.shared_z = got
    m.block = m.block.reshape(4, -1, m.block.shape[1])


def take_settle(m, got):
    gathered, m.shared_low, m.d_mamba, m.state_low, d_block, d_gain = got
    m.mlp_low = z_join(gathered, 1)
    m.d_block = d_block
    m.sums_all = (m.d_taps_bc, d_gain[0])


def take_attend(m, got):
    m.attended, m.qkv_low = got


def take_attend_out(m, got):
    gathered, m.mid_z, m.inv_mlp = got
    m.mlp_in = z_join(gathered, 1)
    m.mid = m.mid_z.reshape(gathered.shape[0], -1, gathered.shape[3])


def take_feed(m, got):
    m.hidden, m.gate_up, m.adapter = got


def take_feed_back(m, got):
    (m.gate_up_low,) = got
    m.gate_up_own = m.gate_up_low[0, :, : m.gate_up.shape[1]]


def take_feed_back_out(m, got):
    gathered, m.d_mid, d_gain = got
    m.attn_low = z_join(gathered, 1)
    m.grad_g_mlp = d_gain[0]


def take_attend_back(m, got):
    (m.d_qkv,) = got


def take_leave(m, got):
    d_gain, m.left = got
    m.grad_g_attn = d_gain[0]


def fused(links, w, number, *work):
    groups = [make(links, w, m) for make, _, m in work]
    for (_, taker, m), got in zip(work, together(groups, number)):
        taker(m, got)


ENTER = (enter_group, take_enter)
ATTEND = (attend_group, take_attend)
ATTEND_OUT = (attend_out_group, take_attend_out)
FEED = (feed_group, take_feed)
FEED_BACK = (feed_back_group, take_feed_back)
FEED_BACK_OUT = (feed_back_out_group, take_feed_back_out)
ATTEND_BACK = (attend_back_group, take_attend_back)
LEAVE = (leave_group, take_leave)
FEED_OUT = (feed_out_group, take_feed_out)
SETTLE = (settle_group, take_settle)


WEIGHT_GRADS = {
    "down": ("crn,crd->nd", "hidden", "mlp_low", False, 1),
    "gate_up": ("crd,crn->dn", "mlp_in", "gate_up_low", True, 1),
    "out": ("crn,crd->nd", "attended", "attn_low", False, 1),
    "qkv": ("crd,crn->dn", "attn_in", "d_qkv", True, 3),
}


def local(
    hidden,
    embedding,
    lengths,
    query_key_value_weight,
    attention_output_weight,
    attention_gain,
    feedforward_gain,
    gate_up_weight,
    adapter_down,
    adapter_up,
    down_weight,
    shared_projection_weight,
    mixer_gain,
    mixer_input_weight,
    state_map_weight,
    step_weight,
    mixer_output_weight,
    mixer_input_taps,
    state_map_taps,
    step_bias,
    decay_logarithm,
    head_skip_weight,
    gated_norm_gain,
    cotangent,
    n_dp,
    n_t,
):
    links = Links(n_dp, n_t)
    smalls = (
        mixer_input_taps,
        state_map_taps,
        step_bias,
        decay_logarithm,
        head_skip_weight,
        gated_norm_gain,
    )
    micro = [
        SimpleNamespace(
            hid=hidden[b], emb=embedding[b], lens=lengths[b, 0], cot=cotangent[b]
        )
        for b in range(hidden.shape[0])
    ]
    w = SimpleNamespace()
    gains = core_pair(links, jnp.stack([attention_gain, feedforward_gain], 0), 1).astype(F32)
    w.g_attn, w.g_mlp = gains[0], gains[1]
    parts = query_key_value_weight.transpose(1, 0, 2)
    w.qkv_pair = RowPair(parts, links.core_swap(parts))
    def stage(work, m):
        with jax.named_scope(f"{work.__name__}_micro{micro.index(m)}"):
            work(links, w, m)

    units = gate_up_weight.shape[2]
    up_own = adapter_up.reshape(adapter_up.shape[0], 2 * units)
    cols = jnp.concatenate([gate_up_weight[:, 0], gate_up_weight[:, 1], adapter_down], axis=1)
    w.out_pair = ColPair(attention_output_weight, links.core_swap(attention_output_weight))
    w.gate_up_pair = RowPair(cols, links.core_swap(cols))
    w.down_pair = ColPair(down_weight, links.core_swap(down_weight))
    w.proj_own = shared_projection_weight
    state_cols, step_cols = state_map_weight.shape[1], step_weight.shape[1]
    packed = jnp.concatenate([state_map_weight, step_weight, mixer_gain[:, None]], axis=1)

    w.smalls = smalls
    def gather_mixer():
        w.adapter_up = lax.all_gather(after(up_own, w.begun), "dp", axis=0, tiled=True)
        whole = lax.all_gather(after(packed, w.begun), "dp", axis=0, tiled=True)
        w.bc = whole[:, :state_cols]
        w.dt = whole[:, state_cols : state_cols + step_cols]
        w.g_mamba = whole[:, state_cols + step_cols].astype(F32)
        shard = after(mixer_input_weight.transpose(1, 0, 2), w.begun)
        w.w_in = lax.all_gather(shard, "dp", axis=1, tiled=True)
        shard = after(mixer_output_weight, w.begun)
        w.mout = lax.all_gather(shard, "dp", axis=1, tiled=True)

    def run(*works):
        for work in works:
            for m in micro:
                stage(work, m)

    def both(get, axis=0):
        return jnp.concatenate([get(m) for m in micro], axis=axis)

    def mixer_grads(done=None):
        ssm_in = both(lambda m: m.ssm_in)
        grad_in = dotl("td,ktc->kdc", ssm_in, both(lambda m: m.gate_x_low, 1))
        begun = grad_in
        grad_in = grad_in if done is None else after(grad_in, done)
        grad_in = lax.psum_scatter(grad_in, "dp", scatter_dimension=1, tiled=True)
        grad_bc = dotl("td,tn->dn", both(lambda m: m.ssm_in_z), both(lambda m: m.state_low))
        grad_dt = dotl("td,tn->dn", ssm_in, both(lambda m: m.step_low))
        grad_small = jnp.concatenate([grad_bc, grad_dt], axis=1)
        grad_small = lax.psum_scatter(grad_small, "dp", scatter_dimension=0, tiled=True)
        grad_up = dotl("ra,rn->an", both(lambda m: m.adapter), both(lambda m: m.gate_up_own))
        grad_up = lax.psum_scatter(grad_up, "dp", scatter_dimension=0, tiled=True)
        return begun, grad_in, grad_small, grad_up

    def mout_grad(done=None):
        grad_mout = dotl("tn,ti->ni", both(lambda m: m.grad_low), both(lambda m: m.gated_norm))
        grad_mout = grad_mout if done is None else after(grad_mout, done)
        grad_mout = lax.psum_scatter(grad_mout, "dp", scatter_dimension=0, tiled=True)
        return grad_mout

    def lines(values):
        flat = jnp.concatenate([v.reshape(-1) for v in values])
        return jnp.pad(flat, (0, -flat.size % 1024)).reshape(-1, 128)

    def small_terms():
        sums = [jax.tree.map(lambda *v: total(v), *[m.sums_all for m in micro])]
        sums += [jax.tree.map(lambda *v: total(v), *[m.sums_dp for m in micro])]
        return [lines(values) for values in sums]

    def tensor_terms():
        terms = [grad_cols[:, 2 * units :].astype(BF16), grad_small[:, :state_cols]]
        return jnp.concatenate([v.reshape(-1, HEAD) for v in terms], 0)

    def weight_grad(name):
        _, a, b, by_rows, parts = WEIGHT_GRADS[name]

        def make(*_):
            return WeightGrad([getattr(m, a) for m in micro], [getattr(m, b) for m in micro], by_rows, parts)

        return (make, lambda _, got: setattr(w, "grad_" + name, got[0]), None)

    if links.chips == 4 and links.n_t == 4 and len(micro) == 2:
        a, b = micro
        spread = (spread_group, lambda _, got: setattr(w, "proj", got[0]), None)
        fused(links, w, 1, (*ENTER, a))
        fused(links, w, 2, (*ATTEND, a), spread, (*ENTER, b))
        w.begun = a.attended
        gather_mixer()
        fused(links, w, 3, (*ATTEND_OUT, a), (*ATTEND, b))
        fused(links, w, 4, (*FEED, a), (*ATTEND_OUT, b))
        fused(links, w, 5, (*FEED, b), (*FEED_OUT, a))
        mixer_rows(links, a)
        stage(mix, a)
        fused(links, w, 6, (*FEED_OUT, b), (*SETTLE, a))
        mixer_rows(links, b)
        stage(mix, b)
        outputs = (outputs_group, lambda _, got: setattr(w, "results", got[0]), micro)
        fused(links, w, 7, (*FEED_BACK, a), (*SETTLE, b), outputs)
        collect = (lambda *_: Collect(*projection_grads(links, micro)), lambda _, got: setattr(w, "grad_proj", got[0]), None)
        fused(links, w, 8, (*FEED_BACK_OUT, a), (*FEED_BACK, b))
        terms = small_terms()
        rows_all = terms[0].shape[0]
        sums = (
            lambda *_: SmallSum(jnp.concatenate(terms, 0), rows_all),
            lambda _, got: setattr(w, "flat", got[0]),
            None,
        )
        fused(links, w, 9, (*FEED_BACK_OUT, b), (*ATTEND_BACK, a), weight_grad("gate_up"), sums)
        flat, grad_cols = w.flat, w.grad_gate_up
        fused(links, w, 10, (*LEAVE, a), (*ATTEND_BACK, b), weight_grad("down"), collect)
        grad_mout = mout_grad(b.d_qkv)
        _, grad_in, grad_small, grad_up = mixer_grads(b.d_qkv)

        fused(links, w, 11, (*LEAVE, b), weight_grad("qkv"), weight_grad("out"))
        whole_t = links.z_sum(tensor_terms())
        grad_down, grad_out = w.grad_down, w.grad_out
        grad_qkv = w.grad_qkv.transpose(1, 0, 2)
        grad_proj = w.grad_proj
        for m in micro:
            m.d_hid, m.d_emb = jnp.split(m.left.reshape(-1, m.left.shape[2]), 2, axis=1)
        results = w.results.reshape(links.n_t, len(micro), -1, w.results.shape[2])
        results = z_join(results.transpose(1, 0, 2, 3), 1)
    else:
        for m in micro:
            stage(enter, m)
        inverses = jnp.stack([m.inverse for m in micro], 0)
        inverses = jnp.stack(links.chip_a2a([inverses] * links.chips), 1)
        for b, m in enumerate(micro):
            m.inv_attn = inverses[b]
        w.qkv, w.out = w.qkv_pair.whole(), w.out_pair.whole()
        w.gate_up, w.down = w.gate_up_pair.whole(), w.down_pair.whole()
        w.proj = proj_spread(links, shared_projection_weight)
        run(attend)
        w.begun = micro[0].attended
        gather_mixer()
        run(attend_out, feed, feed_out, mix, settle)
        run(feed_back, feed_back_out, attend_back, leave)
        results = finish_output(links, micro)
        grad_proj = proj_collect(links, *projection_grads(links, micro))
        mixed = mixer_grads()
        grad_mout = mout_grad()

        def grad(name, axis):
            spec, a, b = WEIGHT_GRADS[name][:3]
            terms = [dotf(spec, getattr(m, a), getattr(m, b)) for m in micro]
            return core_rs(links, total(terms), axis)

        grad_down, grad_cols, grad_out = grad("down", 1), grad("gate_up", 0), grad("out", 1)
        grad_qkv = jnp.stack(jnp.split(grad("qkv", 0), 3, axis=1), 1)
        _, grad_in, grad_small, grad_up = mixed
        flat_all, flat_dp = small_terms()
        rows_all = flat_all.shape[0]
        flat = links.dp_sum(jnp.concatenate([links.z_sum(flat_all), flat_dp], 0))
        whole_t = links.z_sum(tensor_terms())
    small_sums, flat = [], flat.reshape(-1)
    for start, parts in ((0, micro[0].sums_all), (rows_all * 128, micro[0].sums_dp)):
        for v in parts:
            small_sums.append(flat[start : start + v.size].reshape(v.shape))
            start += v.size
    own_gain = mixer_gain.shape[0]
    grad_g_mamba = lax.dynamic_slice_in_dim(small_sums[1], links.d * own_gain, own_gain)

    g_rows = total([jnp.stack([m.grad_g_attn, m.grad_g_mlp], 0) for m in micro])
    half = g_rows.shape[1] // 2
    g_rows = g_rows[:, :half] + links.core_swap(g_rows[:, half:])
    g_rows = links.z_sum(g_rows)

    grad_gate_up = jnp.stack([grad_cols[:, :units], grad_cols[:, units : 2 * units]], 1)
    split = grad_cols.shape[0] * (grad_cols.shape[1] - 2 * units) // HEAD
    grad_adapter_down = whole_t[:split].reshape(grad_cols.shape[0], -1).astype(F32)
    grad_bc = whole_t[split:].reshape(-1, state_cols).astype(F32)

    return (
        results,
        jnp.stack([m.d_hid for m in micro]),
        jnp.stack([m.d_emb for m in micro]),
        grad_qkv,
        grad_out,
        g_rows[0],
        g_rows[1],
        grad_gate_up,
        grad_adapter_down,
        grad_up.reshape(adapter_up.shape).astype(F32),
        grad_down,
        grad_proj,
        grad_g_mamba,
        grad_in.transpose(1, 0, 2).astype(F32),
        grad_bc,
        grad_small[:, state_cols:].astype(F32),
        grad_mout.T.astype(F32),
        small_sums[2],
        small_sums[0],
        small_sums[4],
        small_sums[5],
        small_sums[6],
        small_sums[3],
    )


def solution(mesh):
    rows = P(None, "dp", None)
    by_dp = P("dp", None, "tensor")
    by_t = P("tensor", "dp")
    weights = (by_dp, by_t, P("dp"), P("dp"), by_dp, P("dp", None), by_dp, by_t, by_t, P("dp"))
    weights += (by_dp, P("dp", None), P("dp", "tensor"), by_t)
    smalls = (P(None, "tensor"), P(), P("tensor"), P("tensor"), P("tensor"), P("tensor"))
    return jax.shard_map(
        partial(local, n_dp=mesh.shape["dp"], n_t=mesh.shape["tensor"]),
        mesh=mesh,
        in_specs=(rows, rows, rows) + weights + smalls + (rows,),
        out_specs=(rows, rows, rows) + weights + smalls,
        check_vma=False,
    )
```

```python
from functools import partial
from types import SimpleNamespace

import jax
import jax.numpy as jnp
from jax import lax
from jax.experimental import pallas as pl
from jax.experimental.pallas import tpu as pltpu
from jax.sharding import PartitionSpec as P

HEAD = 128
EPSILON = 1e-05
ROPE_BASE = 10000.0
MASKED = -1e30
TOP_PRECISION = lax.Precision.HIGHEST
F32 = jnp.float32
BF16 = jnp.bfloat16


def layout(len_row, places):
    bounds = jnp.cumsum(len_row)[:-1]
    passed = places[:, None] >= bounds[None, :]
    segment = jnp.sum(passed.astype(jnp.int32), axis=1)
    starts = jnp.max(jnp.where(passed, bounds[None, :], 0), axis=1)
    position = places - starts
    valid = segment < bounds.shape[0]
    allowed = (segment[:, None] == segment[None, :]) & (places[None, :] <= places[:, None])
    return (segment, position, valid, allowed)


def rope_tables(position):
    half = HEAD // 2
    frequency = ROPE_BASE ** (-2.0 * jnp.arange(half, dtype=F32) / HEAD)
    angles = position.astype(F32)[:, None] * frequency[None, :]
    cosine, sine = jnp.cos(angles), jnp.sin(angles)
    return jnp.concatenate([cosine, cosine], axis=1), jnp.concatenate([-sine, sine], axis=1)


def rows_down(x, count):
    return x if count == 0 else pltpu.roll(x, count, 0)


def rows_up(x, count):
    return x if count == 0 else pltpu.roll(x, x.shape[0] - count, 0)


def conv_taps(x, taps_ref, same_ref):
    summed = x * taps_ref[0:1, :]
    for j in range(1, taps_ref.shape[0]):
        summed = summed + rows_down(x, j) * same_ref[:, j : j + 1] * taps_ref[j : j + 1, :]
    return summed


def conv_taps_back(x, d_out, taps_ref, same_ref, d_taps_ref, cols):
    d_x = d_out * taps_ref[0:1, cols]
    d_taps_ref[0:1, cols] = jnp.sum(d_out * x, axis=0, keepdims=True)
    for j in range(1, taps_ref.shape[0]):
        kept = d_out * same_ref[:, j : j + 1]
        d_taps_ref[j : j + 1, cols] = jnp.sum(kept * rows_down(x, j), axis=0, keepdims=True)
        d_x = d_x + rows_up(kept * taps_ref[j : j + 1, cols], j)
    return d_x


def exact(a, b, dims):
    return lax.dot_general(
        a, b, (dims, ((), ())), precision=TOP_PRECISION, preferred_element_type=F32
    )


def fast(a, b, dims):
    return lax.dot_general(
        a.astype(BF16), b.astype(BF16), (dims, ((), ())), preferred_element_type=F32
    )


PLAIN = ((1,), (0,))
BY_COLS = ((1,), (1,))
BY_ROWS = ((0,), (0,))


def triangle(rows):
    t = lax.broadcasted_iota(jnp.int32, (rows, rows), 0)
    s = lax.broadcasted_iota(jnp.int32, (rows, rows), 1)
    return t, s


def step_terms(step_ref, bias_ref, decay_ref, rows):
    t, s = triangle(rows)
    raw = step_ref[...] + bias_ref[...]
    step = jnp.maximum(raw, 0.0) + jnp.log1p(jnp.exp(-jnp.abs(raw)))
    log_decay = -step * jnp.exp(decay_ref[...])
    running = exact((s <= t).astype(F32), log_decay, PLAIN)
    running_t = exact(log_decay, (t <= s).astype(F32), BY_ROWS)
    step_t = exact(step, (t == s).astype(F32), BY_ROWS)
    return raw, step, log_decay, running, running_t, step_t


def decayed(running, running_t, h, allowed):
    gap = running[:, h : h + 1] - running_t[h : h + 1, :]
    return jnp.exp(jnp.where(allowed, gap, MASKED))


def mix_kernel(
    gate_ref, state_ref, step_ref, taps_x_ref, taps_bc_ref, bias_ref, decay_ref, skip_ref,
    same_ref, allowed_ref, d_scaled_ref, gated_ref, sums_ref,
):
    rows = state_ref.shape[0]
    size = state_ref.shape[1] // 2
    heads = step_ref.shape[1]
    lanes = 128
    per = lanes * heads // gate_ref.shape[2]
    allowed = allowed_ref[...] > 0.0
    _, _, _, running, running_t, step_t = step_terms(step_ref, bias_ref, decay_ref, rows)
    conv_bc = conv_taps(state_ref[...], taps_bc_ref, same_ref)
    state = conv_bc * jax.nn.sigmoid(conv_bc)
    affinity = exact(state[:, size:], state[:, :size], BY_COLS)
    lane = lax.broadcasted_iota(jnp.int32, (rows, lanes), 1) * per // lanes
    squares = jnp.zeros((rows, lanes), F32)
    weighted = jnp.zeros((rows, lanes), F32)
    for group in range(gate_ref.shape[2] // lanes):
        cols = slice(group * lanes, (group + 1) * lanes)
        x = gate_ref[1, :, cols]
        conv = x * taps_x_ref[0:1, cols]
        for j in range(1, taps_x_ref.shape[0]):
            conv = conv + rows_down(x, j) * same_ref[:, j : j + 1] * taps_x_ref[j : j + 1, cols]
        act = conv * jax.nn.sigmoid(conv)
        mixed = act * skip_ref[0:1, cols]
        for i in range(per):
            h = group * per + i
            mixing = decayed(running, running_t, h, allowed) * affinity * step_t[h : h + 1, :]
            mixed = mixed + jnp.where(lane == i, fast(mixing, act, PLAIN), 0.0)
        z = gate_ref[0, :, cols]
        gated = mixed * (z * jax.nn.sigmoid(z))
        gated_ref[:, cols] = gated
        squares = squares + gated * gated
        weighted = weighted + gated * d_scaled_ref[:, cols]
    sums_ref[:, 0:1] = jnp.sum(squares, axis=1, keepdims=True)
    sums_ref[:, 1:2] = jnp.sum(weighted, axis=1, keepdims=True)


def mix_back_kernel(
    gate_ref, state_ref, step_ref, taps_x_ref, taps_bc_ref, bias_ref, decay_ref, skip_ref,
    same_ref, allowed_ref, d_scaled_ref, gated_ref, scales_ref,
    d_gate_ref, d_state_ref, d_step_ref, d_taps_x_ref, d_taps_bc_ref, d_bias_ref, d_decay_ref,
    d_skip_ref,
):
    rows = state_ref.shape[0]
    size = state_ref.shape[1] // 2
    heads = step_ref.shape[1]
    lanes = 128
    per = lanes * heads // gate_ref.shape[2]
    allowed = allowed_ref[...] > 0.0
    raw, step, log_decay, running, running_t, step_t = step_terms(
        step_ref, bias_ref, decay_ref, rows
    )
    conv_bc = conv_taps(state_ref[...], taps_bc_ref, same_ref)
    sig_bc = jax.nn.sigmoid(conv_bc)
    state = conv_bc * sig_bc
    affinity = exact(state[:, size:], state[:, :size], BY_COLS)
    lane = lax.broadcasted_iota(jnp.int32, (rows, lanes), 1) * per // lanes
    head_lane = lax.broadcasted_iota(jnp.int32, (rows, heads), 1)
    head_row = lax.broadcasted_iota(jnp.int32, (heads, rows), 0)
    d_affinity = jnp.zeros((rows, rows), F32)
    d_run = jnp.zeros((rows, heads), F32)
    d_step_t = jnp.zeros((heads, rows), F32)
    for group in range(gate_ref.shape[2] // lanes):
        cols = slice(group * lanes, (group + 1) * lanes)
        x = gate_ref[1, :, cols]
        conv = x * taps_x_ref[0:1, cols]
        for j in range(1, taps_x_ref.shape[0]):
            conv = conv + rows_down(x, j) * same_ref[:, j : j + 1] * taps_x_ref[j : j + 1, cols]
        sig = jax.nn.sigmoid(conv)
        act = conv * sig
        z = gate_ref[0, :, cols]
        sig_z = jax.nn.sigmoid(z)
        d_gated = d_scaled_ref[:, cols] * scales_ref[:, 0:1] - gated_ref[:, cols] * scales_ref[:, 1:2]
        d_mixed = d_gated * (z * sig_z)
        mixed = act * skip_ref[0:1, cols]
        d_act = d_mixed * skip_ref[0:1, cols]
        d_skip_ref[0:1, cols] = jnp.sum(d_mixed * act, axis=0, keepdims=True)
        for i in range(per):
            h = group * per + i
            decay = decayed(running, running_t, h, allowed)
            weight = affinity * step_t[h : h + 1, :]
            mixing = decay * weight
            mixed = mixed + jnp.where(lane == i, fast(mixing, act, PLAIN), 0.0)
            d_act = d_act + jnp.where(lane == i, fast(mixing, d_mixed, BY_ROWS), 0.0)
            d_mixing = fast(jnp.where(lane == i, d_mixed, 0.0), act, BY_COLS) * decay
            d_affinity = d_affinity + d_mixing * step_t[h : h + 1, :]
            by_aff = d_mixing * affinity
            d_step_t = d_step_t + jnp.where(
                head_row == h, jnp.sum(by_aff, axis=0, keepdims=True), 0.0
            )
            by_gap = jnp.sum(by_aff * step_t[h : h + 1, :], axis=1, keepdims=True)
            d_run = d_run + jnp.where(head_lane == h, by_gap, 0.0)
        d_gate_ref[0, :, cols] = (d_gated * mixed * (sig_z * (1.0 + z * (1.0 - sig_z)))).astype(BF16)
        d_conv = d_act * (sig * (1.0 + conv * (1.0 - sig)))
        d_x = conv_taps_back(x, d_conv, taps_x_ref, same_ref, d_taps_x_ref, cols)
        d_gate_ref[1, :, cols] = d_x.astype(BF16)
    t, s = triangle(rows)
    eye = (t == s).astype(F32)
    d_run = d_run - exact(eye, d_step_t * step_t, BY_COLS)
    d_log = exact((s >= t).astype(F32), d_run, PLAIN)
    d_step = exact(eye, d_step_t, BY_COLS) - jnp.exp(decay_ref[...]) * d_log
    d_raw = d_step * jax.nn.sigmoid(raw)
    d_step_ref[...] = d_raw
    d_bias_ref[...] = jnp.sum(d_raw, axis=0, keepdims=True)
    d_decay_ref[...] = jnp.sum(d_log * log_decay, axis=0, keepdims=True)
    d_b = exact(d_affinity, state[:, size:], BY_ROWS)
    d_c = exact(d_affinity, state[:, :size], PLAIN)
    d_silu = sig_bc * (1.0 + conv_bc * (1.0 - sig_bc))
    for part, d_part in enumerate((d_b, d_c)):
        cols = slice(part * size, (part + 1) * size)
        d_conv = d_part * d_silu[:, cols]
        d_x = conv_taps_back(
            state_ref[:, cols], d_conv, taps_bc_ref, same_ref, d_taps_bc_ref, cols
        )
        d_state_ref[:, cols] = d_x.astype(BF16)


def turned(x, cos_ref, sin_ref, sign):
    return x * cos_ref[...] + pltpu.roll(x, HEAD // 2, 1) * (sign * sin_ref[...])


def probabilities(query, key, allowed):
    scores = fast(query, key, BY_COLS) * HEAD ** (-0.5)
    scores = jnp.where(allowed, scores, MASKED)
    raised = jnp.exp(scores - jnp.max(scores, axis=1, keepdims=True))
    return raised / jnp.sum(raised, axis=1, keepdims=True)


def attend_kernel(qkv_ref, cos_ref, sin_ref, allowed_ref, low_ref, attended_ref):
    allowed = allowed_ref[...] > 0.0
    width = attended_ref.shape[1]
    for h in range(width // HEAD):
        q, k, v = (slice(i * width + h * HEAD, i * width + (h + 1) * HEAD) for i in range(3))
        query = turned(qkv_ref[:, q], cos_ref, sin_ref, 1.0).astype(BF16)
        key = turned(qkv_ref[:, k], cos_ref, sin_ref, 1.0).astype(BF16)
        value = qkv_ref[:, v].astype(BF16)
        low_ref[:, q] = query
        low_ref[:, k] = key
        low_ref[:, v] = value
        probs = probabilities(query, key, allowed)
        attended_ref[:, q] = fast(probs, value, PLAIN).astype(BF16)


def attend_back_kernel(low_ref, d_ref, cos_ref, sin_ref, allowed_ref, d_qkv_ref):
    allowed = allowed_ref[...] > 0.0
    width = d_ref.shape[1]
    for h in range(width // HEAD):
        q, k, v = (slice(i * width + h * HEAD, i * width + (h + 1) * HEAD) for i in range(3))
        query, key, value = low_ref[:, q], low_ref[:, k], low_ref[:, v]
        d_out = d_ref[:, q].astype(BF16)
        probs = probabilities(query, key, allowed)
        d_qkv_ref[:, v] = fast(probs, d_out, BY_ROWS).astype(BF16)
        d_probs = fast(d_out, value, BY_COLS)
        inner = jnp.sum(probs * d_probs, axis=1, keepdims=True)
        d_scores = (probs * (d_probs - inner) * HEAD ** (-0.5)).astype(BF16)
        d_query = fast(d_scores, key, PLAIN)
        d_key = fast(d_scores, query, BY_ROWS)
        d_qkv_ref[:, q] = turned(d_query, cos_ref, sin_ref, -1.0).astype(BF16)
        d_qkv_ref[:, k] = turned(d_key, cos_ref, sin_ref, -1.0).astype(BF16)


def in_vmem(kernel, outs, args, flops):
    size = sum(x.size * x.dtype.itemsize for x in tuple(args) + tuple(outs))
    return pl.pallas_call(
        kernel,
        out_shape=outs,
        in_specs=[pl.BlockSpec(memory_space=pltpu.VMEM)] * len(args),
        out_specs=[pl.BlockSpec(memory_space=pltpu.VMEM)] * len(outs),
        compiler_params=pltpu.CompilerParams(vmem_limit_bytes=40 * 2**20),
        cost_estimate=pl.CostEstimate(flops=flops, bytes_accessed=size, transcendentals=0),
    )(*args)


def gated_gelu(gate_up):
    half = gate_up.shape[1] // 2
    return jax.nn.gelu(gate_up[:, :half], approximate=True) * gate_up[:, half:]


def total(values):
    summed = values[0]
    for value in values[1:]:
        summed = summed + value
    return summed


def after(x, done):
    mark = done[(-1,) * done.ndim].astype(F32)
    return x + jnp.minimum(jnp.abs(mark), 0.0).astype(x.dtype)


class Links:
    def __init__(self, n_dp, n_t):
        self.n_dp = n_dp
        self.n_t = n_t
        self.chips = n_dp // 2
        self.chip_bits = self.chips.bit_length() - 1
        self.z_bits = n_t.bit_length() - 1
        d = lax.axis_index("dp")
        self.d = d
        self.core = d % 2
        self.chip = d // 2
        self.t = lax.axis_index("tensor")

    def core_swap(self, x):
        return lax.ppermute(x, "dp", [(i, i ^ 1) for i in range(self.n_dp)])

    def chip_swap(self, x, rel):
        return lax.ppermute(x, "dp", [(i, i ^ (rel << 1)) for i in range(self.n_dp)])

    def z_swap(self, x, rel):
        return lax.ppermute(x, "tensor", [(i, i ^ rel) for i in range(self.n_t)])

    def row_parts(self, rows):
        count = max(1, min(self.chip_bits, rows // 16))
        units = rows // 16
        edges = [0] + [16 * ((units * (i + 1)) // count) for i in range(count)]
        edges[-1] = rows
        return [(edges[i], edges[i + 1]) for i in range(count)]

    def chip_rs(self, terms, axis, direct=False):
        if direct:
            blocks = [
                lax.index_in_dim(terms, rel, axis, keepdims=False) for rel in range(self.chips)
            ]
            return total([block.astype(F32) for block in self.chip_a2a(blocks)])
        outs = []
        bits = self.chip_bits
        for number, (low, high) in enumerate(self.row_parts(terms.shape[axis + 1])):
            cur = lax.slice_in_dim(terms, low, high, axis=axis + 1)
            cur = cur.reshape(cur.shape[:axis] + (2,) * bits + cur.shape[axis + 1 :])
            left = list(range(bits))[::-1]
            for step in range(bits):
                bit = (number + step) % bits
                at = axis + left.index(bit)
                left.remove(bit)
                keep = lax.index_in_dim(cur, 0, at, keepdims=False)
                send = lax.index_in_dim(cur, 1, at, keepdims=False)
                got = self.chip_swap(send.astype(BF16), 1 << bit)
                cur = keep.astype(F32) + got.astype(F32)
            outs.append(cur)
        return outs[0] if len(outs) == 1 else jnp.concatenate(outs, axis=axis)

    def chip_ag(self, x, axis, direct=False):
        if direct:
            return jnp.stack(self.chip_a2a([x] * self.chips), axis=axis)
        bits = self.chip_bits
        outs = []
        for number, (low, high) in enumerate(self.row_parts(x.shape[axis])):
            blocks = {0: lax.slice_in_dim(x, low, high, axis=axis)}
            for step in range(bits):
                bit = (number + step) % bits
                for rel in list(blocks):
                    blocks[rel | (1 << bit)] = self.chip_swap(blocks[rel], 1 << bit)
            outs.append([blocks[rel] for rel in range(self.chips)])
        merged = []
        for rel in range(self.chips):
            pieces = [part[rel] for part in outs]
            merged.append(pieces[0] if len(pieces) == 1 else jnp.concatenate(pieces, axis=axis))
        return jnp.stack(merged, axis=axis)

    def chip_a2a(self, blocks):
        return [blocks[0]] + [self.chip_swap(blocks[rel], rel) for rel in range(1, self.chips)]

    def chip_sum(self, x):
        total = x
        for rel in range(1, self.chips):
            moved = jnp.stack([x[i ^ rel] for i in range(self.chips)], 0)
            total = total + self.chip_swap(moved, rel)
        return total

    def z_sum(self, x):
        return total([x] + [self.z_swap(x, rel) for rel in range(1, self.n_t)])

    def dp_sum(self, x):
        x = x + self.core_swap(x)
        return total(self.chip_a2a([x] * self.chips))

    def z_rs(self, terms, axis):
        bits = self.z_bits
        cur = terms.reshape(terms.shape[:axis] + (2,) * bits + terms.shape[axis + 1 :])
        left = list(range(bits))[::-1]
        for bit in range(bits):
            at = axis + left.index(bit)
            left.remove(bit)
            keep = lax.index_in_dim(cur, 0, at, keepdims=False)
            send = lax.index_in_dim(cur, 1, at, keepdims=False)
            got = self.z_swap(send.astype(BF16), 1 << bit)
            cur = keep.astype(F32) + got.astype(F32)
        return cur

    def z_ag(self, x, axis):
        blocks = {0: x}
        for bit in range(self.z_bits)[::-1]:
            for rel in list(blocks):
                blocks[rel | (1 << bit)] = self.z_swap(blocks[rel], 1 << bit)
        return jnp.stack([blocks[rel] for rel in range(self.n_t)], axis=axis)

    def dp_order(self, x, axis):
        split = x.reshape(x.shape[:axis] + (self.chips, 2, -1) + x.shape[axis + 1 :])
        split = self.by_index(self.by_index(split, axis + 1, self.core), axis, self.chip)
        return split.reshape(x.shape)

    def by_index(self, x, axis, own):
        count = x.shape[axis]
        return jnp.concatenate(
            [lax.dynamic_slice_in_dim(x, own ^ i, 1, axis=axis) for i in range(count)], axis=axis
        )

    def rows_by_t(self, x):
        rows = x.shape[0]
        split = x.reshape((self.n_t, rows // self.n_t) + x.shape[1:])
        return self.by_index(split, 0, self.t).reshape(x.shape)


def core_pair(links, x, axis):
    return jnp.concatenate([x, links.core_swap(x)], axis=axis)


def core_rs(links, x, axis):
    half = x.shape[axis] // 2
    own = lax.slice_in_dim(x, 0, half, axis=axis)
    other = lax.slice_in_dim(x, half, 2 * half, axis=axis)
    return own + links.core_swap(other.astype(BF16)).astype(F32)


def dotf(spec, a, b):
    return jnp.einsum(spec, a, b, preferred_element_type=F32)


def dotl(spec, a, b):
    return jnp.einsum(spec, a, b, preferred_element_type=F32).astype(BF16)


def flip(index, bit):
    return index + (1 - 2 * ((index // bit) % 2)) * bit


def chip_partner(rel):
    d = lax.axis_index("dp")
    for bit in (1, 2):
        if rel & bit:
            d = flip(d, 2 * bit)
    return {"dp": d}


def z_partner(rel):
    t = lax.axis_index("tensor")
    for bit in (1, 2):
        if rel & bit:
            t = flip(t, bit)
    return {"tensor": t}


def core_partner():
    return {"dp": flip(lax.axis_index("dp"), 1)}


def partner_of(axis, rel):
    if axis == "core":
        return core_partner()
    return chip_partner(rel) if axis == "dp" else z_partner(rel)


def xor(a, b):
    return sum(((a // bit + b // bit) % 2) * bit for bit in (1, 2))


def core_order(x):
    half = x.shape[-1] // 2
    turned = jnp.concatenate([x[..., half:], x[..., :half]], axis=-1)
    return jnp.where(lax.axis_index("dp") % 2 == 1, turned, x)


class Wire:
    def __init__(self, send, recv):
        self.send, self.recv, self.used = send, recv, 0

    def start(self, src, dst, partner):
        i = self.used
        self.used += 1
        copy = pltpu.make_async_remote_copy(
            src_ref=src,
            dst_ref=dst,
            send_sem=self.send.at[i],
            recv_sem=self.recv.at[i],
            device_id=partner,
            device_id_type=pl.DeviceIdType.MESH,
        )
        copy.start()
        return copy


TILE = 256


def over_tiles(width, body, *offsets):
    offsets = (0,) + (offsets or (0,))

    def step(i, carry):
        starts = [pl.multiple_of(offset + i * TILE, 128) for offset in offsets]
        body(*[pl.ds(start, TILE) for start in starts])
        return carry

    count = width // TILE
    lax.fori_loop(0, count, step, 0)
    if width % TILE:
        body(*[pl.ds(offset + count * TILE, width % TILE) for offset in offsets])


class RowPair:
    def __init__(self, own, other):
        self.args = (own, other)
        self.parts = own.shape[0] if own.ndim == 3 else 1
        self.half, self.cols = own.shape[-2:]
        self.shape = (2 * self.half, self.parts * self.cols)

    def whole(self):
        both = jnp.concatenate(self.args, axis=-2)
        return both if both.ndim == 2 else jnp.concatenate(list(both), axis=1)

    def pick(self, ref, part):
        return ref if self.parts == 1 else ref.at[part]

    def chunks(self, by_cols):
        if by_cols:
            return [(0, self.half), (self.half, self.half)]
        if self.parts > 1:
            return [(i * self.cols, self.cols) for i in range(self.parts)]
        low = self.cols // 2 // TILE * TILE
        return [(0, low), (low, self.cols - low)]

    def times(self, x, refs, by_cols, store, chunk):
        half, cols = self.half, self.cols
        start, width = self.chunks(by_cols)[chunk]
        if by_cols:
            ref = refs[chunk]

            def body(at, to):
                terms = [
                    fast(x(slice(i * cols, i * cols + cols)), self.pick(ref, i)[at, :], BY_COLS)
                    for i in range(self.parts)
                ]
                store(to, total(terms))

            over_tiles(width, body, start)
            return
        part, low = (chunk, 0) if self.parts > 1 else (0, start)

        def body(_, at, to):
            own, other = (self.pick(ref, part)[:, at] for ref in refs)
            left, right = x(slice(0, half)), x(slice(half, 2 * half))
            store(to, fast(left, own, PLAIN) + fast(right, other, PLAIN))

        over_tiles(width, body, low, start)


class ColPair:
    def __init__(self, own, other):
        self.args = (own, other)
        self.rows, self.half = own.shape
        self.shape = (self.rows, 2 * self.half)

    def whole(self):
        return jnp.concatenate(self.args, axis=1)

    def chunks(self, by_cols):
        width = self.rows // 2 if by_cols else self.half
        return [(0, width), (width, width)]

    def times(self, x, refs, by_cols, store, chunk):
        half = self.half
        start, width = self.chunks(by_cols)[chunk]
        if by_cols:
            own, other = refs

            def body(_, at):
                left, right = x(slice(0, half)), x(slice(half, 2 * half))
                store(at, fast(left, own[at, :], BY_COLS) + fast(right, other[at, :], BY_COLS))

            over_tiles(width, body, start)
            return
        ref = refs[chunk]

        def body(at, to):
            store(to, fast(x(slice(0, self.rows)), ref[:, at], PLAIN))

        over_tiles(width, body, start)


class ByChips:
    partners = [("dp", 1), ("dp", 2)]

    def __init__(self, x, w, by_cols, out_width, local, args, outs, scratch=()):
        self.by_cols, self.local, self.count = by_cols, local, len(args)
        self.rows = x.shape[1]
        self.width = w.shape[0] if by_cols else w.shape[1]
        self.w = w
        self.args = (x,) + w.args + tuple(args)
        self.outs = (jax.ShapeDtypeStruct((4, self.rows, out_width), BF16),) + tuple(outs)
        self.chunks = w.chunks(by_cols)
        self.copies = 6 * len(self.chunks) + 12
        self.scratch = chip_scratch(self.rows, self.width)
        self.scratch += [pltpu.VMEM((self.rows, self.width), F32)] + list(scratch)
        self.flops = 8 * self.rows * x.shape[2] * self.width

    def run(self, wire, args, outs, scratch):
        x, w = args[0], args[1:3]
        part, first, second, summed = scratch[:4]
        gathered = outs[0]
        rows = self.rows

        def dot(low, high, chunk):
            def left(at):
                return x[low:high, :, at].reshape((high - low) * rows, at.stop - at.start)

            def store(to, value):
                part[low:high, :, to] = value.astype(BF16).reshape(high - low, rows, value.shape[1])

            self.w.times(left, w, self.by_cols, store, chunk)

        yield from chip_sum(wire, part, first, second, summed, self.chunks, dot)
        self.local(summed, gathered.at[0], args[3:], outs[1:], scratch[4:])
        yield from chip_gather(wire, gathered)


def pieces(rows):
    half = rows // 2
    return [(p, slice(p * half, (p + 1) * half), 1 << p, 1 << (1 - p)) for p in range(2)]


def chip_sum(wire, part, first, second, summed, chunks, dot):
    halves = pieces(summed.shape[0])
    sent, later = {}, {}
    for n, (start, width) in enumerate(chunks):
        cols = slice(start, start + width)
        dot(1, 4, n)
        for p, at, bit, _ in halves:
            for i, rel in ((1, 3), (0, bit)):
                src, dst = part.at[rel, at, cols], first.at[p, i, :, cols]
                sent[n, p, i] = wire.start(src, dst, chip_partner(bit))
        yield
    for n in range(len(chunks)):
        dot(0, 1, n)
    for n, (start, width) in enumerate(chunks):
        cols = slice(start, start + width)
        for p, at, _, other in halves:
            sent[n, p, 1].wait_recv()

            def add(_, cols, p=p, at=at, other=other):
                both = part[other, at, cols].astype(F32) + first[p, 1, :, cols].astype(F32)
                part[other, at, cols] = both.astype(BF16)

            over_tiles(width, add, start)
            src, dst = part.at[other, at, cols], second.at[p, :, cols]
            later[n, p] = wire.start(src, dst, chip_partner(other))
        yield
    for n, (start, width) in enumerate(chunks):
        for p, at, _, _ in halves:
            sent[n, p, 0].wait_recv()
            later[n, p].wait_recv()

            def finish(_, cols, p=p, at=at):
                both = part[0, at, cols].astype(F32) + first[p, 0, :, cols].astype(F32)
                summed[at, cols] = both + second[p, :, cols].astype(F32)

            over_tiles(width, finish, start)
    for copy in list(sent.values()) + list(later.values()):
        copy.wait_send()


def chip_gather(wire, out):
    _, rows, width = out.shape
    low = width // 2 // 128 * 128
    ranges = [slice(0, low), slice(low, width)]
    near, far, last = {}, [], []
    for n, cols in enumerate(ranges):
        for p, at, bit, other in pieces(rows):
            src = out.at[0, at, cols]
            near[n, p] = wire.start(src, out.at[bit, at, cols], chip_partner(bit))
            far.append(wire.start(src, out.at[other, at, cols], chip_partner(other)))
    yield
    for n, cols in enumerate(ranges):
        for p, at, bit, other in pieces(rows):
            near[n, p].wait_recv()
            src, dst = out.at[bit, at, cols], out.at[3, at, cols]
            last.append(wire.start(src, dst, chip_partner(other)))
        yield
    for copy in far + last:
        copy.wait_recv()
    for copy in list(near.values()) + far + last:
        copy.wait_send()


def chip_scratch(rows, width):
    half = rows // 2
    return [
        pltpu.VMEM((4, rows, width), BF16),
        pltpu.VMEM((2, 2, half, width), BF16),
        pltpu.VMEM((2, half, width), BF16),
    ]


def tensor_sum(weight, x, w, by_cols, wire, scratch):
    part, first, second, summed = scratch
    rows, width = summed.shape
    r = rows // 4

    def left(at):
        return x[:, :, at].reshape(4 * rows, at.stop - at.start)

    def store(to, value):
        low = value.astype(BF16)
        for c in range(4):
            for z in range(4):
                part[z, c * r : (c + 1) * r, to] = low[c * rows + z * r : c * rows + z * r + r]

    half = width // 2
    halves = [slice(h * half, (h + 1) * half) for h in range(2)]
    sent, later = [], []
    for n, h in enumerate(halves):
        weight.times(left, w, by_cols, store, n)
        for i, z in ((1, 3), (0, 1)):
            sent.append(wire.start(part.at[z, :, h], first.at[i, :, h], z_partner(1)))
        yield
    for n, h in enumerate(halves):
        sent[2 * n].wait_recv()

        def add(_, cols):
            both = part[2, :, cols].astype(F32) + first[1, :, cols].astype(F32)
            part[2, :, cols] = both.astype(BF16)

        over_tiles(half, add, n * half)
        later.append(wire.start(part.at[2, :, h], second.at[:, h], z_partner(2)))
        yield
    for n in range(2):
        sent[2 * n + 1].wait_recv()
        later[n].wait_recv()

        def finish(_, cols):
            both = part[0, :, cols].astype(F32) + first[0, :, cols].astype(F32)
            summed[:, cols] = both + second[:, cols].astype(F32)

        over_tiles(half, finish, n * half)
    for copy in sent + later:
        copy.wait_send()


def sum_scratch(rows, width):
    return [
        pltpu.VMEM((4, rows, width), BF16),
        pltpu.VMEM((2, rows, width), BF16),
        pltpu.VMEM((rows, width), BF16),
        pltpu.VMEM((rows, width), F32),
    ]


def true_slots(ref):
    t = lax.axis_index("tensor")
    own = [ref.at[xor(t, rel)] for rel in range(4)]
    return own, [None, own[0], own[0], own[2]]


def tensor_gather(wire, slots, there=None):
    there = there or slots
    far = wire.start(slots[0], there[2], z_partner(2))
    near = wire.start(slots[0], there[1], z_partner(1))
    yield
    far.wait_recv()
    last = wire.start(slots[2], there[3], z_partner(1))
    yield
    near.wait_recv()
    last.wait_recv()
    for copy in (far, near, last):
        copy.wait_send()


class ByTensor:
    copies = 9
    partners = [("tensor", 1), ("tensor", 2), ("dp", 1), ("dp", 2), ("dp", 3)]

    def __init__(self, x, w, by_cols, local, args, outs, gather=True):
        self.by_cols, self.local, self.gather = by_cols, local, gather
        self.rows = x.shape[1]
        self.width = w.shape[0] if by_cols else w.shape[1]
        self.w = w
        self.args = (x,) + w.args + tuple(args)
        shape = (4, 4, self.rows // 4, self.width)
        self.outs = (jax.ShapeDtypeStruct(shape, BF16),) if gather else ()
        self.outs += tuple(outs)
        self.copies = 12 if gather else 9
        self.scratch = sum_scratch(self.rows, self.width)
        self.scratch += [pltpu.VMEM((4, self.rows, 128), F32)]
        self.flops = 8 * self.rows * x.shape[2] * self.width

    def run(self, wire, args, outs, scratch):
        summed, stats = scratch[3:5]
        rows = self.rows
        r = rows // 4
        yield from tensor_sum(self.w, args[0], args[1:3], self.by_cols, wire, scratch[:4])
        rest = outs[1:] if self.gather else outs[:1]
        local = self.local(summed, args[3:7], rest)
        stats[0] = jnp.broadcast_to(next(local), (rows, 128))
        sums = [
            wire.start(stats.at[0], stats.at[rel], chip_partner(rel)) for rel in range(1, 4)
        ]
        yield
        total_sums = stats[0]
        for rel in range(1, 4):
            sums[rel - 1].wait_recv()
            moved = [stats[rel, (i ^ rel) * r : (i ^ rel) * r + r, :] for i in range(4)]
            total_sums = total_sums + jnp.concatenate(moved, axis=0)
        low = local.send(total_sums[:, 0:1])
        if self.gather:
            gathered = outs[0]
            for c in range(4):
                gathered[c, 0] = low[c * r : (c + 1) * r]
            far = wire.start(gathered.at[:, 0], gathered.at[:, 2], z_partner(2))
            near = wire.start(gathered.at[:, 0], gathered.at[:, 1], z_partner(1))
            yield
            far.wait_recv()
            last = wire.start(gathered.at[:, 2], gathered.at[:, 3], z_partner(1))
            yield
            near.wait_recv()
            last.wait_recv()
            sums += [far, near, last]
        else:
            yield from self.tail(wire, low, args, outs, scratch)
        for copy in sums:
            copy.wait_send()


class Leave(ByTensor):
    def __init__(self, x, w, local, args, d_gain, theirs):
        super().__init__(x, w, True, local, args, (d_gain,), gather=False)
        r = self.rows // 4
        self.args += (theirs,)
        self.outs += (jax.ShapeDtypeStruct((4, r, 4 * self.width), BF16),)
        self.copies = 15
        self.scratch += [pltpu.VMEM((4, r, self.width), BF16)] * 2
        self.scratch += [pltpu.VMEM((r, 4 * self.width), BF16)]

    def tail(self, wire, low, args, outs, scratch):
        theirs, out = args[-1], outs[-1]
        mine, came, block_ref = scratch[5:]
        r, width = self.rows // 4, self.width
        half = width // 2
        d, t = lax.axis_index("dp"), lax.axis_index("tensor")
        for c in range(4):
            mine[c] = low[c * r : (c + 1) * r]
        sent = [
            wire.start(mine.at[rel], came.at[rel], chip_partner(rel)) for rel in range(1, 4)
        ]
        yield
        for rel in range(4):
            if rel:
                sent[rel - 1].wait_recv()
            block = (came if rel else mine)[rel].astype(F32)
            for j in range(2):
                at = 2 * xor(d // 2, rel) + (d + j) % 2
                at = pl.ds(pl.multiple_of(at * half, 128), half)
                low = block[:, j * half : (j + 1) * half] + theirs[:, at]
                block_ref[:, at] = low.astype(BF16)
        out[t] = block_ref[...]
        yield from tensor_gather(wire, *true_slots(out))
        for copy in sent:
            copy.wait_send()


class FeedOut:
    partners = [("tensor", 1), ("tensor", 2), ("dp", 1), ("dp", 2), ("dp", 3)]
    copies = 12

    def __init__(self, x, w, mid, proj):
        self.w = w
        self.rows, self.width = x.shape[1], w.shape[1]
        self.cols = proj.shape[3]
        r = self.rows // 4
        self.args = (x,) + w.args + (mid, proj)
        wide = 8 * self.cols
        self.outs = (
            jax.ShapeDtypeStruct((self.rows, self.width), BF16),
            jax.ShapeDtypeStruct((4, r, wide), BF16),
            jax.ShapeDtypeStruct((r, wide), BF16),
        )
        self.scratch = sum_scratch(self.rows, self.width)
        self.scratch += [pltpu.VMEM((4, r, wide), BF16)] * 2
        self.flops = 8 * self.rows * x.shape[2] * self.width

    def run(self, wire, args, outs, scratch):
        mid, proj = args[3:]
        block, gathered, own = outs
        summed, part, came = scratch[3:]
        r = self.rows // 4
        d = lax.axis_index("dp")
        yield from tensor_sum(self.w, args[0], args[1:3], False, wire, scratch[:4])
        block[...] = core_order((mid[...] + summed[...]).astype(BF16))
        for x in range(4):
            for y in range(2):
                at = 2 * xor(d // 2, x) + (d + y) % 2
                at = pl.ds(pl.multiple_of(at * self.cols, 128), self.cols)
                value = fast(block[...], proj[x, y], PLAIN).astype(BF16)
                part[:, :, at] = value.reshape(4, r, self.cols)
        sent = [
            wire.start(part.at[rel], came.at[rel], chip_partner(rel)) for rel in range(1, 4)
        ]
        yield
        shared = part[0].astype(F32)
        for rel in range(1, 4):
            sent[rel - 1].wait_recv()
            shared = shared + came[rel].astype(F32)
        own[...] = shared.astype(BF16)
        gathered[lax.axis_index("tensor")] = own[...]
        yield from tensor_gather(wire, *true_slots(gathered))
        for copy in sent:
            copy.wait_send()


class Settle:
    partners = [("tensor", 1), ("tensor", 2), ("dp", 1), ("dp", 2), ("dp", 3)]
    copies = 9

    def __init__(self, terms, bc, mamba_in, gain, grad, proj):
        self.args = (terms, bc, mamba_in, gain, grad, proj)
        r, wide = mamba_in.shape
        self.r, self.wide, self.cols = r, wide, proj.shape[3]
        states, width = terms.shape[2] - wide, proj.shape[2]
        self.outs = (
            jax.ShapeDtypeStruct((4, 4, r, width), BF16),
            jax.ShapeDtypeStruct((4, r, wide), BF16),
            jax.ShapeDtypeStruct((r, wide), F32),
            jax.ShapeDtypeStruct((r, states), BF16),
            jax.ShapeDtypeStruct((4 * r, width), F32),
            jax.ShapeDtypeStruct((1, wide), F32),
        )
        self.scratch = [
            pltpu.VMEM((2, r, terms.shape[2]), BF16),
            pltpu.VMEM((r, terms.shape[2]), BF16),
            pltpu.VMEM((r, terms.shape[2]), BF16),
        ]
        self.flops = 16 * r * wide * width

    def run(self, wire, args, outs, scratch):
        terms, bc, mamba_in, gain, grad, proj = args
        gathered, shared, d_mamba, state, d_block, d_gain = outs
        first, middle, second = scratch
        wide = self.wide
        d = lax.axis_index("dp")
        sent = [wire.start(terms.at[z], first.at[i], z_partner(1)) for i, z in ((1, 3), (0, 1))]
        yield
        sent[0].wait_recv()
        middle[...] = (terms[2].astype(F32) + first[1].astype(F32)).astype(BF16)
        sent.append(wire.start(middle, second, z_partner(2)))
        yield
        sent[1].wait_recv()
        sent[2].wait_recv()
        summed = terms[0].astype(F32) + first[0].astype(F32) + second[...].astype(F32)
        state[...] = summed[:, wide:].astype(BF16)
        dy = summed[:, :wide] + fast(state[...], bc[...], BY_COLS)
        v = mamba_in[...]
        inv = lax.rsqrt(jnp.mean(v * v, axis=1, keepdims=True) + EPSILON)
        scaled = dy * gain[...]
        inner = jnp.mean(scaled * v, axis=1, keepdims=True)
        d_gain[...] = jnp.sum(dy * v * inv, axis=0, keepdims=True)
        d_mamba[...] = inv * scaled - v * (inv * inv * inv * inner) + grad[...].astype(F32)
        shared[0] = d_mamba[...].astype(BF16)
        more = [
            wire.start(shared.at[0], shared.at[rel], chip_partner(rel)) for rel in range(1, 4)
        ]
        yield
        for copy in more:
            copy.wait_recv()
        result = None
        for x in range(4):
            for y in range(2):
                at = 2 * xor(d // 2, x) + (d + y) % 2
                at = pl.ds(pl.multiple_of(at * self.cols, 128), self.cols)
                left = shared[:, :, at].reshape(4 * self.r, self.cols)
                value = fast(left, proj[x, y], BY_COLS)
                result = value if result is None else result + value
        d_block[...] = core_order(result)
        for c in range(4):
            gathered[c, 0] = d_block[c * self.r : (c + 1) * self.r].astype(BF16)
        yield from tensor_gather(wire, [gathered.at[:, i] for i in range(4)])
        for copy in sent + more:
            copy.wait_send()


class Spread:
    every = 2

    partners = [("tensor", 1), ("tensor", 2), ("dp", 1), ("dp", 2), ("dp", 3), ("core", 1)]
    copies = 7
    flops = 0

    def __init__(self, w):
        self.args = (w,)
        self.outs = (jax.ShapeDtypeStruct((4, 2) + w.shape, BF16),)
        self.scratch = [pltpu.VMEM((4,) + w.shape, BF16)]

    def run(self, wire, args, outs, scratch):
        (out,), (rows,) = outs, scratch
        rows[0] = args[0][...]
        yield from tensor_gather(wire, [rows.at[i] for i in range(4)])
        here = xor(lax.axis_index("dp") // 2, lax.axis_index("tensor"))
        sent = [
            wire.start(rows.at[xor(here, rel)], out.at[rel, 0], chip_partner(rel))
            for rel in range(1, 4)
        ]
        out[0, 0] = rows[here]
        yield
        for copy in sent:
            copy.wait_recv()
        sent.append(wire.start(out.at[:, 0], out.at[:, 1], core_partner()))
        yield
        sent[3].wait_recv()
        for copy in sent:
            copy.wait_send()


class Collect:
    every = 2

    partners = Spread.partners
    copies = 7
    flops = 0

    def __init__(self, own, other):
        self.args = (own, other)
        shape = own.shape[1:]
        self.outs = (jax.ShapeDtypeStruct(shape, F32),)
        self.scratch = [pltpu.VMEM((4,) + shape, BF16)] * 3
        self.scratch += [pltpu.VMEM((2,) + shape, BF16), pltpu.VMEM(shape, BF16)]

    def run(self, wire, args, outs, scratch):
        own, other = args
        (out,) = outs
        swapped, mine, came, first, second = scratch
        rows = own.shape[1]
        tile = 128
        sent = [wire.start(other, swapped, core_partner())]
        yield
        sent[0].wait_recv()
        for rel in range(4):

            def add(i, carry, rel=rel):
                at = pl.ds(pl.multiple_of(i * tile, tile), tile)
                both = own[rel, at, :] + swapped[rel, at, :].astype(F32)
                (mine if rel else came)[rel, at, :] = both.astype(BF16)
                return carry

            lax.fori_loop(0, rows // tile, add, 0)
            if rel:
                sent.append(wire.start(mine.at[rel], came.at[rel], chip_partner(rel)))
        yield
        for copy in sent[1:]:
            copy.wait_recv()
        here = xor(lax.axis_index("dp") // 2, lax.axis_index("tensor"))
        at = [xor(here, z) for z in range(4)]
        more = [wire.start(came.at[at[z]], first.at[i], z_partner(1)) for i, z in ((1, 3), (0, 1))]
        yield
        more[0].wait_recv()

        def middle(i, carry):
            to = pl.ds(pl.multiple_of(i * tile, tile), tile)
            both = came[at[2], to, :].astype(F32) + first[1, to, :].astype(F32)
            swapped[0, to, :] = both.astype(BF16)
            return carry

        lax.fori_loop(0, rows // tile, middle, 0)
        more.append(wire.start(swapped.at[0], second, z_partner(2)))
        yield
        more[1].wait_recv()
        more[2].wait_recv()

        def finish(i, carry):
            to = pl.ds(pl.multiple_of(i * tile, tile), tile)
            both = came[at[0], to, :].astype(F32) + first[0, to, :].astype(F32)
            out[to, :] = both + second[to, :].astype(F32)
            return carry

        lax.fori_loop(0, rows // tile, finish, 0)
        for copy in sent + more:
            copy.wait_send()


class Outputs:
    partners = [("tensor", 1), ("tensor", 2)]
    copies = 6
    flops = 0

    def __init__(self, terms, base, valid):
        self.args = (terms, base, valid)
        self.outs = (jax.ShapeDtypeStruct(terms.shape, BF16),)
        shape = terms.shape[1:]
        self.scratch = [pltpu.VMEM((2,) + shape, BF16), pltpu.VMEM(shape, BF16)]
        self.scratch += [pltpu.VMEM(shape, BF16)]

    def run(self, wire, args, outs, scratch):
        terms, base, valid = args
        (gathered,) = outs
        first, middle, second = scratch
        sent = [wire.start(terms.at[z], first.at[i], z_partner(1)) for i, z in ((1, 3), (0, 1))]
        yield
        sent[0].wait_recv()
        middle[...] = (terms[2].astype(F32) + first[1].astype(F32)).astype(BF16)
        sent.append(wire.start(middle, second, z_partner(2)))
        yield
        sent[1].wait_recv()
        sent[2].wait_recv()
        summed = terms[0].astype(F32) + first[0].astype(F32) + second[...].astype(F32)
        gathered[lax.axis_index("tensor")] = ((base[...] + summed) * valid[...]).astype(BF16)
        yield from tensor_gather(wire, *true_slots(gathered))
        for copy in sent:
            copy.wait_send()


class SmallSum:
    partners = [("tensor", 1), ("tensor", 2), ("tensor", 3)]
    partners += [("dp", 1), ("dp", 2), ("dp", 3), ("core", 1)]
    copies = 7
    flops = 0

    def __init__(self, x, rows_all):
        self.args, self.rows_all = (x,), rows_all
        self.outs = (jax.ShapeDtypeStruct(x.shape, F32),)
        self.scratch = [pltpu.VMEM(x.shape, F32)] * 3
        self.scratch += [pltpu.VMEM((3,) + x.shape, F32), pltpu.VMEM((3, rows_all, 128), F32)]

    def run(self, wire, args, outs, scratch):
        (x,), (out,) = args, outs
        from_core, mine, whole, from_chips, from_z = scratch
        top = slice(0, self.rows_all)
        swap = wire.start(x, from_core, core_partner())
        yield
        swap.wait_recv()
        mine[...] = x[...] + from_core[...]
        sent = [
            wire.start(mine, from_chips.at[rel - 1], chip_partner(rel)) for rel in range(1, 4)
        ]
        yield
        for copy in sent:
            copy.wait_recv()
        whole[...] = total([mine[...]] + [from_chips[i] for i in range(3)])
        more = [
            wire.start(whole.at[top], from_z.at[rel - 1], z_partner(rel)) for rel in range(1, 4)
        ]
        yield
        for copy in more:
            copy.wait_recv()
        out[...] = whole[...]
        out[top] = total([whole[top]] + [from_z[i] for i in range(3)])
        for copy in [swap] + sent + more:
            copy.wait_send()


class Enter:
    partners = [("dp", 1), ("dp", 2), ("dp", 3)]
    copies = 9
    flops = 0

    def __init__(self, hid, emb, gain):
        self.args = (hid, emb, gain)
        self.rows, self.half = hid.shape[0], gain.shape[1] // 2
        rows, width = self.rows, gain.shape[1]
        self.outs = (
            jax.ShapeDtypeStruct((4, rows, width), BF16),
            jax.ShapeDtypeStruct((rows, width), F32),
            jax.ShapeDtypeStruct((rows, 1), F32),
        )
        self.scratch = [
            pltpu.VMEM((rows, 4 * width), BF16),
            pltpu.VMEM((4, rows, width), BF16),
            pltpu.VMEM((4, rows, 128), F32),
        ]

    def run(self, wire, args, outs, scratch):
        hid, emb, gain = args
        attn_in, joined_z, inv_z = outs
        joined, came, stats = scratch
        rows, half = self.rows, self.half
        r, wide = rows // 4, hid.shape[1]
        d, t = lax.axis_index("dp"), lax.axis_index("tensor")
        for i in range(4):
            at = pl.ds(pl.multiple_of(xor(t, i) * r, r), r)
            to = slice(i * r, (i + 1) * r)
            left, right = hid[at, :], emb[at, :]
            joined[to, :wide] = left
            joined[to, wide:] = right
            left, right = left.astype(F32), right.astype(F32)
            squares = jnp.sum(left * left, axis=1, keepdims=True)
            squares = squares + jnp.sum(right * right, axis=1, keepdims=True)
            inverse = lax.rsqrt(squares / (2 * wide) + EPSILON)
            stats[0, to, :] = jnp.broadcast_to(inverse, (r, 128))
        sent = []
        for rel in (3, 1, 2):
            sent.append(wire.start(stats.at[0], stats.at[rel], chip_partner(rel)))
        for rel in (3, 1, 2, 0):
            for j in range(2):
                at = 2 * xor(d // 2, rel) + (d + j) % 2
                at = pl.ds(pl.multiple_of(at * half, 128), half)
                to = slice(j * half, (j + 1) * half)
                if rel:
                    src, dst = joined.at[:, at], came.at[rel, :, to]
                    sent.append(wire.start(src, dst, chip_partner(rel)))
                else:
                    came[0, :, to] = joined[:, at]
        yield
        for copy in sent:
            copy.wait_recv()
        for c in range(4):
            block = came[c].astype(F32)
            inverse = stats[c][:, 0:1]
            attn_in[c] = (block * inverse * gain[...]).astype(BF16)
            joined_z[c * r : (c + 1) * r] = block[:r]
            inv_z[c * r : (c + 1) * r] = inverse[:r]
        for copy in sent:
            copy.wait_send()


class WeightGrad:
    partners = [("core", 1)]
    copies = 1

    def __init__(self, a, b, by_rows, parts=1):
        self.count, self.by_rows, self.parts = len(a), by_rows, parts
        self.args = tuple(a) + tuple(b)
        self.height, self.width = a[0].shape[2], b[0].shape[2]
        if by_rows:
            self.height //= 2
        else:
            self.width //= 2
        self.cols = self.width // parts
        shape = (self.height, self.cols)
        shape = (parts,) + shape if parts > 1 else shape
        self.outs = (jax.ShapeDtypeStruct(shape, F32),)
        self.step = min(self.height, 512)
        self.scratch = [pltpu.VMEM(shape, BF16)] * 2
        self.scratch += [pltpu.VMEM((self.count, self.step, 4 * a[0].shape[1]), BF16)]
        self.flops = 4 * self.count * a[0].shape[1] * self.height * self.width * 2

    def run(self, wire, args, outs, scratch):
        (out,) = outs
        other, got, turned = scratch
        a, b = args[: self.count], args[self.count :]
        step = self.step
        tokens = 4 * a[0].shape[1]

        def work(half, ref):
            row, col = (half * self.height, 0) if self.by_rows else (0, half * self.width)
            for low in range(0, self.height, step):
                rows = slice(row + low, row + low + step)
                for i, x in enumerate(a):
                    turned[i] = x[:, :, rows].reshape(tokens, step).T
                for part in range(self.parts):
                    to_ref = ref if self.parts == 1 else ref.at[part]

                    def body(to, at, low=low, to_ref=to_ref):
                        terms = [
                            fast(turned[i], y[:, :, at].reshape(tokens, at.size), PLAIN)
                            for i, y in enumerate(b)
                        ]
                        to_ref[low : low + step, to] = total(terms).astype(to_ref.dtype)

                    over_tiles(self.cols, body, col + part * self.cols)
                    yield

        yield
        yield from work(1, other)
        swap = wire.start(other, got, core_partner())
        yield from work(0, out)
        swap.wait_recv()
        for part in range(self.parts):
            to_ref, got_ref = (out, got) if self.parts == 1 else (out.at[part], got.at[part])

            def add(cols, _, to_ref=to_ref, got_ref=got_ref):
                to_ref[:, cols] += got_ref[:, cols].astype(F32)

            over_tiles(self.cols, add)
        swap.wait_send()


def together(groups, collective_id):
    partners = sorted({p for g in groups for p in g.partners})

    def kernel(*refs):
        refs = list(refs)

        def take(count):
            got = refs[:count]
            del refs[:count]
            return got

        args = [take(len(g.args)) for g in groups]
        outs = [take(len(g.outs)) for g in groups]
        scratch = [take(len(g.scratch)) for g in groups]
        wires = [Wire(*take(2)) for g in groups]
        barrier = pltpu.get_barrier_semaphore()
        for axis, rel in partners:
            pl.semaphore_signal(
                barrier,
                inc=1,
                device_id=partner_of(axis, rel),
                device_id_type=pl.DeviceIdType.MESH,
            )
        pl.semaphore_wait(barrier, len(partners))
        running = [
            (g, g.run(wire, a, o, s))
            for g, wire, a, o, s in zip(groups, wires, args, outs, scratch)
        ]
        turn = 0
        while running:
            left = []
            slow_alone = all(getattr(g, "every", 1) > 1 for g, _ in running)
            for g, run in running:
                waits = turn % getattr(g, "every", 1) and not slow_alone
                if waits or next(run, running) is not running:
                    left.append((g, run))
            running = left
            turn += 1

    args = [x for g in groups for x in g.args]
    outs = [x for g in groups for x in g.outs]
    scratch = [x for g in groups for x in g.scratch]
    for g in groups:
        scratch += [pltpu.SemaphoreType.DMA((g.copies,))] * 2
    size = sum(x.size * x.dtype.itemsize for x in args + outs)
    flat = pl.pallas_call(
        kernel,
        out_shape=outs,
        in_specs=[pl.BlockSpec(memory_space=pltpu.VMEM)] * len(args),
        out_specs=[pl.BlockSpec(memory_space=pltpu.VMEM)] * len(outs),
        scratch_shapes=scratch,
        compiler_params=pltpu.CompilerParams(
            collective_id=collective_id, has_side_effects=True, vmem_limit_bytes=62 * 2**20
        ),
        cost_estimate=pl.CostEstimate(
            flops=sum(g.flops for g in groups), bytes_accessed=size, transcendentals=0
        ),
    )(*args)
    results = []
    for g in groups:
        results.append(flat[: len(g.outs)])
        flat = flat[len(g.outs) :]
    return results


def attend_local(qkv, slot, args, outs, scratch):
    cos, sin, allowed = args
    attend_kernel(qkv, cos, sin, allowed, outs[0], slot)


def attend_back_local(d_attended, slot, args, outs, scratch):
    low, cos, sin, allowed = args
    attend_back_kernel(low, d_attended, cos, sin, allowed, slot)


GELU_SCALE = (2.0 / 3.141592653589793) ** 0.5


def feed_local(summed, slot, args, outs, scratch):
    (up,) = args
    gate_up, adapter = outs
    units = slot.shape[1]
    low = summed[:, 2 * units :].astype(BF16)
    adapter[...] = low

    def widen(cols, _):
        gate_up[:, cols] = summed[:, cols] + fast(low, up[:, cols], PLAIN)

    over_tiles(2 * units, widen)
    tile = 256

    def act(i, carry):
        at = pl.ds(pl.multiple_of(i * tile, 128), tile)
        also = pl.ds(pl.multiple_of(units + i * tile, 128), tile)
        v = gate_up[:, at]
        bent = jnp.tanh(GELU_SCALE * (v + 0.044715 * (v * v * v)))
        slot[:, at] = (0.5 * v * (1.0 + bent) * gate_up[:, also]).astype(BF16)
        return carry

    lax.fori_loop(0, units // tile, act, 0)


def feed_back_local(d_hidden, slot, args, outs, scratch):
    gate_up, up = args
    (adapter,) = scratch
    units = d_hidden.shape[1]
    tile = 256
    adapter[...] = jnp.zeros(adapter.shape, F32)

    def act(i, carry):
        at = pl.ds(pl.multiple_of(i * tile, 128), tile)
        also = pl.ds(pl.multiple_of(units + i * tile, 128), tile)
        v, u, d = gate_up[:, at], gate_up[:, also], d_hidden[:, at]
        bent = jnp.tanh(GELU_SCALE * (v + 0.044715 * (v * v * v)))
        slope = 0.5 * (1.0 + bent) + 0.5 * v * (1.0 - bent * bent) * GELU_SCALE * (
            1.0 + 3.0 * 0.044715 * (v * v)
        )
        d_gate = (d * u * slope).astype(BF16)
        d_up = (d * (0.5 * v * (1.0 + bent))).astype(BF16)
        slot[:, at] = d_gate
        slot[:, also] = d_up
        adapter[...] += fast(d_gate, up[:, at], BY_COLS) + fast(d_up, up[:, also], BY_COLS)
        return carry

    lax.fori_loop(0, units // tile, act, 0)
    slot[:, 2 * units :] = adapter[...].astype(BF16)


def norm_local(width, summed, args, outs):
    base, gain = args
    mid, inverse = outs
    value = base[...] + summed[...]
    mid[...] = value
    squares = yield jnp.sum(value * value, axis=1, keepdims=True)
    inv = lax.rsqrt(squares / width + EPSILON)
    inverse[...] = inv
    yield (value * inv * gain[...]).astype(BF16)


def norm_back_local(width, summed, args, outs):
    value, inverse, gain, skip = args
    d_gain = outs[-1]
    dy = summed[...]
    scaled = dy * gain[...]
    v, inv = value[...], inverse[...]
    weighted = yield jnp.sum(scaled * v, axis=1, keepdims=True)
    d_gain[...] = jnp.sum(dy * v * inv, axis=0, keepdims=True)
    result = scaled * inv - v * (inv * inv * inv * weighted / width) + skip[...]
    if len(outs) == 2:
        outs[0][...] = result
    yield result.astype(BF16)


def proj_spread(links, w):
    rows = links.z_ag(w, 0)
    if links.chips == links.n_t:
        blocks = [
            lax.dynamic_index_in_dim(rows, links.chip ^ links.t ^ rel, 0, keepdims=False)
            for rel in range(links.chips)
        ]
    else:
        rows = links.by_index(rows, 0, links.t).reshape(links.chips, -1, w.shape[1])
        blocks = [
            lax.dynamic_index_in_dim(rows, links.chip ^ rel, 0, keepdims=False)
            for rel in range(links.chips)
        ]
    came = jnp.stack(links.chip_a2a(blocks), 0)
    return jnp.stack([came, links.core_swap(came)], 1)


def proj_collect(links, own, other):
    mine = (own + links.core_swap(other).astype(F32)).astype(BF16)
    blocks = [mine[rel] for rel in range(links.chips)]
    rows = jnp.stack(links.chip_a2a(blocks), 0)
    if links.chips == links.n_t:
        rows = links.by_index(rows, 0, links.chip ^ links.t)
    else:
        rows = links.by_index(rows, 0, links.chip).reshape(links.n_t, -1, own.shape[2])
        rows = links.by_index(rows, 0, links.t)
    return links.z_rs(rows, 0)


def core_halves(links, x):
    split = x.reshape(x.shape[:-1] + (2, x.shape[-1] // 2))
    return links.by_index(split, x.ndim - 1, links.core).reshape(x.shape)


def enter(links, w, m):
    rows = m.hid.shape[0]
    joined = links.rows_by_t(jnp.concatenate([m.hid, m.emb], axis=1))
    wide = joined.astype(F32)
    m.inverse = lax.rsqrt(jnp.mean(wide * wide, axis=1) + EPSILON)
    half = joined.shape[1] // links.n_dp
    blocks = []
    for rel in range(links.chips):
        at = 2 * (links.chip ^ rel)
        pieces = [
            lax.dynamic_slice_in_dim(joined, (at + (links.core ^ j)) * half, half, axis=1)
            for j in range(2)
        ]
        blocks.append(jnp.concatenate(pieces, axis=1))
    m.joined = jnp.stack(links.chip_a2a(blocks), 0)
    places = jnp.arange(rows, dtype=jnp.int32)
    m.true = layout(m.lens, places)
    _, position, _, allowed = layout(m.lens, links.rows_by_t(places))
    m.allowed_rel = allowed.astype(F32)
    m.cos, m.sin = rope_tables(position)


def attend(links, w, m):
    wide = m.joined.astype(F32) * m.inv_attn[:, :, None]
    m.attn_in = lax.optimization_barrier((wide * w.g_attn).astype(BF16))
    qkv = links.chip_rs(dotl("crd,dn->crn", m.attn_in, w.qkv), 0)
    rows, width = qkv.shape[0], qkv.shape[1] // 3
    outs = (
        jax.ShapeDtypeStruct((rows, 3 * width), BF16),
        jax.ShapeDtypeStruct((rows, width), BF16),
    )
    args = (qkv, m.cos, m.sin, m.allowed_rel)
    m.qkv_low, attended = in_vmem(attend_kernel, outs, args, 4 * rows * rows * width)
    m.attended = links.chip_ag(attended, 0, direct=True)


def z_split(links, x, axis):
    rows = x.shape[axis]
    return x.reshape(x.shape[:axis] + (links.n_t, rows // links.n_t) + x.shape[axis + 1 :])


def z_join(x, axis):
    return x.reshape(x.shape[:axis] + (-1,) + x.shape[axis + 2 :])


def attend_out(links, w, m):
    part = dotl("crn,nd->crd", m.attended, w.out)
    summed = links.z_rs(z_split(links, part, 1), 1)
    rows = summed.shape[1]
    m.joined_z = m.joined[:, :rows].astype(F32)
    m.inv_attn_z = m.inv_attn[:, :rows]
    mid = m.joined_z + summed
    m.mid = mid
    squares = links.chip_sum(jnp.sum(mid * mid, axis=2))
    width = mid.shape[2] * links.chips
    m.inv_mlp = lax.rsqrt(squares / width + EPSILON)
    low = (mid * m.inv_mlp[:, :, None] * w.g_mlp).astype(BF16)
    m.mlp_in = z_join(links.z_ag(low, 1), 1)


def feed(links, w, m):
    summed = links.chip_rs(dotl("crd,dn->crn", m.mlp_in, w.gate_up), 0)
    units = 2 * w.down.shape[0]
    m.adapter = summed[:, units:].astype(BF16)
    gate_up = summed[:, :units] + dotf("ra,an->rn", m.adapter, w.adapter_up)
    activated, m.gate_back = jax.vjp(gated_gelu, gate_up)
    m.hidden = links.chip_ag(activated.astype(BF16), 0, direct=True)


def feed_out(links, w, m):
    part = dotl("crn,nd->crd", m.hidden, w.down)
    summed = links.z_rs(z_split(links, part, 1), 1)
    m.block = (m.mid + summed).astype(BF16)
    m.block = core_halves(links, m.block)
    part = dotl("crd,xydn->xycrn", m.block, w.proj)
    part = links.by_index(links.by_index(part, 1, links.core), 0, links.chip)
    part = z_join(part, 0).transpose(1, 2, 0, 3)
    part = part.reshape(part.shape[:2] + (-1,))
    shared = links.chip_rs(part, 0, direct=True).astype(BF16)
    whole = links.by_index(links.z_ag(shared, 0), 0, links.t)
    shared_full = whole.reshape(-1, whole.shape[2])
    m.mamba_in = m.hid.astype(F32) + shared_full.astype(F32)
    own = z_split(links, m.hid, 0)
    own = lax.dynamic_index_in_dim(own, links.t, 0, keepdims=False)
    m.mamba_in_z = own.astype(F32) + shared.astype(F32)


def mix(links, w, m):
    taps_x, taps_bc, step_bias, decay_log, skip, gate_gain = w.smalls
    segment, _, valid, allowed = m.true
    mamba_in = m.mamba_in
    inverse = lax.rsqrt(jnp.mean(mamba_in * mamba_in, axis=1, keepdims=True) + EPSILON)
    ssm_in = (mamba_in * inverse * w.g_mamba).astype(BF16)
    gate_x = dotf("td,kdc->ktc", ssm_in, w.w_in)
    state_io = dotf("td,dn->tn", ssm_in, w.bc)
    step_raw = dotf("td,dn->tn", ssm_in, w.dt)
    grad_low = m.cot * valid[:, None].astype(BF16)
    d_norm = dotf("tn,in->ti", grad_low, w.mout)
    d_scaled = d_norm * gate_gain
    rows, width = gate_x.shape[1:]
    heads = step_raw.shape[1]
    earlier = [jnp.pad(segment, (j, 0), constant_values=-1)[:rows] for j in range(taps_x.shape[0])]
    same = jnp.stack([(e == segment).astype(F32) for e in earlier], 1)
    skips = jnp.repeat(skip, width // heads)[None, :]
    args = (gate_x, state_io, step_raw, taps_x, taps_bc, step_bias[None, :], decay_log[None, :])
    args += (skips, same, allowed.astype(F32), d_scaled)
    outs = (jax.ShapeDtypeStruct((rows, width), F32), jax.ShapeDtypeStruct((rows, 2), F32))
    gated, sums = in_vmem(mix_kernel, outs, args, 4 * rows * rows * width)
    inner = width * links.n_t
    sums = links.z_sum(sums)
    squares, weighted = sums[:, 0], sums[:, 1]
    row_scale = lax.rsqrt(squares / inner + EPSILON)
    m.gated_norm = (gated * row_scale[:, None] * gate_gain).astype(BF16)
    m.mamba_out = dotl("ti,in->tn", m.gated_norm, w.mout)

    grad_gain = jnp.sum(d_norm * gated * row_scale[:, None], axis=0)
    scales = jnp.stack([row_scale, row_scale**3 * weighted / inner], 1)
    outs = (
        jax.ShapeDtypeStruct(gate_x.shape, BF16),
        jax.ShapeDtypeStruct(state_io.shape, BF16),
        jax.ShapeDtypeStruct(step_raw.shape, F32),
        jax.ShapeDtypeStruct(taps_x.shape, F32),
        jax.ShapeDtypeStruct(taps_bc.shape, F32),
        jax.ShapeDtypeStruct((1, heads), F32),
        jax.ShapeDtypeStruct((1, heads), F32),
        jax.ShapeDtypeStruct((1, width), F32),
    )
    args += (gated, scales)
    grads = in_vmem(mix_back_kernel, outs, args, 16 * rows * rows * width)
    m.gate_x_low, d_state_io, d_step, d_taps_x, d_taps_bc, d_bias, d_decay, d_skip = grads
    d_skip = jnp.sum(d_skip.reshape(heads, width // heads), axis=1)
    m.step_low = d_step.astype(BF16)
    part_in = dotf("ktc,kdc->td", m.gate_x_low, w.w_in) + dotf("tn,dn->td", m.step_low, w.dt)
    terms = jnp.concatenate([part_in.astype(BF16), d_state_io], axis=1)
    m.terms = z_split(links, links.rows_by_t(terms), 0)
    m.ssm_in = ssm_in
    m.ssm_in_z = own_rows(links, ssm_in)
    m.grad_low = grad_low
    m.sums_dp = (d_taps_x, grad_gain, d_bias[0], d_decay[0], d_skip)
    m.d_taps_bc = d_taps_bc


def settle(links, w, m):
    summed = links.z_rs(m.terms, 0)
    model_width = m.mamba_in_z.shape[1]
    m.state_low = summed[:, model_width:].astype(BF16)
    dy = summed[:, :model_width] + dotf("tn,dn->td", m.state_low, w.bc)
    v = m.mamba_in_z
    inv = lax.rsqrt(jnp.mean(v * v, axis=1, keepdims=True) + EPSILON)
    scaled = dy * w.g_mamba
    dv = inv * scaled - v * (inv**3 * jnp.mean(scaled * v, axis=1, keepdims=True))
    grad_g_mamba = jnp.sum(dy * v * inv, axis=0)
    m.sums_all = (m.d_taps_bc, grad_g_mamba)
    m.d_mamba = dv + own_rows(links, m.grad_low).astype(F32)
    m.shared_low = links.chip_ag(m.d_mamba.astype(BF16), 0, direct=True)
    split = m.shared_low.reshape(m.shared_low.shape[:2] + w.proj.shape[:2] + (-1,))
    m.shared_cols = links.by_index(links.by_index(split, 3, links.core), 2, links.chip)
    d_block = core_halves(links, dotf("crxyn,xydn->crd", m.shared_cols, w.proj))
    m.d_block = d_block
    m.mlp_low = z_join(links.z_ag(d_block.astype(BF16), 1), 1)


def own_rows(links, x):
    return lax.dynamic_index_in_dim(z_split(links, x, 0), links.t, 0, keepdims=False)


def finish_output(links, micro):
    terms = jnp.stack([z_split(links, links.rows_by_t(m.mamba_out), 0) for m in micro], 0)
    summed = links.z_rs(terms, 1)
    base = jnp.stack([m.mamba_in_z for m in micro], 0)
    valid = jnp.stack([own_rows(links, m.true[2]) for m in micro], 0)
    low = ((base + summed) * valid[:, :, None].astype(F32)).astype(BF16)
    whole = links.by_index(links.z_ag(low, 1), 1, links.t)
    return z_join(whole, 1)


def feed_back(links, w, m):
    part = dotl("crd,nd->crn", m.mlp_low, w.down)
    d_hidden = links.chip_rs(part, 0)
    (d_gate_up,) = m.gate_back(d_hidden)
    m.gate_up_own = d_gate_up.astype(BF16)
    part = dotl("rn,an->ra", m.gate_up_own, w.adapter_up)
    m.gate_up_low = links.chip_ag(jnp.concatenate([m.gate_up_own, part], 1), 0)


def feed_back_out(links, w, m):
    part = dotl("crn,dn->crd", m.gate_up_low, w.gate_up)
    dy = links.z_rs(z_split(links, part, 1), 1)
    scaled = dy * w.g_mlp
    v, inv = m.mid, m.inv_mlp
    weighted = links.chip_sum(jnp.sum(scaled * v, axis=2))
    width = v.shape[2] * links.chips
    dv = scaled * inv[:, :, None] - v * (inv**3 * weighted / width)[:, :, None]
    m.grad_g_mlp = jnp.sum(dy * v * inv[:, :, None], axis=(0, 1))
    m.d_mid = dv + m.d_block
    m.attn_low = z_join(links.z_ag(m.d_mid.astype(BF16), 1), 1)


def attend_back(links, w, m):
    part = dotl("crd,nd->crn", m.attn_low, w.out)
    d_attended = links.chip_rs(part, 0, direct=True)
    rows, width = d_attended.shape
    outs = (jax.ShapeDtypeStruct((rows, 3 * width), BF16),)
    args = (m.qkv_low, d_attended, m.cos, m.sin, m.allowed_rel)
    (d_qkv,) = in_vmem(attend_back_kernel, outs, args, 10 * rows * rows * width)
    m.d_qkv = links.chip_ag(d_qkv, 0)


def leave(links, w, m):
    part = dotl("crn,dn->crd", m.d_qkv, w.qkv)
    dy = links.z_rs(z_split(links, part, 1), 1)
    scaled = dy * w.g_attn
    v, inv = m.joined_z, m.inv_attn_z
    weighted = links.chip_sum(jnp.sum(scaled * v, axis=2))
    width = v.shape[2] * links.chips
    dv = scaled * inv[:, :, None] - v * (inv**3 * weighted / width)[:, :, None]
    m.grad_g_attn = jnp.sum(dy * v * inv[:, :, None], axis=(0, 1))
    m.d_joined = (dv + m.d_mid).astype(BF16)
    leave_rows(links, m)


def leave_rows(links, m):
    d_joined = m.d_joined.reshape(links.chips, -1, m.d_joined.shape[-1])
    came = jnp.stack(links.chip_a2a([d_joined[rel] for rel in range(links.chips)]), 0)
    rows = came.shape[1]
    came = came.reshape(links.chips, rows, 2, -1)
    came = links.by_index(links.by_index(came, 2, links.core), 0, links.chip)
    came = came.transpose(1, 0, 2, 3).reshape(rows, -1)
    model_width = m.d_mamba.shape[1]
    d_hid = (came[:, :model_width].astype(F32) + m.d_mamba).astype(BF16)
    both = jnp.concatenate([d_hid, came[:, model_width:]], axis=1)
    whole = links.by_index(links.z_ag(both, 0), 0, links.t)
    whole = whole.reshape(-1, both.shape[1])
    m.d_hid, m.d_emb = whole[:, :model_width], whole[:, model_width:]


def sds(shape, dtype=F32):
    return jax.ShapeDtypeStruct(shape, dtype)


def mixer_rows(links, m):
    whole = m.shared_all.reshape(-1, m.shared_all.shape[2])
    m.mamba_in = m.hid.astype(F32) + whole.astype(F32)
    m.mamba_in_z = own_rows(links, m.hid).astype(F32) + m.shared_z.astype(F32)


def projection_grads(links, micro):
    block = jnp.concatenate([m.block for m in micro], axis=0)
    low = jnp.concatenate([m.shared_low for m in micro], axis=0)
    cols = links.dp_order(low, 2).reshape(low.shape[:2] + (links.chips, 2, -1))
    spec = "crd,crxn->xdn"
    return dotf(spec, block, cols[:, :, :, 0]), dotl(spec, block, cols[:, :, :, 1])


def enter_group(links, w, m):
    rows = m.hid.shape[0]
    places = jnp.arange(rows, dtype=jnp.int32)
    m.true = layout(m.lens, places)
    _, position, _, allowed = layout(m.lens, links.rows_by_t(places))
    m.allowed_rel = allowed.astype(F32)
    m.cos, m.sin = rope_tables(position)
    return Enter(m.hid, m.emb, w.g_attn[None, :])


def take_enter(m, got):
    m.attn_in, m.joined_z, m.inv_attn_z = got


def attend_group(links, w, m):
    rows, width = m.attn_in.shape[1], w.qkv_pair.shape[1]
    args = (m.cos, m.sin, m.allowed_rel)
    outs = (sds((rows, width), BF16),)
    return ByChips(m.attn_in, w.qkv_pair, False, width // 3, attend_local, args, outs)


def attend_out_group(links, w, m):
    width = m.joined_z.shape[1]
    outs = (sds(m.joined_z.shape), sds(m.inv_attn_z.shape))
    args = (m.joined_z, w.g_mlp[None, :])
    work = partial(norm_local, width * links.chips)
    return ByTensor(m.attended, w.out_pair, False, work, args, outs)


def feed_group(links, w, m):
    rows, units = m.mlp_in.shape[1], w.down_pair.shape[0]
    outs = (sds((rows, 2 * units)), sds((rows, w.gate_up_pair.shape[1] - 2 * units), BF16))
    args = (w.adapter_up,)
    return ByChips(m.mlp_in, w.gate_up_pair, False, units, feed_local, args, outs)


def feed_back_group(links, w, m):
    args = (m.gate_up, w.adapter_up)
    rank = w.gate_up_pair.shape[1] - m.gate_up.shape[1]
    scratch = (pltpu.VMEM((m.gate_up.shape[0], rank), F32),)
    width = w.gate_up_pair.shape[1]
    return ByChips(m.mlp_low, w.down_pair, True, width, feed_back_local, args, (), scratch)


def feed_back_out_group(links, w, m):
    width = m.mid_z.shape[1]
    args = (m.mid_z, m.inv_mlp, w.g_mlp[None, :], m.d_block.reshape(m.mid_z.shape))
    outs = (sds(m.mid_z.shape), sds((1, width)))
    work = partial(norm_back_local, width * links.chips)
    return ByTensor(m.gate_up_low, w.gate_up_pair, True, work, args, outs)


def attend_back_group(links, w, m):
    args = (m.qkv_low, m.cos, m.sin, m.allowed_rel)
    width = w.qkv_pair.shape[1]
    return ByChips(m.attn_low, w.out_pair, True, width, attend_back_local, args, ())


def leave_group(links, w, m):
    width = m.joined_z.shape[1]
    args = (m.joined_z, m.inv_attn_z, w.g_attn[None, :], m.d_mid)
    work = partial(norm_back_local, width * links.chips)
    theirs = jnp.concatenate([m.d_mamba, jnp.zeros_like(m.d_mamba)], axis=1)
    return Leave(m.d_qkv, w.qkv_pair, work, args, sds((1, width)), theirs)


def feed_out_group(links, w, m):
    return FeedOut(m.hidden, w.down_pair, m.mid_z, w.proj)


def settle_group(links, w, m):
    grad = own_rows(links, m.grad_low)
    return Settle(m.terms, w.bc, m.mamba_in_z, w.g_mamba[None, :], grad, w.proj)


def spread_group(links, w, m):
    return Spread(w.proj_own)


def outputs_group(links, w, micro):
    terms = [z_split(links, links.rows_by_t(m.mamba_out), 0) for m in micro]
    base = [m.mamba_in_z for m in micro]
    valid = [own_rows(links, m.true[2])[:, None].astype(F32) for m in micro]
    args = (jnp.concatenate(terms, 1), jnp.concatenate(base, 0), jnp.concatenate(valid, 0))
    return Outputs(*args)


def take_feed_out(m, got):
    m.block, m.shared_all, m.shared_z = got
    m.block = m.block.reshape(4, -1, m.block.shape[1])


def take_settle(m, got):
    gathered, m.shared_low, m.d_mamba, m.state_low, d_block, d_gain = got
    m.mlp_low = z_join(gathered, 1)
    m.d_block = d_block
    m.sums_all = (m.d_taps_bc, d_gain[0])


def take_attend(m, got):
    m.attended, m.qkv_low = got


def take_attend_out(m, got):
    gathered, m.mid_z, m.inv_mlp = got
    m.mlp_in = z_join(gathered, 1)
    m.mid = m.mid_z.reshape(gathered.shape[0], -1, gathered.shape[3])


def take_feed(m, got):
    m.hidden, m.gate_up, m.adapter = got


def take_feed_back(m, got):
    (m.gate_up_low,) = got
    m.gate_up_own = m.gate_up_low[0, :, : m.gate_up.shape[1]]


def take_feed_back_out(m, got):
    gathered, m.d_mid, d_gain = got
    m.attn_low = z_join(gathered, 1)
    m.grad_g_mlp = d_gain[0]


def take_attend_back(m, got):
    (m.d_qkv,) = got


def take_leave(m, got):
    d_gain, m.left = got
    m.grad_g_attn = d_gain[0]


def fused(links, w, number, *work):
    groups = [make(links, w, m) for make, _, m in work]
    for (_, taker, m), got in zip(work, together(groups, number)):
        taker(m, got)


ENTER = (enter_group, take_enter)
ATTEND = (attend_group, take_attend)
ATTEND_OUT = (attend_out_group, take_attend_out)
FEED = (feed_group, take_feed)
FEED_BACK = (feed_back_group, take_feed_back)
FEED_BACK_OUT = (feed_back_out_group, take_feed_back_out)
ATTEND_BACK = (attend_back_group, take_attend_back)
LEAVE = (leave_group, take_leave)
FEED_OUT = (feed_out_group, take_feed_out)
SETTLE = (settle_group, take_settle)


WEIGHT_GRADS = {
    "down": ("crn,crd->nd", "hidden", "mlp_low", False, 1),
    "gate_up": ("crd,crn->dn", "mlp_in", "gate_up_low", True, 1),
    "out": ("crn,crd->nd", "attended", "attn_low", False, 1),
    "qkv": ("crd,crn->dn", "attn_in", "d_qkv", True, 3),
}


def local(
    hidden,
    embedding,
    lengths,
    query_key_value_weight,
    attention_output_weight,
    attention_gain,
    feedforward_gain,
    gate_up_weight,
    adapter_down,
    adapter_up,
    down_weight,
    shared_projection_weight,
    mixer_gain,
    mixer_input_weight,
    state_map_weight,
    step_weight,
    mixer_output_weight,
    mixer_input_taps,
    state_map_taps,
    step_bias,
    decay_logarithm,
    head_skip_weight,
    gated_norm_gain,
    cotangent,
    n_dp,
    n_t,
):
    links = Links(n_dp, n_t)
    smalls = (
        mixer_input_taps,
        state_map_taps,
        step_bias,
        decay_logarithm,
        head_skip_weight,
        gated_norm_gain,
    )
    micro = [
        SimpleNamespace(
            hid=hidden[b], emb=embedding[b], lens=lengths[b, 0], cot=cotangent[b]
        )
        for b in range(hidden.shape[0])
    ]
    w = SimpleNamespace()
    gains = core_pair(links, jnp.stack([attention_gain, feedforward_gain], 0), 1).astype(F32)
    w.g_attn, w.g_mlp = gains[0], gains[1]
    parts = query_key_value_weight.transpose(1, 0, 2)
    w.qkv_pair = RowPair(parts, links.core_swap(parts))
    def stage(work, m):
        with jax.named_scope(f"{work.__name__}_micro{micro.index(m)}"):
            work(links, w, m)

    units = gate_up_weight.shape[2]
    up_own = adapter_up.reshape(adapter_up.shape[0], 2 * units)
    cols = jnp.concatenate([gate_up_weight[:, 0], gate_up_weight[:, 1], adapter_down], axis=1)
    w.out_pair = ColPair(attention_output_weight, links.core_swap(attention_output_weight))
    w.gate_up_pair = RowPair(cols, links.core_swap(cols))
    w.down_pair = ColPair(down_weight, links.core_swap(down_weight))
    w.proj_own = shared_projection_weight
    state_cols, step_cols = state_map_weight.shape[1], step_weight.shape[1]
    packed = jnp.concatenate([state_map_weight, step_weight, mixer_gain[:, None]], axis=1)

    w.smalls = smalls
    def gather_mixer():
        w.adapter_up = lax.all_gather(after(up_own, w.begun), "dp", axis=0, tiled=True)
        whole = lax.all_gather(after(packed, w.begun), "dp", axis=0, tiled=True)
        w.bc = whole[:, :state_cols]
        w.dt = whole[:, state_cols : state_cols + step_cols]
        w.g_mamba = whole[:, state_cols + step_cols].astype(F32)
        shard = after(mixer_input_weight.transpose(1, 0, 2), w.begun)
        w.w_in = lax.all_gather(shard, "dp", axis=1, tiled=True)
        shard = after(mixer_output_weight, w.begun)
        w.mout = lax.all_gather(shard, "dp", axis=1, tiled=True)

    def run(*works):
        for work in works:
            for m in micro:
                stage(work, m)

    def both(get, axis=0):
        return jnp.concatenate([get(m) for m in micro], axis=axis)

    def mixer_grads(done=None):
        ssm_in = both(lambda m: m.ssm_in)
        grad_in = dotl("td,ktc->kdc", ssm_in, both(lambda m: m.gate_x_low, 1))
        begun = grad_in
        grad_in = grad_in if done is None else after(grad_in, done)
        grad_in = lax.psum_scatter(grad_in, "dp", scatter_dimension=1, tiled=True)
        grad_bc = dotl("td,tn->dn", both(lambda m: m.ssm_in_z), both(lambda m: m.state_low))
        grad_dt = dotl("td,tn->dn", ssm_in, both(lambda m: m.step_low))
        grad_small = jnp.concatenate([grad_bc, grad_dt], axis=1)
        grad_small = lax.psum_scatter(grad_small, "dp", scatter_dimension=0, tiled=True)
        grad_up = dotl("ra,rn->an", both(lambda m: m.adapter), both(lambda m: m.gate_up_own))
        grad_up = lax.psum_scatter(grad_up, "dp", scatter_dimension=0, tiled=True)
        return begun, grad_in, grad_small, grad_up

    def mout_grad(done=None):
        grad_mout = dotl("tn,ti->ni", both(lambda m: m.grad_low), both(lambda m: m.gated_norm))
        grad_mout = grad_mout if done is None else after(grad_mout, done)
        grad_mout = lax.psum_scatter(grad_mout, "dp", scatter_dimension=0, tiled=True)
        return grad_mout

    def lines(values):
        flat = jnp.concatenate([v.reshape(-1) for v in values])
        return jnp.pad(flat, (0, -flat.size % 1024)).reshape(-1, 128)

    def small_terms():
        sums = [jax.tree.map(lambda *v: total(v), *[m.sums_all for m in micro])]
        sums += [jax.tree.map(lambda *v: total(v), *[m.sums_dp for m in micro])]
        return [lines(values) for values in sums]

    def tensor_terms():
        terms = [grad_cols[:, 2 * units :].astype(BF16), grad_small[:, :state_cols]]
        return jnp.concatenate([v.reshape(-1, HEAD) for v in terms], 0)

    def weight_grad(name):
        _, a, b, by_rows, parts = WEIGHT_GRADS[name]

        def make(*_):
            return WeightGrad([getattr(m, a) for m in micro], [getattr(m, b) for m in micro], by_rows, parts)

        return (make, lambda _, got: setattr(w, "grad_" + name, got[0]), None)

    if links.chips == 4 and links.n_t == 4 and len(micro) == 2:
        a, b = micro
        spread = (spread_group, lambda _, got: setattr(w, "proj", got[0]), None)
        fused(links, w, 1, (*ENTER, a))
        fused(links, w, 2, (*ATTEND, a), spread, (*ENTER, b))
        w.begun = a.attended
        gather_mixer()
        fused(links, w, 3, (*ATTEND_OUT, a), (*ATTEND, b))
        fused(links, w, 4, (*FEED, a), (*ATTEND_OUT, b))
        fused(links, w, 5, (*FEED, b), (*FEED_OUT, a))
        mixer_rows(links, a)
        stage(mix, a)
        fused(links, w, 6, (*FEED_OUT, b), (*SETTLE, a))
        mixer_rows(links, b)
        stage(mix, b)
        outputs = (outputs_group, lambda _, got: setattr(w, "results", got[0]), micro)
        fused(links, w, 7, (*FEED_BACK, a), (*SETTLE, b), outputs)
        collect = (lambda *_: Collect(*projection_grads(links, micro)), lambda _, got: setattr(w, "grad_proj", got[0]), None)
        fused(links, w, 8, (*FEED_BACK_OUT, a), (*FEED_BACK, b))
        terms = small_terms()
        rows_all = terms[0].shape[0]
        sums = (
            lambda *_: SmallSum(jnp.concatenate(terms, 0), rows_all),
            lambda _, got: setattr(w, "flat", got[0]),
            None,
        )
        fused(links, w, 9, (*FEED_BACK_OUT, b), (*ATTEND_BACK, a), weight_grad("gate_up"), sums)
        flat, grad_cols = w.flat, w.grad_gate_up
        fused(links, w, 10, (*LEAVE, a), (*ATTEND_BACK, b), weight_grad("down"), collect)
        grad_mout = mout_grad(b.d_qkv)
        _, grad_in, grad_small, grad_up = mixer_grads(b.d_qkv)

        fused(links, w, 11, (*LEAVE, b), weight_grad("qkv"), weight_grad("out"))
        whole_t = links.z_sum(tensor_terms())
        grad_down, grad_out = w.grad_down, w.grad_out
        grad_qkv = w.grad_qkv.transpose(1, 0, 2)
        grad_proj = w.grad_proj
        for m in micro:
            m.d_hid, m.d_emb = jnp.split(m.left.reshape(-1, m.left.shape[2]), 2, axis=1)
        results = w.results.reshape(links.n_t, len(micro), -1, w.results.shape[2])
        results = z_join(results.transpose(1, 0, 2, 3), 1)
    else:
        for m in micro:
            stage(enter, m)
        inverses = jnp.stack([m.inverse for m in micro], 0)
        inverses = jnp.stack(links.chip_a2a([inverses] * links.chips), 1)
        for b, m in enumerate(micro):
            m.inv_attn = inverses[b]
        w.qkv, w.out = w.qkv_pair.whole(), w.out_pair.whole()
        w.gate_up, w.down = w.gate_up_pair.whole(), w.down_pair.whole()
        w.proj = proj_spread(links, shared_projection_weight)
        run(attend)
        w.begun = micro[0].attended
        gather_mixer()
        run(attend_out, feed, feed_out, mix, settle)
        run(feed_back, feed_back_out, attend_back, leave)
        results = finish_output(links, micro)
        grad_proj = proj_collect(links, *projection_grads(links, micro))
        mixed = mixer_grads()
        grad_mout = mout_grad()

        def grad(name, axis):
            spec, a, b = WEIGHT_GRADS[name][:3]
            terms = [dotf(spec, getattr(m, a), getattr(m, b)) for m in micro]
            return core_rs(links, total(terms), axis)

        grad_down, grad_cols, grad_out = grad("down", 1), grad("gate_up", 0), grad("out", 1)
        grad_qkv = jnp.stack(jnp.split(grad("qkv", 0), 3, axis=1), 1)
        _, grad_in, grad_small, grad_up = mixed
        flat_all, flat_dp = small_terms()
        rows_all = flat_all.shape[0]
        flat = links.dp_sum(jnp.concatenate([links.z_sum(flat_all), flat_dp], 0))
        whole_t = links.z_sum(tensor_terms())
    small_sums, flat = [], flat.reshape(-1)
    for start, parts in ((0, micro[0].sums_all), (rows_all * 128, micro[0].sums_dp)):
        for v in parts:
            small_sums.append(flat[start : start + v.size].reshape(v.shape))
            start += v.size
    own_gain = mixer_gain.shape[0]
    grad_g_mamba = lax.dynamic_slice_in_dim(small_sums[1], links.d * own_gain, own_gain)

    g_rows = total([jnp.stack([m.grad_g_attn, m.grad_g_mlp], 0) for m in micro])
    half = g_rows.shape[1] // 2
    g_rows = g_rows[:, :half] + links.core_swap(g_rows[:, half:])
    g_rows = links.z_sum(g_rows)

    grad_gate_up = jnp.stack([grad_cols[:, :units], grad_cols[:, units : 2 * units]], 1)
    split = grad_cols.shape[0] * (grad_cols.shape[1] - 2 * units) // HEAD
    grad_adapter_down = whole_t[:split].reshape(grad_cols.shape[0], -1).astype(F32)
    grad_bc = whole_t[split:].reshape(-1, state_cols).astype(F32)

    return (
        results,
        jnp.stack([m.d_hid for m in micro]),
        jnp.stack([m.d_emb for m in micro]),
        grad_qkv,
        grad_out,
        g_rows[0],
        g_rows[1],
        grad_gate_up,
        grad_adapter_down,
        grad_up.reshape(adapter_up.shape).astype(F32),
        grad_down,
        grad_proj,
        grad_g_mamba,
        grad_in.transpose(1, 0, 2).astype(F32),
        grad_bc,
        grad_small[:, state_cols:].astype(F32),
        grad_mout.T.astype(F32),
        small_sums[2],
        small_sums[0],
        small_sums[4],
        small_sums[5],
        small_sums[6],
        small_sums[3],
    )


def solution(mesh):
    rows = P(None, "dp", None)
    by_dp = P("dp", None, "tensor")
    by_t = P("tensor", "dp")
    weights = (by_dp, by_t, P("dp"), P("dp"), by_dp, P("dp", None), by_dp, by_t, by_t, P("dp"))
    weights += (by_dp, P("dp", None), P("dp", "tensor"), by_t)
    smalls = (P(None, "tensor"), P(), P("tensor"), P("tensor"), P("tensor"), P("tensor"))
    return jax.shard_map(
        partial(local, n_dp=mesh.shape["dp"], n_t=mesh.shape["tensor"]),
        mesh=mesh,
        in_specs=(rows, rows, rows) + weights + smalls + (rows,),
        out_specs=(rows, rows, rows) + weights + smalls,
        check_vma=False,
    )
```
